32 devices in a mesh: dp: 8 (over z, x), tensor: 4 (over y, core).
Axes of the slice: x: 2, y: 2, z: 4, core: 2. Of those that a mesh axis runs over, the one named last changes fastest.
Arguments:
- hidden_in: bfloat16 [8192, 768], P(('dp', 'tensor')), may hold values from -6 to 6
- cotangent: bfloat16 [8192, 768], P(('dp', 'tensor')), may hold values from -6 to 6
- w_query: bfloat16 [2, 768, 768], P(None, 'dp', 'tensor'), may hold values from -0.21875 to 0.21875
- w_key: bfloat16 [2, 768, 768], P(None, 'dp', 'tensor'), may hold values from -0.21875 to 0.21875
- w_value: bfloat16 [2, 768, 768], P(None, 'dp', 'tensor'), may hold values from -0.21875 to 0.21875
- w_outgate: bfloat16 [2, 768, 768], P(None, 'dp', 'tensor'), may hold values from -0.21875 to 0.21875
- w_rate: bfloat16 [2, 768, 12], P(None, 'dp', 'tensor'), may hold values from -0.21875 to 0.21875
- w_output: bfloat16 [2, 768, 768], P(None, 'tensor', 'dp'), may hold values from -0.21875 to 0.21875
- init_first: bfloat16 [2, 12, 64, 256], P(None, 'tensor', None, 'dp'), may hold values from -0.75 to 0.75
- init_first_bias: bfloat16 [2, 12, 256], P(None, 'tensor', 'dp'), may hold values from -2 to 2
- init_second: bfloat16 [2, 12, 256, 64], P(None, 'tensor', 'dp'), may hold values from -0.375 to 0.375
- init_second_bias: bfloat16 [2, 12, 64], P(None, 'tensor', 'dp'), may hold values from -2 to 2
- inner_gain: bfloat16 [2, 12, 64], P(None, 'tensor', 'dp'), may hold values from 0.5 to 1.5
- inner_shift: bfloat16 [2, 12, 64], P(None, 'tensor', 'dp'), may hold values from -2 to 2
- post_gain: bfloat16 [2, 12, 64], P(None, 'tensor', 'dp'), may hold values from 0.5 to 1.5
- post_shift: bfloat16 [2, 12, 64], P(None, 'tensor', 'dp'), may hold values from -2 to 2
- mixer_gain: bfloat16 [2, 768], P(None, ('dp', 'tensor')), may hold values from 0.5 to 1.5
- mlp_gain: bfloat16 [2, 768], P(None, ('dp', 'tensor')), may hold values from 0.5 to 1.5
- w_gate: bfloat16 [2, 768, 2048], P(None, 'dp', 'tensor'), may hold values from -0.21875 to 0.21875
- w_up: bfloat16 [2, 768, 2048], P(None, 'dp', 'tensor'), may hold values from -0.21875 to 0.21875
- w_down: bfloat16 [2, 2048, 768], P(None, 'tensor', 'dp'), may hold values from -0.125 to 0.125
Outputs:
- block_out: bfloat16 [8192, 768], P(('dp', 'tensor'))
- grad_in: float32 [8192, 768], P(('dp', 'tensor'))
- grad_query: float32 [2, 768, 768], P(None, 'dp', 'tensor')
- grad_key: float32 [2, 768, 768], P(None, 'dp', 'tensor')
- grad_value: float32 [2, 768, 768], P(None, 'dp', 'tensor')
- grad_outgate: float32 [2, 768, 768], P(None, 'dp', 'tensor')
- grad_rate: float32 [2, 768, 12], P(None, 'dp', 'tensor')
- grad_output: float32 [2, 768, 768], P(None, 'tensor', 'dp')
- gradient_hidden_weight: float32 [2, 12, 64, 256], P(None, 'tensor', None, 'dp')
- grad_first_bias: float32 [2, 12, 256], P(None, 'tensor', 'dp')
- gradient_output_weight: float32 [2, 12, 256, 64], P(None, 'tensor', 'dp')
- grad_second_bias: float32 [2, 12, 64], P(None, 'tensor', 'dp')
- grad_inner_gain: float32 [2, 12, 64], P(None, 'tensor', 'dp')
- grad_inner_shift: float32 [2, 12, 64], P(None, 'tensor', 'dp')
- grad_post_gain: float32 [2, 12, 64], P(None, 'tensor', 'dp')
- grad_post_shift: float32 [2, 12, 64], P(None, 'tensor', 'dp')
- grad_mixer_gain: float32 [2, 768], P(None, ('dp', 'tensor'))
- grad_mlp_gain: float32 [2, 768], P(None, ('dp', 'tensor'))
- grad_w_gate: float32 [2, 768, 2048], P(None, 'dp', 'tensor')
- grad_w_up: float32 [2, 768, 2048], P(None, 'dp', 'tensor')
- grad_w_down: float32 [2, 2048, 768], P(None, 'tensor', 'dp')
The draws below stay inside these ranges and needn't reach their ends.
All inputs are finite; a program needn't handle non-finite values.
Results may differ from the reference program's by a relative error of at most 0.03.
Values may be sent and summed in bfloat16 or wider, within the bound.
No kernel may reach another device: no remote copies, remote signals or barrier semaphores. Data moves between devices by JAX's collectives and lax.ppermute only.
A program may use at most 128 MiB of HBM per device.

```python
import jax
import jax.numpy as jnp
from jax import lax

D = 768
H = 12
HD = 64
INNER = 256
FF = 2048
CS = 16
LEN = 1024
SEQS = 1
LAYERS = 2
TOKENS = 8192


def shard_levels(rng, shape, cuts, least, top_value):
    loudness, own = 1.0, jax.random.fold_in(rng, 6)
    for dim, blocks in cuts:
        draws = jnp.exp(jax.random.uniform(jax.random.fold_in(own, dim), (blocks,), jnp.float32, least / len(cuts), top_value / len(cuts)))
        loudness = loudness * jnp.repeat(draws, shape[dim] // blocks).reshape([-1 if axis == dim else 1 for axis in range(len(shape))])
    return loudness


def normal_values(key, shape, spread, reach, shards=(), held_as=jnp.bfloat16):
    values = jax.random.normal(key, shape, jnp.float32) * spread
    if len(shards) > 0:
        values = shard_levels(key, shape, shards, -0.22, 0.18) * values
    return jnp.clip(values, min=-reach, max=reach).astype(held_as)


def setup_inputs(seed: int = 0) -> dict:
    streams_of = jax.random.split(jax.random.key(seed), 22)
    hidden_in = normal_values(streams_of[0], (TOKENS, D), 1.0, 6.0, ((0, 32),))
    cotangent = normal_values(streams_of[1], (TOKENS, D), 1.0, 6.0, ((0, 32),))
    w_query = normal_values(streams_of[2], (LAYERS, D, D), D ** -0.5, 0.21875, ((1, 8), (2, 4)))
    w_key = normal_values(streams_of[3], (LAYERS, D, D), D ** -0.5, 0.21875, ((1, 8), (2, 4)))
    w_value = normal_values(streams_of[4], (LAYERS, D, D), D ** -0.5, 0.21875, ((1, 8), (2, 4)))
    w_outgate = normal_values(streams_of[5], (LAYERS, D, D), D ** -0.5, 0.21875, ((1, 8), (2, 4)))
    w_rate = normal_values(streams_of[6], (LAYERS, D, H), D ** -0.5, 0.21875, ((1, 8), (2, 4)))
    w_output = normal_values(streams_of[7], (LAYERS, D, D), D ** -0.5, 0.21875, ((1, 4), (2, 8)))
    init_first = normal_values(streams_of[8], (LAYERS, H, HD, INNER), HD ** -0.5, 0.75, ((1, 4), (3, 8)))
    init_first_bias = normal_values(streams_of[9], (LAYERS, H, INNER), 0.3, 2.0, ((1, 4), (2, 8)))
    init_second = normal_values(streams_of[10], (LAYERS, H, INNER, HD), INNER ** -0.5, 0.375, ((1, 4), (2, 8)))
    init_second_bias = normal_values(streams_of[11], (LAYERS, H, HD), 0.3, 2.0, ((1, 4), (2, 8)))
    inner_gain = jnp.clip(1.0 + 0.1 * jax.random.normal(streams_of[12], (LAYERS, H, HD), jnp.float32), 0.5, 1.5).astype(jnp.bfloat16)
    inner_shift = normal_values(streams_of[13], (LAYERS, H, HD), 0.3, 2.0, ((1, 4), (2, 8)))
    post_gain = jnp.clip(1.0 + 0.1 * jax.random.normal(streams_of[14], (LAYERS, H, HD), jnp.float32), 0.5, 1.5).astype(jnp.bfloat16)
    post_shift = normal_values(streams_of[15], (LAYERS, H, HD), 0.3, 2.0, ((1, 4), (2, 8)))
    mixer_gain = jnp.clip(1.0 + 0.1 * jax.random.normal(streams_of[16], (LAYERS, D), jnp.float32), 0.5, 1.5).astype(jnp.bfloat16)
    mlp_gain = jnp.clip(1.0 + 0.1 * jax.random.normal(streams_of[17], (LAYERS, D), jnp.float32), 0.5, 1.5).astype(jnp.bfloat16)
    w_gate = normal_values(streams_of[18], (LAYERS, D, FF), D ** -0.5, 0.21875, ((1, 8), (2, 4)))
    w_up = normal_values(streams_of[19], (LAYERS, D, FF), D ** -0.5, 0.21875, ((1, 8), (2, 4)))
    w_down = normal_values(streams_of[20], (LAYERS, FF, D), FF ** -0.5, 0.125, ((1, 4), (2, 8)))
    return {"hidden_in": hidden_in, "cotangent": cotangent, "w_query": w_query, "w_key": w_key, "w_value": w_value, "w_outgate": w_outgate, "w_rate": w_rate, "w_output": w_output, "init_first": init_first, "init_first_bias": init_first_bias, "init_second": init_second, "init_second_bias": init_second_bias, "inner_gain": inner_gain, "inner_shift": inner_shift, "post_gain": post_gain, "post_shift": post_shift, "mixer_gain": mixer_gain, "mlp_gain": mlp_gain, "w_gate": w_gate, "w_up": w_up, "w_down": w_down}


@jax.custom_vjp
def low(v):
    return lax.optimization_barrier(v.astype(jnp.bfloat16)).astype(jnp.float32)

@jax.custom_vjp
def low_back(v):
    return v

def low_keep(v):
    return (low(v), None)

def low_pass(kept, grad):
    return (grad,)

def back_keep(v):
    return (v, None)

def back_low(kept, grad):
    return (low(grad),)
low.defvjp(low_keep, low_pass)
low_back.defvjp(back_keep, back_low)
epsilon = 1e-06
base_rate = 1.0
precision_level = lax.Precision.HIGHEST

def matmul_high(left, right):
    return jnp.matmul(left, right, precision=precision_level)

def rms_scale(row_vals, gain_vec):
    return row_vals * lax.rsqrt(lax.optimization_barrier(jnp.mean(row_vals * row_vals, axis=-1, keepdims=True)) + epsilon) * gain_vec

def layer_norm(row_vals, weight, shift_vec):
    center = row_vals - lax.optimization_barrier(jnp.mean(row_vals, axis=-1, keepdims=True))
    return center * lax.rsqrt(lax.optimization_barrier(jnp.mean(center * center, axis=-1, keepdims=True)) + epsilon) * weight + shift_vec

def gelu_tanh(values_in):
    return jax.nn.gelu(values_in, approximate=True)

def activation_slope(values_in):
    tanh_val = jnp.tanh(0.7978845608028654 * (values_in + 0.044715 * values_in * values_in * values_in))
    return 0.5 * (1.0 + tanh_val) + 0.5 * values_in * (1.0 - tanh_val * tanh_val) * 0.7978845608028654 * (1.0 + 3.0 * 0.044715 * values_in * values_in)

def inner_step(ln_weight, ln_shift, state_now, block_in):
    hidden_weight, hidden_bias, output_weight, output_bias = state_now
    query_rows_all, key_matrix_rows, value_rows, step_rates = block_in
    mini_size = query_rows_all.shape[1]
    position = jnp.arange(mini_size, dtype=jnp.float32)
    causal = (jnp.arange(mini_size)[:, None] >= jnp.arange(mini_size)[None, :]).astype(jnp.float32)
    inner_rate_matrix = (1.0 / (position + 1.0))[None, :, None] * step_rates[:, None, :] * causal[None]
    hidden_preactivation = jnp.einsum('umr,urt->umt', key_matrix_rows, hidden_weight, precision=precision_level) + hidden_bias[:, None, :]
    activation_hidden = gelu_tanh(hidden_preactivation)
    output_preactivation = jnp.einsum('uez,uzy->uey', activation_hidden, output_weight, precision=precision_level) + output_bias[:, None, :]
    center = output_preactivation - lax.optimization_barrier(jnp.mean(output_preactivation, axis=-1, keepdims=True))
    inv_std = lax.rsqrt(lax.optimization_barrier(jnp.mean(center * center, axis=-1, keepdims=True)) + epsilon)
    unit_rows = center * inv_std
    grad_out = unit_rows * ln_weight[:, None, :] + ln_shift[:, None, :] - (value_rows - key_matrix_rows)
    grad_hat = grad_out * ln_weight[:, None, :]
    gradient_output_weight = inv_std * (grad_hat - lax.optimization_barrier(jnp.mean(grad_hat, axis=-1, keepdims=True)) - unit_rows * lax.optimization_barrier(jnp.mean(grad_hat * unit_rows, axis=-1, keepdims=True)))
    gradient_hidden_weight = jnp.einsum('qml,qrl->qmr', gradient_output_weight, output_weight, precision=precision_level) * activation_slope(hidden_preactivation)
    attention_scores_inner = jnp.einsum('cbd,ced->cbe', query_rows_all, key_matrix_rows, precision=precision_level) + 1.0
    hidden_preactivation_cotangent = jnp.einsum('umr,urt->umt', query_rows_all, hidden_weight, precision=precision_level) + hidden_bias[:, None, :] - jnp.einsum('suz,szt->sut', inner_rate_matrix * attention_scores_inner, gradient_hidden_weight, precision=precision_level)
    activation_cotangent = gelu_tanh(hidden_preactivation_cotangent)
    attention_scores_outer = jnp.einsum('psj,ptj->pst', activation_cotangent, activation_hidden, precision=precision_level) + 1.0
    output_preactivation_cotangent = jnp.einsum('uez,uzy->uey', activation_cotangent, output_weight, precision=precision_level) + output_bias[:, None, :] - jnp.einsum('ntl,nlp->ntp', inner_rate_matrix * attention_scores_outer, gradient_output_weight, precision=precision_level)
    final_row_slice = inner_rate_matrix[:, -1, :]
    updated_hidden_weight = hidden_weight - jnp.einsum('ki,kir,kil->krl', final_row_slice, key_matrix_rows, gradient_hidden_weight, precision=precision_level)
    updated_hidden_bias = hidden_bias - jnp.einsum('qg,qgx->qx', final_row_slice, gradient_hidden_weight, precision=precision_level)
    updated_output_weight = output_weight - jnp.einsum('ae,aet,aeu->atu', final_row_slice, activation_hidden, gradient_output_weight, precision=precision_level)
    second_bias_new = output_bias - jnp.einsum('cb,cbd->cd', final_row_slice, gradient_output_weight, precision=precision_level)
    output = query_rows_all + layer_norm(output_preactivation_cotangent, ln_weight[:, None, :], ln_shift[:, None, :])
    return ((updated_hidden_weight, updated_hidden_bias, updated_output_weight, second_bias_new), output)

def inner_chains(query_rows_all, key_matrix_rows, value_rows, rate_logit, hidden_weight, hidden_bias, output_weight, output_bias, ln_weight, ln_shift):
    head_count = hidden_weight.shape[0]
    head_dim = hidden_weight.shape[1]
    seq_count = query_rows_all.shape[0] // LEN
    blocks = LEN // CS

    def arrange(field_in):
        return field_in.reshape(seq_count, blocks, CS, head_count, head_dim).transpose(1, 0, 3, 2, 4).reshape(blocks, seq_count * head_count, CS, head_dim)
    step_rates = base_rate * jax.nn.sigmoid(rate_logit) / head_dim
    step_rates = step_rates.reshape(seq_count, blocks, CS, head_count).transpose(1, 0, 3, 2).reshape(blocks, seq_count * head_count, CS)
    weight_all = jnp.tile(ln_weight, (seq_count, 1))
    shift_all = jnp.tile(ln_shift, (seq_count, 1))
    state_now = (jnp.tile(hidden_weight, (seq_count, 1, 1)), jnp.tile(hidden_bias, (seq_count, 1)), jnp.tile(output_weight, (seq_count, 1, 1)), jnp.tile(output_bias, (seq_count, 1)))

    def single(state_in, block_in):
        return inner_step(weight_all, shift_all, state_in, block_in)
    final_state, outputs = lax.scan(jax.checkpoint(single), state_now, (arrange(query_rows_all), arrange(key_matrix_rows), arrange(value_rows), step_rates))
    return outputs.reshape(blocks, seq_count, head_count, CS, head_dim).transpose(1, 0, 3, 2, 4).reshape(seq_count * LEN, head_count * head_dim)

def forward(row_vals, params):
    w_query, w_key, w_value, w_outgate, w_rate, w_output, init_first, init_first_bias, init_second, init_second_bias, inner_gain, inner_shift, post_gain, post_shift, mixer_gain, mlp_gain, w_gate, w_up, w_down = params
    residual = row_vals
    for layer_idx in range(LAYERS):
        normed = low(rms_scale(residual, mixer_gain[layer_idx]))
        query_rows_all = low_back(low(matmul_high(normed, w_query[layer_idx])))
        key_matrix_rows = low_back(low(matmul_high(normed, w_key[layer_idx])))
        value_rows = low_back(low(matmul_high(normed, w_value[layer_idx])))
        gate_pre = low_back(matmul_high(normed, w_outgate[layer_idx]))
        rate_logit = low_back(matmul_high(normed, w_rate[layer_idx]))
        inner_out = inner_chains(query_rows_all, key_matrix_rows, value_rows, rate_logit, init_first[layer_idx], init_first_bias[layer_idx], init_second[layer_idx], init_second_bias[layer_idx], inner_gain[layer_idx], inner_shift[layer_idx])
        post_out = layer_norm(inner_out, post_gain[layer_idx].reshape(-1), post_shift[layer_idx].reshape(-1))
        heads_out = low(gelu_tanh(gate_pre) * post_out)
        residual = residual + low_back(matmul_high(heads_out, w_output[layer_idx]))
        normed_two = low(rms_scale(residual, mlp_gain[layer_idx]))
        gate_proj = low_back(matmul_high(normed_two, w_gate[layer_idx]))
        up_proj = low_back(matmul_high(normed_two, w_up[layer_idx]))
        hidden = low(jax.nn.silu(gate_proj) * up_proj)
        residual = residual + low_back(matmul_high(hidden, w_down[layer_idx]))
    return residual

def reference(hidden_in, cotangent, w_query, w_key, w_value, w_outgate, w_rate, w_output, init_first, init_first_bias, init_second, init_second_bias, inner_gain, inner_shift, post_gain, post_shift, mixer_gain, mlp_gain, w_gate, w_up, w_down):
    params = tuple((p.astype(jnp.float32) for p in (w_query, w_key, w_value, w_outgate, w_rate, w_output, init_first, init_first_bias, init_second, init_second_bias, inner_gain, inner_shift, post_gain, post_shift, mixer_gain, mlp_gain, w_gate, w_up, w_down)))
    group_rows = SEQS * LEN
    groups = hidden_in.shape[0] // group_rows
    rows_all = hidden_in.astype(jnp.float32).reshape(groups, group_rows, D)
    cot_all = cotangent.astype(jnp.float32).reshape(groups, group_rows, D)

    def one_block(grad_total, pair):
        row_vals, cot_vals = pair
        block_val, pull_back = jax.vjp(forward, row_vals, params)
        grad_rows, grad_params = pull_back(cot_vals)
        grad_total = jax.tree.map(lambda acc, new: acc + new, grad_total, grad_params)
        return (grad_total, (block_val, grad_rows))
    zeros_start = jax.tree.map(jnp.zeros_like, params)
    grad_total, (block_vals, grad_rows) = lax.scan(one_block, zeros_start, (rows_all, cot_all))
    block_out = block_vals.reshape(hidden_in.shape[0], D).astype(jnp.bfloat16)
    grad_in = grad_rows.reshape(hidden_in.shape[0], D)
    return (block_out, grad_in, grad_total[0], grad_total[1], grad_total[2], grad_total[3], grad_total[4], grad_total[5], grad_total[6], grad_total[7], grad_total[8], grad_total[9], grad_total[10], grad_total[11], grad_total[12], grad_total[13], grad_total[14], grad_total[15], grad_total[16], grad_total[17], grad_total[18])
```

```python
import functools

import jax
import jax.numpy as jnp
from jax import lax
from jax.experimental import pallas as pl
from jax.sharding import PartitionSpec as P
from jax.experimental.pallas import tpu as pltpu

F32 = jnp.float32
BF = jnp.bfloat16
HD = 64
INNER = 256
CS = 16
CH = 128
STEPS = CH // CS
PACK = 640
EPS = 1e-6
K0 = 0.7978845608028654
K1 = 0.7978845608028654 * 0.044715


def mm(a, b, ca, cb):
    return lax.dot_general(
        a.astype(BF), b.astype(BF), (((ca,), (cb,)), ((), ())), preferred_element_type=F32
    )


def nn(a, b):
    return mm(a, b, 1, 0)


def nt(a, b):
    return mm(a, b, 1, 1)


def tn(a, b):
    return mm(a, b, 0, 0)


def gelu_two(z):
    zz = z * z
    t = jnp.tanh(z * (K0 + K1 * zz))
    half = 0.5 + 0.5 * t
    return z * half, half + 0.5 * z * (1.0 - t * t) * (K0 + 3.0 * K1 * zz)


def gelu_three(z):
    zz = z * z
    t = jnp.tanh(z * (K0 + K1 * zz))
    half = 0.5 + 0.5 * t
    rest = 1.0 - t * t
    p = K0 + 3.0 * K1 * zz
    return z * half, half + 0.5 * z * rest * p, rest * (p + 3.0 * K1 * zz - z * t * p * p)


def mean(x):
    return jnp.sum(x, axis=1, keepdims=True) * (1.0 / HD)


def masks():
    row = lax.broadcasted_iota(jnp.int32, (CH, CH), 0)
    col = lax.broadcasted_iota(jnp.int32, (CH, CH), 1)
    row_block, col_block = row // CS, col // CS
    inside = (row_block == col_block) & (col <= row)
    earlier = col_block < row_block
    own = 1.0 / ((row % CS) + 1).astype(F32)
    coef = jnp.where(earlier, 1.0 / CS, jnp.where(inside, own, 0.0))
    return coef, jnp.where(earlier, 1.0, 0.0)


def split_pack(pack, heads):
    wide = pack.astype(F32)
    first = wide[:, :CH]
    turned = first.T
    rates_row = [jax.nn.sigmoid(turned[h : h + 1]) * (1.0 / HD) for h in range(heads)]
    rates_col = [jax.nn.sigmoid(first[:, h : h + 1]) * (1.0 / HD) for h in range(heads)]
    off = HD
    xq = [wide[:, off + HD * h : off + HD * (h + 1)] for h in range(heads)]
    off += HD * heads
    xk = [wide[:, off + HD * h : off + HD * (h + 1)] for h in range(heads)]
    off += HD * heads
    xv = [wide[:, off + HD * h : off + HD * (h + 1)] for h in range(heads)]
    return xq, xk, xv, rates_row, rates_col


def forward_kernel(
    heads, place_ref, pack_ref, w1_ref, b1_ref, w2_ref, b2_ref, g_ref, h_ref,
    o_ref, z1_ref, a_ref, z1b_ref, c_ref, z2b_ref, w1s_ref, w2s_ref,
    w1, b1, w2, b2, pre, kke, cc, ecol, g1buf, g2buf, x2buf,
):
    H = range(heads)

    @pl.when(pl.program_id(0) == 0)
    def _():
        w1[...] = w1_ref[...]
        b1[...] = b1_ref[...]
        w2[...] = w2_ref[...]
        b2[...] = b2_ref[...]
        g1buf[...] = jnp.zeros_like(g1buf)

    coef, before = masks()
    xq, xk, xv, rrow, rcol = split_pack(pack_ref[...], heads)
    b2_start = [b2[h] for h in H]
    mcc = []
    for h in H:
        pre[h] = nn(xk[h], w1[h]) + b1[h]
        kke[h] = ((nt(xk[h], xk[h]) + 1.0) * (before * (rrow[h] * (1.0 / CS)))).astype(BF)
        g, sh = g_ref[h], h_ref[h]
        cval = (sh - xv[h] + xk[h]) * g
        cc[h] = cval
        mcc.append(mean(cval))
        ecol[h] = jnp.broadcast_to(rcol[h] * (1.0 / CS), (CH, HD))
        w1s_ref[0, h] = w1[h].astype(w1s_ref.dtype)
    ma = [mean(g_ref[h] * g_ref[h]) for h in H]
    w2v = [w2[h] for h in H]
    b2v = list(b2_start)
    for i in range(STEPS):
        rows = slice(CS * i, CS * (i + 1))
        z1 = [pre[h, rows, :] for h in H]
        if i >= 2:
            z1 = [z1[h] - nn(kke[h, rows, : CS * (i - 1)], g1buf[h, : CS * (i - 1), :]) for h in H]
        if i >= 1:
            z1 = [z1[h] - nn(kke[h, rows, :][:, CS * (i - 1) : CS * i], g1buf[h, CS * (i - 1) : CS * i, :]) for h in H]
        xd = [gelu_two(z1[h]) for h in H]
        x2b = [xd[h][0].astype(BF) for h in H]
        w2b = [w2v[h].astype(BF) for h in H]
        c = [nt(x2b[h], w2b[h]) + b2v[h] for h in H]
        g2 = []
        for h in H:
            g = g_ref[h]
            a = g * g
            ca = c[h] * a
            cch = cc[h, rows, :]
            mc = mcc[h][rows]
            mu, q1, q2, q3, q4 = mean(c[h]), mean(c[h] * c[h]), mean(ca), mean(ca * c[h]), mean(c[h] * cch)
            s = lax.rsqrt(q1 - mu * mu + EPS)
            m1 = s * (q2 - mu * ma[h]) + mc
            m2 = s * (s * (q3 - mu * (2.0 * q2 - mu * ma[h])) + (q4 - mu * mc))
            c[h] = c[h] - mu
            g2.append(s * (c[h] * (s * (a - m2)) + cch - m1))
        av = [nn(g2[h], w2b[h]) for h in H]
        g1 = [av[h] * xd[h][1] for h in H]
        for h in H:
            g1buf[h, rows, :] = g1[h].astype(BF)
            g2buf[h, rows, :] = g2[h].astype(BF)
            x2buf[h, rows, :] = x2b[h]
            w2s_ref[i, h] = w2b[h].astype(w2s_ref.dtype)
            z1_ref[rows, INNER * h : INNER * (h + 1)] = z1[h]
            a_ref[rows, INNER * h : INNER * (h + 1)] = av[h]
            c_ref[h, rows, :] = c[h]
            eg2 = ecol[h, rows, :] * g2[h]
            w2v[h] = w2v[h] - tn(eg2, x2b[h])
            b2v[h] = b2v[h] - jnp.sum(eg2, axis=0, keepdims=True)
    for h in H:
        mask = coef * rrow[h]
        g1, g2, x2 = g1buf[h], g2buf[h], x2buf[h]
        z1b = nn(xq[h], w1[h]) + b1[h] - nn((nt(xq[h], xk[h]) + 1.0) * mask, g1)
        z1b_ref[:, INNER * h : INNER * (h + 1)] = z1b
        x2q = jax.nn.gelu(z1b, approximate=True).astype(BF)
        z2b = nt(x2q, w2[h]) + b2_start[h] - nn((nt(x2q, x2) + 1.0) * mask, g2)
        z2b = z2b - mean(z2b)
        z2b_ref[h] = z2b
        unit = z2b * lax.rsqrt(mean(z2b * z2b) + EPS)
        o_ref[:, HD * h : HD * (h + 1)] = xq[h] + unit * g_ref[h] + h_ref[h]
        ek = ecol[h] * xk[h]
        w1[h] = w1[h] - tn(ek, g1)
        b1[h] = b1[h] - jnp.sum(ecol[h][:, :1] * g1.astype(F32), axis=0, keepdims=True)
        w2[h] = w2v[h]
        b2[h] = b2v[h]


def forward_call(place, pack, w1, b1, w2, b2, g, h):
    heads = w1.shape[0]
    rows = pack.shape[0]
    chunks = rows // CH
    per_block = chunks // 4

    def spot(c, place):
        return ((c // per_block) ^ place[0]) * per_block + c % per_block

    def whole(*shape):
        return pl.BlockSpec(shape, lambda c, place: (0,) * len(shape))

    def moved(n):
        return pl.BlockSpec((CH, n), lambda c, place: (spot(c, place), 0))

    def kept(n):
        return pl.BlockSpec((CH, n), lambda c, place: (c, 0))

    by_head = pl.BlockSpec((heads, CH, HD), lambda c, place: (0, c, 0))
    sds = jax.ShapeDtypeStruct
    return pl.pallas_call(
        functools.partial(forward_kernel, heads),
        grid_spec=pltpu.PrefetchScalarGridSpec(
            num_scalar_prefetch=1,
            grid=(chunks,),
            in_specs=[
                moved(PACK),
                whole(heads, HD, INNER),
                whole(heads, 1, INNER),
                whole(heads, HD, INNER),
                whole(heads, 1, HD),
                whole(heads, 1, HD),
                whole(heads, 1, HD),
            ],
            out_specs=[
                moved(heads * HD),
                kept(heads * INNER),
                kept(heads * INNER),
                kept(heads * INNER),
                by_head,
                by_head,
                pl.BlockSpec((1, heads, HD, INNER), lambda c, place: (c, 0, 0, 0)),
                pl.BlockSpec((STEPS, heads, HD, INNER), lambda c, place: (c, 0, 0, 0)),
            ],
            scratch_shapes=[
                pltpu.VMEM((heads, HD, INNER), F32),
                pltpu.VMEM((heads, 1, INNER), F32),
                pltpu.VMEM((heads, HD, INNER), F32),
                pltpu.VMEM((heads, 1, HD), F32),
                pltpu.VMEM((heads, CH, INNER), F32),
                pltpu.VMEM((heads, CH, CH), BF),
                pltpu.VMEM((heads, CH, HD), F32),
                pltpu.VMEM((heads, CH, HD), F32),
                pltpu.VMEM((heads, CH, INNER), BF),
                pltpu.VMEM((heads, CH, HD), BF),
                pltpu.VMEM((heads, CH, INNER), BF),
            ],
        ),
        out_shape=[
            sds((rows, heads * HD), F32),
            sds((rows, heads * INNER), F32),
            sds((rows, heads * INNER), F32),
            sds((rows, heads * INNER), F32),
            sds((heads, rows, HD), F32),
            sds((heads, rows, HD), F32),
            sds((chunks, heads, HD, INNER), BF),
            sds((chunks * STEPS, heads, HD, INNER), BF),
        ],
        compiler_params=pltpu.CompilerParams(vmem_limit_bytes=40 * 2**20),
        cost_estimate=pl.CostEstimate(flops=65 * 10**9, bytes_accessed=25 * 10**6, transcendentals=0),
    )(place, pack, w1, b1, w2, b2, g, h)


def backward_kernel(
    heads, place_ref, pack_ref, do_ref, z1_ref, a_ref, z1b_ref, c_ref, z2b_ref, w1s_ref, w2s_ref, g_ref, h_ref,
    dpack_ref, dw1, db1, dw2, db2, dg_ref, dh_ref,
    dg1b, dg2b, dx2b, d1v, ad2, g2v, kkt, dz1buf, k1v, k2v, dyv, ecol, x2buf,
):
    H = range(heads)

    @pl.when(pl.program_id(0) == 0)
    def _():
        dw1[...] = jnp.zeros_like(dw1)
        db1[...] = jnp.zeros_like(db1)
        dw2[...] = jnp.zeros_like(dw2)
        db2[...] = jnp.zeros_like(db2)
        dg_ref[...] = jnp.zeros_like(dg_ref)
        dh_ref[...] = jnp.zeros_like(dh_ref)
        dz1buf[...] = jnp.zeros_like(dz1buf)

    coef, before = masks()
    xq, xk, xv, rrow, rcol = split_pack(pack_ref[...], heads)
    uv, yv, st = [], [], []
    dxq, dxk, dr_row = [], [], []
    dw1_out, db1_out, dw2_out, db2_out = [], [], [], []
    x2_all, g1_all, g2_all, ccv = [], [], [], []
    for h in H:
        wide = slice(INNER * h, INNER * (h + 1))
        g, sh = g_ref[h], h_ref[h]
        a = g * g
        x2, d1, d2 = gelu_three(z1_ref[:, wide])
        av = a_ref[:, wide]
        d1v[h] = d1
        ad2[h] = av * d2
        x2 = x2.astype(BF)
        x2buf[h] = x2
        g1 = (av * d1).astype(BF)
        c = c_ref[h]
        cch = (sh - xv[h] + xk[h]) * g
        ca = c * a
        q1, q2, q3, q4 = mean(c * c), mean(ca), mean(ca * c), mean(c * cch)
        s = lax.rsqrt(q1 + EPS)
        m1 = s * q2 + mean(cch)
        m2 = s * (s * q3 + q4)
        u = c * s
        y = u * a + cch
        g2 = s * (y - m1 - u * m2)
        uv.append(u)
        yv.append(y)
        st.append((s, m2, s * q2, s * s * q3, mean(y), mean(a)))
        g2v[h] = g2
        x2_all.append(x2)
        g1_all.append(g1)
        g2_all.append(g2)
        ccv.append(cch)
        ecol[h] = jnp.broadcast_to(rcol[h] * (1.0 / CS), (CH, HD))
        do = do_ref[:, HD * h : HD * (h + 1)].astype(F32)
        z2b = z2b_ref[h]
        sb = lax.rsqrt(mean(z2b * z2b) + EPS)
        ub = z2b * sb
        dog = do * g
        dg_ref[h] += jnp.sum(do * ub, axis=0, keepdims=True)
        dh_ref[h] += jnp.sum(do, axis=0, keepdims=True)
        dz2b = sb * (dog - mean(dog) - ub * mean(dog * ub))
        x2q, d1b = gelu_two(z1b_ref[:, wide])
        x2q = x2q.astype(BF)
        w2_start, w1_start = w2s_ref[0, h], w1s_ref[0, h]
        mask = coef * rrow[h]
        p = nt(x2q, x2) + 1.0
        dm2 = -nt(dz2b, g2)
        dp = (mask * dm2).astype(BF)
        dg2b[h] = -tn(mask * p, dz2b)
        dx2b[h] = tn(dp, x2q)
        dx2q = nn(dz2b, w2_start) + nn(dp, x2)
        dz1b = dx2q * d1b
        sc = nt(xq[h], xk[h]) + 1.0
        dm1 = -nt(dz1b, g1)
        ds = (mask * dm1).astype(BF)
        kk = nt(xk[h], xk[h]) + 1.0
        kkt[h] = (kk * before.T).astype(BF)
        k1 = nn(xk[h], dw1[h]) + db1[h]
        k1v[h] = k1
        dg1b[h] = -tn(mask * sc, dz1b)
        dr_row.append(jnp.sum(coef * (sc * dm1 + p * dm2), axis=0, keepdims=True))
        dxq.append(do + nt(dz1b, w1_start) + nn(ds, xk[h]))
        dxk.append(tn(ds, xq[h]) - nt((rcol[h] * (1.0 / CS)) * g1.astype(F32), dw1[h]))
        dw1_out.append(tn(xq[h], dz1b))
        db1_out.append(jnp.sum(dz1b, axis=0, keepdims=True))
        dw2_out.append(tn(dz2b, x2q))
        db2_out.append(jnp.sum(dz2b, axis=0, keepdims=True))
    d2 = [dw2[h] for h in H]
    e2 = [db2[h] for h in H]
    for i in reversed(range(STEPS)):
        rows = slice(CS * i, CS * (i + 1))
        k1 = [k1v[h, rows, :] for h in H]
        if i < STEPS - 2:
            k1 = [k1[h] + nn(kkt[h, rows, :][:, CS * (i + 2) :], dz1buf[h, CS * (i + 2) :, :]) for h in H]
        if i < STEPS - 1:
            k1 = [k1[h] + nn(kkt[h, rows, :][:, CS * (i + 1) : CS * (i + 2)], dz1buf[h, CS * (i + 1) : CS * (i + 2), :]) for h in H]
        dg1 = [dg1b[h, rows, :] - ecol[h, rows, :][:, :1] * k1[h] for h in H]
        da = [(dg1[h] * d1v[h, rows, :]).astype(BF) for h in H]
        d2b = [d2[h].astype(BF) for h in H]
        w2i = [w2s_ref[i, h] for h in H]
        g2 = [g2v[h, rows, :] for h in H]
        k2 = [nt(x2buf[h, rows, :], d2b[h]) + e2[h] for h in H]
        dg2 = [dg2b[h, rows, :] - ecol[h, rows, :] * k2[h] + nt(da[h], w2i[h]) for h in H]
        l2 = [dx2b[h, rows, :] - nn(ecol[h, rows, :] * g2[h], d2b[h]) for h in H]
        dz2 = []
        for h in H:
            g = g_ref[h]
            a = g * g
            s, m2, mau, mauu, my = (q[rows] for q in st[h][:5])
            ma = st[h][5]
            u, y = uv[h][rows], yv[h][rows]
            dv = dg2[h]
            dva = dv * a
            n1, n2, n3, n4, n5 = mean(dv), mean(dv * u), mean(dv * g2[h]), mean(dva * u), mean(dva)
            dy = s * (dv - n1 - u * n2)
            muu = s * (n4 - n1 * mau - n2 * (mauu + 2.0 * m2))
            mu = s * (n5 - n1 * (ma + m2) - n2 * (mau + my))
            dz2.append(s * (dy * a - (s * m2) * dv - (s * n2) * y - mu - u * (muu + n3)))
            dyv[h, rows, :] = dy
            k2v[h, rows, :] = k2[h]
        dx2 = [l2[h] + nn(dz2[h], w2i[h]) for h in H]
        dz1 = [dx2[h] * d1v[h, rows, :] + dg1[h] * ad2[h, rows, :] for h in H]
        for h in H:
            dz1buf[h, rows, :] = dz1[h].astype(BF)
            d2[h] = d2[h] + tn(
                jnp.concatenate([g2[h], dz2[h]], axis=0), jnp.concatenate([da[h], x2buf[h, rows, :]], axis=0)
            )
            e2[h] = e2[h] + jnp.sum(dz2[h], axis=0, keepdims=True)
    dq_out, dk_out, dv_out, de_col = [], [], [], []
    for h in H:
        g = g_ref[h]
        dz1 = dz1buf[h]
        dy = dyv[h]
        g1, g2 = g1_all[h], g2_all[h]
        k1 = k1v[h] + nn(kkt[h], dz1)
        de_col.append(jnp.sum(g1.astype(F32) * k1, axis=1, keepdims=True) + jnp.sum(g2 * k2v[h], axis=1, keepdims=True))
        dkk = (-nt(dz1, g1) * (before * (rrow[h] * (1.0 / CS)))).astype(BF)
        dyg = dy * g
        dk = dxk[h] + nn(dkk, xk[h]) + tn(dkk, xk[h]) + nt(dz1, w1s_ref[0, h]) + dyg
        dg_ref[h] += jnp.sum(dy * (uv[h] * g * 2.0 + h_ref[h] - xv[h] + xk[h]), axis=0, keepdims=True)
        dh_ref[h] += jnp.sum(dyg, axis=0, keepdims=True)
        off = HD + HD * h
        dpack_ref[:, off : off + HD] = dxq[h].astype(dpack_ref.dtype)
        off += HD * heads
        dpack_ref[:, off : off + HD] = dk.astype(dpack_ref.dtype)
        off += HD * heads
        dpack_ref[:, off : off + HD] = (-dyg).astype(dpack_ref.dtype)
        dw1[h] = dw1[h] + dw1_out[h] + tn(xk[h], dz1)
        db1[h] = db1[h] + db1_out[h] + jnp.sum(dz1.astype(F32), axis=0, keepdims=True)
        dw2[h] = d2[h] + dw2_out[h]
        db2[h] = e2[h] + db2_out[h]
    sub = lax.broadcasted_iota(jnp.int32, (CH, CH), 0)
    lane = lax.broadcasted_iota(jnp.int32, (CH, CH), 1)
    stack = jnp.zeros((CH, CH), F32)
    cols = jnp.zeros((CH, CH), F32)
    for h in H:
        stack = stack + jnp.where(sub == h, dr_row[h], 0.0)
        slope = rcol[h] * (1.0 - HD * rcol[h])
        cols = cols + jnp.where(lane == h, slope, 0.0)
    turned = stack.T
    for h in H:
        turned = turned - jnp.where(lane == h, de_col[h] * (1.0 / CS), 0.0)
    dpack_ref[:, :HD] = (turned * cols)[:, :HD].astype(dpack_ref.dtype)


def backward_call(place, pack, do, saved, g, h):
    z1, a, z1b, c, z2b, w1s, w2s = saved
    heads = g.shape[0]
    rows = pack.shape[0]
    chunks = rows // CH
    last = chunks - 1
    per_block = chunks // 4

    def spot(c, place):
        return (((last - c) // per_block) ^ place[0]) * per_block + (last - c) % per_block

    def whole(*shape):
        return pl.BlockSpec(shape, lambda c, place: (0,) * len(shape))

    def moved(n):
        return pl.BlockSpec((CH, n), lambda c, place: (spot(c, place), 0))

    def kept(n):
        return pl.BlockSpec((CH, n), lambda c, place: (last - c, 0))

    by_head = pl.BlockSpec((heads, CH, HD), lambda c, place: (0, last - c, 0))
    sds = jax.ShapeDtypeStruct
    return pl.pallas_call(
        functools.partial(backward_kernel, heads),
        grid_spec=pltpu.PrefetchScalarGridSpec(
            num_scalar_prefetch=1,
            grid=(chunks,),
            in_specs=[
                moved(PACK),
                moved(heads * HD),
                kept(heads * INNER),
                kept(heads * INNER),
                kept(heads * INNER),
                by_head,
                by_head,
                pl.BlockSpec((1, heads, HD, INNER), lambda c, place: (last - c, 0, 0, 0)),
                pl.BlockSpec((STEPS, heads, HD, INNER), lambda c, place: (last - c, 0, 0, 0)),
                whole(heads, 1, HD),
                whole(heads, 1, HD),
            ],
            out_specs=[
                moved(PACK),
                whole(heads, HD, INNER),
                whole(heads, 1, INNER),
                whole(heads, HD, INNER),
                whole(heads, 1, HD),
                whole(heads, 1, HD),
                whole(heads, 1, HD),
            ],
            scratch_shapes=[
                pltpu.VMEM((heads, CH, INNER), F32),
                pltpu.VMEM((heads, CH, HD), F32),
                pltpu.VMEM((heads, CH, INNER), F32),
                pltpu.VMEM((heads, CH, INNER), F32),
                pltpu.VMEM((heads, CH, INNER), F32),
                pltpu.VMEM((heads, CH, HD), F32),
                pltpu.VMEM((heads, CH, CH), BF),
                pltpu.VMEM((heads, CH, INNER), BF),
                pltpu.VMEM((heads, CH, INNER), F32),
                pltpu.VMEM((heads, CH, HD), F32),
                pltpu.VMEM((heads, CH, HD), F32),
                pltpu.VMEM((heads, CH, HD), F32),
                pltpu.VMEM((heads, CH, INNER), BF),
            ],
        ),
        out_shape=[
            sds((rows, PACK), BF),
            sds((heads, HD, INNER), F32),
            sds((heads, 1, INNER), F32),
            sds((heads, HD, INNER), F32),
            sds((heads, 1, HD), F32),
            sds((heads, 1, HD), F32),
            sds((heads, 1, HD), F32),
        ],
        compiler_params=pltpu.CompilerParams(vmem_limit_bytes=40 * 2**20),
        cost_estimate=pl.CostEstimate(flops=70 * 10**9, bytes_accessed=25 * 10**6, transcendentals=0),
    )(place, pack, do, z1, a, z1b, c, z2b, w1s, w2s, g, h)


D = 768


def swap(x, bit):
    size = lax.axis_size("tensor")
    return lax.ppermute(x, "tensor", [(i, i ^ bit) for i in range(size)])


def widen(x):
    far = swap(x, 2)
    return jnp.concatenate([x, swap(x, 1), far, swap(far, 1)], axis=0)


def narrow(total):
    quarter = total.shape[0] // 4
    near, pair, far, cross = [total[quarter * i : quarter * (i + 1)] for i in range(4)]
    far = (far + swap(cross.astype(BF), 1).astype(F32)).astype(BF)
    far = swap(far, 2)
    return near + swap(pair.astype(BF), 1).astype(F32) + far.astype(F32)


def dot(a, b):
    return lax.dot_general(a, b, (((1,), (0,)), ((), ())), preferred_element_type=F32)


def dot_t(a, b):
    return lax.dot_general(a, b, (((1,), (1,)), ((), ())), preferred_element_type=F32)


def t_dot(a, b):
    return lax.dot_general(a, b, (((0,), (0,)), ((), ())), preferred_element_type=F32)


def rms(x, gain):
    scale = lax.rsqrt(jnp.mean(x * x, axis=1, keepdims=True) + EPS)
    return (x * scale * gain).astype(BF), scale


def rms_back(x, scale, gain, grad):
    q = grad * gain
    back = scale * q - x * (scale * scale * scale) * jnp.mean(q * x, axis=1, keepdims=True)
    return back, jnp.sum(grad * (x * scale), axis=0)


def gather(x):
    return lax.all_gather(x, "dp", axis=0, tiled=True)


def scatter(x):
    return lax.psum_scatter(x, "dp", scatter_dimension=0, tiled=True).astype(F32)


def exchange_sum(x):
    moved = lax.all_to_all(x, "dp", split_axis=0, concat_axis=0, tiled=True)
    return jnp.sum(moved.astype(F32), axis=0)


def per_device(
    hidden_in, cotangent, w_query, w_key, w_value, w_outgate, w_rate, w_output, init_first, init_first_bias,
    init_second, init_second_bias, inner_gain, inner_shift, post_gain, post_shift, mixer_gain, mlp_gain,
    w_gate, w_up, w_down,
):
    layers, part, mine = w_query.shape
    heads = w_rate.shape[2]
    ff = w_gate.shape[2]
    inner_part = init_first.shape[3]
    small_part = inner_gain.shape[2]
    gain_part = mixer_gain.shape[1]
    dp = lax.axis_size("dp")
    tp = lax.axis_size("tensor")
    rows = hidden_in.shape[0]
    place = lax.axis_index("tensor").astype(jnp.int32).reshape(1)
    lead = HD - heads

    gains_here = jnp.concatenate([mixer_gain, mlp_gain], axis=0)
    gains_group = lax.all_gather(gains_here, "tensor", axis=1, tiled=True)
    span = 2 * mine + 6 * heads
    blocks = []
    for l in range(layers):
        first = init_first[l].transpose(2, 0, 1).reshape(inner_part, mine)
        second = init_second[l].transpose(1, 0, 2).reshape(inner_part, mine)
        small = jnp.concatenate(
            [init_second_bias[l], inner_gain[l], inner_shift[l], post_gain[l], post_shift[l]], axis=0
        )
        small = jnp.pad(small.T, ((0, inner_part - small_part), (0, 0)))
        blocks += [first, second, init_first_bias[l].T, small]
    tail = gains_group.reshape(inner_part, -1) if gains_group.size % inner_part == 0 else None
    blocks.append(tail)
    inner_all = gather(jnp.concatenate(blocks, axis=1))
    gains = inner_all[:, layers * span :].reshape(dp, 2 * layers, tp * gain_part)
    gains = gains.transpose(1, 0, 2).reshape(2 * layers, D).astype(F32)
    inner = []
    for l in range(layers):
        own = inner_all[:, l * span : (l + 1) * span]
        turned = own[:, : 2 * mine + heads].T.astype(F32)
        w1 = turned[:mine].reshape(heads, HD, INNER)
        w2 = turned[mine : 2 * mine].reshape(heads, HD, INNER)
        b1 = turned[2 * mine :].reshape(heads, 1, INNER)
        small = own[:, 2 * mine + heads :].reshape(dp, inner_part, 5 * heads)[:, :small_part]
        small = small.reshape(HD, 5 * heads).T.astype(F32).reshape(5, heads, HD)
        w2 = w2 - jnp.mean(w2, axis=1, keepdims=True)
        b2 = small[0] - jnp.mean(small[0], axis=1, keepdims=True)
        inner.append((w1, b1, w2, b2[:, None], small[1][:, None], small[2][:, None], small[3], small[4]))

    blank = jnp.zeros((part, lead), BF)
    mix_w = [
        gather(jnp.concatenate([w_rate[l], blank, w_query[l], w_key[l], w_value[l]], axis=1)) for l in range(layers)
    ]
    rest_w = [
        gather(jnp.concatenate([w_outgate[l], w_gate[l], w_up[l], w_output[l].T, w_down[l].T], axis=1))
        for l in range(layers)
    ]
    edges = [0, mine, mine + ff, mine + 2 * ff, 2 * mine + 2 * ff, 2 * mine + 3 * ff]

    def piece(l, i):
        return rest_w[l][:, edges[i] : edges[i + 1]]

    residual = hidden_in.astype(F32)
    raw_wide = widen(hidden_in)
    kept = []
    for l in range(layers):
        w1, b1, w2, b2, g, h, pg, ps = inner[l]
        gain_one, gain_two = gains[l], gains[layers + l]
        res_one = residual
        if l == 0:
            wide, _ = rms(raw_wide.astype(F32), gain_one)
            scale_one = lax.rsqrt(jnp.mean(residual * residual, axis=1, keepdims=True) + EPS)
        else:
            normed, scale_one = rms(residual, gain_one)
            wide = widen(normed)
        pack = dot(wide, mix_w[l]).astype(BF)
        outs = forward_call(place, pack, w1, b1, w2, b2, g, h)
        inner_out, saved = outs[0], outs[1:]
        gate_pre = dot(wide, piece(l, 0))
        sums = jnp.stack([jnp.sum(inner_out, axis=1), jnp.sum(inner_out * inner_out, axis=1)])
        sums = order_sum(sums)
        mean_all = sums[0] / D
        inv = lax.rsqrt(sums[1] / D - mean_all * mean_all + EPS)[:, None]
        unit = (inner_out - mean_all[:, None]) * inv
        post = unit * pg.reshape(-1) + ps.reshape(-1)
        heads_out = (jax.nn.gelu(gate_pre, approximate=True) * post).astype(BF)
        residual = residual + narrow(dot_t(heads_out, piece(l, 3)))
        res_two = residual
        normed, scale_two = rms(residual, gain_two)
        wide_two = widen(normed)
        gate = dot(wide_two, piece(l, 1))
        up = dot(wide_two, piece(l, 2))
        hidden = (jax.nn.silu(gate) * up).astype(BF)
        residual = residual + narrow(dot_t(hidden, piece(l, 4)))
        kept.append(
            (res_one, scale_one, wide, pack, saved, gate_pre, unit, inv, heads_out, res_two, scale_two, wide_two,
             gate, up, hidden)
        )
    block_out = residual.astype(BF)

    grad = cotangent.astype(F32)
    mix_grads, rest_grads = [None] * layers, [None] * layers
    gain_grads = [None] * (2 * layers)
    for l in reversed(range(layers)):
        w1, b1, w2, b2, g, h, pg, ps = inner[l]
        gain_one, gain_two = gains[l], gains[layers + l]
        (res_one, scale_one, wide, pack, saved, gate_pre, unit, inv, heads_out, res_two, scale_two, wide_two,
         gate, up, hidden) = kept[l]
        branch = widen(cotangent if l == layers - 1 else grad.astype(BF))
        d_hidden = dot(branch, piece(l, 4))
        q = jax.nn.sigmoid(gate)
        swish = gate * q
        d_gate = (d_hidden * up * (q + swish * (1.0 - q))).astype(BF)
        d_up = (d_hidden * swish).astype(BF)
        d_down = t_dot(branch, hidden)
        d_norm = narrow(dot_t(d_gate, piece(l, 1)) + dot_t(d_up, piece(l, 2)))
        back, gain_grads[layers + l] = rms_back(res_two, scale_two, gain_two, d_norm)
        grad = grad + back
        branch_two = widen(grad.astype(BF))
        d_heads = dot(branch_two, piece(l, 3))
        post = unit * pg.reshape(-1) + ps.reshape(-1)
        ge, slope = gelu_two(gate_pre)
        d_pre = (d_heads * post * slope).astype(BF)
        d_post = d_heads * ge
        d_pg = jnp.sum(d_post * unit, axis=0)
        d_ps = jnp.sum(d_post, axis=0)
        p = d_post * pg.reshape(-1)
        sums = order_sum(jnp.stack([jnp.sum(p, axis=1), jnp.sum(p * unit, axis=1)])) / D
        d_inner = inv * (p - sums[0][:, None] - unit * sums[1][:, None])
        rest_grads[l] = scatter(
            jnp.concatenate(
                [t_dot(wide, d_pre), t_dot(wide_two, d_gate), t_dot(wide_two, d_up), t_dot(branch_two, heads_out), d_down],
                axis=1,
            ).astype(BF)
        )
        d_pack, dw1, db1, dw2, db2, dg, dh = backward_call(place, pack, d_inner, saved, g, h)
        d_norm = narrow(dot_t(d_pack, mix_w[l]) + dot_t(d_pre, piece(l, 0)))
        back, gain_grads[l] = rms_back(res_one, scale_one, gain_one, d_norm)
        grad = grad + back
        turned = jnp.concatenate([dw1.reshape(mine, INNER), dw2.reshape(mine, INNER), db1[:, 0]], axis=0).T
        small = jnp.concatenate([db2[:, 0], dg[:, 0], dh[:, 0], d_pg.reshape(heads, HD), d_ps.reshape(heads, HD)], axis=0)
        small = jnp.pad(small.T.reshape(dp, small_part, 5 * heads), ((0, 0), (0, inner_part - small_part), (0, 0)))
        block = [turned.reshape(dp, inner_part, 2 * mine + heads), small]
        if l == 0:
            all_gains = jnp.stack(gain_grads).reshape(2 * layers, dp, tp * gain_part)
            block.append(all_gains.transpose(1, 0, 2).reshape(dp, inner_part, -1))
        block = jnp.concatenate(block, axis=2)
        block = jnp.pad(block, ((0, 0), (0, 0), (0, PACK - block.shape[2])))
        mixed = jnp.concatenate([t_dot(wide, d_pack).reshape(dp, part, PACK), block], axis=1).astype(BF)
        mix_grads[l] = exchange_sum(mixed) if l == 0 else scatter(mixed)[0]
    grad_in = grad

    both = jnp.stack(mix_grads)
    mats, block = both[:, :part], both[:, part:]
    rest = jnp.stack(rest_grads)
    d_gains = mix_grads[0][part:, span : span + gains_group.size // inner_part].reshape(2 * layers, tp, gain_part)
    d_gains = lax.psum(d_gains, "tensor")
    d_gains = lax.dynamic_index_in_dim(d_gains, lax.axis_index("tensor"), axis=1, keepdims=False)
    small = block[:, :small_part, 2 * mine + heads : span].transpose(0, 2, 1).reshape(layers, 5, heads, small_part)

    def matrix(i):
        return mats[:, :, HD + mine * i : HD + mine * (i + 1)]

    def tail_piece(i):
        return rest[:, :, edges[i] : edges[i + 1]]

    def states(i):
        return block[:, :, mine * i : mine * (i + 1)].reshape(layers, inner_part, heads, HD)

    return (
        block_out,
        grad_in,
        matrix(0),
        matrix(1),
        matrix(2),
        tail_piece(0),
        mats[:, :, :heads],
        tail_piece(3).transpose(0, 2, 1),
        states(0).transpose(0, 2, 3, 1),
        block[:, :, 2 * mine : 2 * mine + heads].transpose(0, 2, 1),
        states(1).transpose(0, 2, 1, 3),
        small[:, 0],
        small[:, 1],
        small[:, 2],
        small[:, 3],
        small[:, 4],
        d_gains[:layers],
        d_gains[layers:],
        tail_piece(1),
        tail_piece(2),
        tail_piece(4).transpose(0, 2, 1),
    )


def order_sum(sums):
    def turn(x, bit):
        parts = jnp.split(x, 4, axis=1)
        return jnp.concatenate([parts[i ^ bit] for i in range(4)], axis=1)

    sums = sums + turn(swap(sums, 1), 1)
    return sums + turn(swap(sums, 2), 2)


def solution(mesh):
    placed = (
        P(("dp", "tensor"), None),
        P(("dp", "tensor"), None),
        P(None, "dp", "tensor"),
        P(None, "dp", "tensor"),
        P(None, "dp", "tensor"),
        P(None, "dp", "tensor"),
        P(None, "dp", "tensor"),
        P(None, "tensor", "dp"),
        P(None, "tensor", None, "dp"),
        P(None, "tensor", "dp"),
        P(None, "tensor", "dp", None),
        P(None, "tensor", "dp"),
        P(None, "tensor", "dp"),
        P(None, "tensor", "dp"),
        P(None, "tensor", "dp"),
        P(None, "tensor", "dp"),
        P(None, ("dp", "tensor")),
        P(None, ("dp", "tensor")),
        P(None, "dp", "tensor"),
        P(None, "dp", "tensor"),
        P(None, "tensor", "dp"),
    )
    return jax.shard_map(
        per_device,
        mesh=mesh,
        in_specs=placed,
        out_specs=(
            P(("dp", "tensor"), None),
            P(("dp", "tensor"), None),
            P(None, "dp", "tensor"),
            P(None, "dp", "tensor"),
            P(None, "dp", "tensor"),
            P(None, "dp", "tensor"),
            P(None, "dp", "tensor"),
            P(None, "tensor", "dp"),
            P(None, "tensor", None, "dp"),
            P(None, "tensor", "dp"),
            P(None, "tensor", "dp", None),
            P(None, "tensor", "dp"),
            P(None, "tensor", "dp"),
            P(None, "tensor", "dp"),
            P(None, "tensor", "dp"),
            P(None, "tensor", "dp"),
            P(None, ("dp", "tensor")),
            P(None, ("dp", "tensor")),
            P(None, "dp", "tensor"),
            P(None, "dp", "tensor"),
            P(None, "tensor", "dp"),
        ),
        check_vma=False,
    )
```

```python
import functools

import jax
import jax.numpy as jnp
from jax import lax
from jax.experimental import pallas as pl
from jax.sharding import PartitionSpec as P
from jax.experimental.pallas import tpu as pltpu

F32 = jnp.float32
BF = jnp.bfloat16
HD = 64
INNER = 256
CS = 16
CH = 128
STEPS = CH // CS
PACK = 640
EPS = 1e-6
K0 = 0.7978845608028654
K1 = 0.7978845608028654 * 0.044715


def mm(a, b, ca, cb):
    return lax.dot_general(
        a.astype(BF), b.astype(BF), (((ca,), (cb,)), ((), ())), preferred_element_type=F32
    )


def nn(a, b):
    return mm(a, b, 1, 0)


def nt(a, b):
    return mm(a, b, 1, 1)


def tn(a, b):
    return mm(a, b, 0, 0)


def gelu_two(z):
    zz = z * z
    t = jnp.tanh(z * (K0 + K1 * zz))
    half = 0.5 + 0.5 * t
    return z * half, half + 0.5 * z * (1.0 - t * t) * (K0 + 3.0 * K1 * zz)


def gelu_three(z):
    zz = z * z
    t = jnp.tanh(z * (K0 + K1 * zz))
    half = 0.5 + 0.5 * t
    rest = 1.0 - t * t
    p = K0 + 3.0 * K1 * zz
    return z * half, half + 0.5 * z * rest * p, rest * (p + 3.0 * K1 * zz - z * t * p * p)


def mean(x):
    return jnp.sum(x, axis=1, keepdims=True) * (1.0 / HD)


def masks():
    row = lax.broadcasted_iota(jnp.int32, (CH, CH), 0)
    col = lax.broadcasted_iota(jnp.int32, (CH, CH), 1)
    row_block, col_block = row // CS, col // CS
    inside = (row_block == col_block) & (col <= row)
    earlier = col_block < row_block
    own = 1.0 / ((row % CS) + 1).astype(F32)
    coef = jnp.where(earlier, 1.0 / CS, jnp.where(inside, own, 0.0))
    return coef, jnp.where(earlier, 1.0, 0.0)


def split_pack(pack, heads):
    wide = pack.astype(F32)
    first = wide[:, :CH]
    turned = first.T
    rates_row = [jax.nn.sigmoid(turned[h : h + 1]) * (1.0 / HD) for h in range(heads)]
    rates_col = [jax.nn.sigmoid(first[:, h : h + 1]) * (1.0 / HD) for h in range(heads)]
    off = HD
    xq = [wide[:, off + HD * h : off + HD * (h + 1)] for h in range(heads)]
    off += HD * heads
    xk = [wide[:, off + HD * h : off + HD * (h + 1)] for h in range(heads)]
    off += HD * heads
    xv = [wide[:, off + HD * h : off + HD * (h + 1)] for h in range(heads)]
    return xq, xk, xv, rates_row, rates_col


def forward_kernel(
    heads, dp, place_ref, pack_ref, in_ref,
    o_ref, z1_ref, a_ref, z1b_ref, c_ref, z2b_ref, w1s_ref, w2s_ref, small_ref,
    w1, b1, w2, b2, pre, kke, cc, ecol, g1buf, g2buf, x2buf,
):
    H = range(heads)

    @pl.when(pl.program_id(0) == 0)
    def _():
        mine = heads * HD
        params = in_ref[...].astype(F32)
        first, second, rest = params[:, :mine].T, params[:, mine : 2 * mine].T, params[:, 2 * mine :]
        biases = rest.T
        few, step = HD // dp, INNER // dp
        small = jnp.concatenate([rest[step * d : step * d + few] for d in range(dp)], axis=0).T
        small_ref[...] = small[heads:]
        for h in H:
            w1[h] = first[HD * h : HD * (h + 1)]
            w2_own = second[HD * h : HD * (h + 1)]
            w2[h] = w2_own - jnp.mean(w2_own, axis=0, keepdims=True)
            b1[h] = biases[h : h + 1]
            b2_own = small[heads + h : heads + h + 1]
            b2[h] = b2_own - mean(b2_own)
        g1buf[...] = jnp.zeros_like(g1buf)

    coef, before = masks()
    xq, xk, xv, rrow, rcol = split_pack(pack_ref[...], heads)
    b2_start = [b2[h] for h in H]
    mcc = []
    for h in H:
        pre[h] = nn(xk[h], w1[h]) + b1[h]
        kke[h] = ((nt(xk[h], xk[h]) + 1.0) * (before * (rrow[h] * (1.0 / CS)))).astype(BF)
        g, sh = small_ref[heads + h : heads + h + 1], small_ref[2 * heads + h : 2 * heads + h + 1]
        cval = (sh - xv[h] + xk[h]) * g
        cc[h] = cval
        mcc.append(mean(cval))
        ecol[h] = jnp.broadcast_to(rcol[h] * (1.0 / CS), (CH, HD))
        w1s_ref[0, h] = w1[h].astype(w1s_ref.dtype)
    ma = [mean(small_ref[heads + h : heads + h + 1] * small_ref[heads + h : heads + h + 1]) for h in H]
    w2v = [w2[h] for h in H]
    b2v = list(b2_start)
    for i in range(STEPS):
        rows = slice(CS * i, CS * (i + 1))
        z1 = [pre[h, rows, :] for h in H]
        if i >= 2:
            z1 = [z1[h] - nn(kke[h, rows, : CS * (i - 1)], g1buf[h, : CS * (i - 1), :]) for h in H]
        if i >= 1:
            z1 = [z1[h] - nn(kke[h, rows, :][:, CS * (i - 1) : CS * i], g1buf[h, CS * (i - 1) : CS * i, :]) for h in H]
        xd = [gelu_two(z1[h]) for h in H]
        x2b = [xd[h][0].astype(BF) for h in H]
        w2b = [w2v[h].astype(BF) for h in H]
        c = [nt(x2b[h], w2b[h]) + b2v[h] for h in H]
        g2 = []
        for h in H:
            g = small_ref[heads + h : heads + h + 1]
            a = g * g
            ca = c[h] * a
            cch = cc[h, rows, :]
            mc = mcc[h][rows]
            mu, q1, q2, q3, q4 = mean(c[h]), mean(c[h] * c[h]), mean(ca), mean(ca * c[h]), mean(c[h] * cch)
            s = lax.rsqrt(q1 - mu * mu + EPS)
            m1 = s * (q2 - mu * ma[h]) + mc
            m2 = s * (s * (q3 - mu * (2.0 * q2 - mu * ma[h])) + (q4 - mu * mc))
            c[h] = c[h] - mu
            g2.append(s * (c[h] * (s * (a - m2)) + cch - m1))
        av = [nn(g2[h], w2b[h]) for h in H]
        g1 = [av[h] * xd[h][1] for h in H]
        for h in H:
            g1buf[h, rows, :] = g1[h].astype(BF)
            g2buf[h, rows, :] = g2[h].astype(BF)
            x2buf[h, rows, :] = x2b[h]
            w2s_ref[i, h] = w2b[h].astype(w2s_ref.dtype)
            z1_ref[rows, INNER * h : INNER * (h + 1)] = z1[h].astype(BF)
            a_ref[rows, INNER * h : INNER * (h + 1)] = av[h].astype(BF)
            c_ref[h, rows, :] = c[h].astype(BF)
            eg2 = ecol[h, rows, :] * g2[h]
            w2v[h] = w2v[h] - tn(eg2, x2b[h])
            b2v[h] = b2v[h] - jnp.sum(eg2, axis=0, keepdims=True)
    for h in H:
        mask = coef * rrow[h]
        g1, g2, x2 = g1buf[h], g2buf[h], x2buf[h]
        z1b = nn(xq[h], w1[h]) + b1[h] - nn((nt(xq[h], xk[h]) + 1.0) * mask, g1)
        z1b_ref[:, INNER * h : INNER * (h + 1)] = z1b.astype(BF)
        x2q = jax.nn.gelu(z1b, approximate=True).astype(BF)
        z2b = nt(x2q, w2[h]) + b2_start[h] - nn((nt(x2q, x2) + 1.0) * mask, g2)
        z2b = z2b - mean(z2b)
        z2b_ref[h] = z2b.astype(BF)
        unit = z2b * lax.rsqrt(mean(z2b * z2b) + EPS)
        o_ref[:, HD * h : HD * (h + 1)] = xq[h] + unit * small_ref[heads + h : heads + h + 1] + small_ref[2 * heads + h : 2 * heads + h + 1]
        ek = ecol[h] * xk[h]
        w1[h] = w1[h] - tn(ek, g1)
        b1[h] = b1[h] - jnp.sum(ecol[h][:, :1] * g1.astype(F32), axis=0, keepdims=True)
        w2[h] = w2v[h]
        b2[h] = b2v[h]


def forward_call(place, pack, params, heads, dp):
    rows = pack.shape[0]
    chunks = rows // CH
    per_block = chunks // 4

    def spot(c, place):
        return ((c // per_block) ^ place[0]) * per_block + c % per_block

    def whole(*shape):
        return pl.BlockSpec(shape, lambda c, place: (0,) * len(shape))

    def moved(n):
        return pl.BlockSpec((CH, n), lambda c, place: (spot(c, place), 0))

    def kept(n):
        return pl.BlockSpec((CH, n), lambda c, place: (c, 0))

    by_head = pl.BlockSpec((heads, CH, HD), lambda c, place: (0, c, 0))
    sds = jax.ShapeDtypeStruct
    return pl.pallas_call(
        functools.partial(forward_kernel, heads, dp),
        grid_spec=pltpu.PrefetchScalarGridSpec(
            num_scalar_prefetch=1,
            grid=(chunks,),
            in_specs=[
                moved(PACK),
                whole(*params.shape),
            ],
            out_specs=[
                moved(heads * HD),
                kept(heads * INNER),
                kept(heads * INNER),
                kept(heads * INNER),
                by_head,
                by_head,
                pl.BlockSpec((1, heads, HD, INNER), lambda c, place: (c, 0, 0, 0)),
                pl.BlockSpec((STEPS, heads, HD, INNER), lambda c, place: (c, 0, 0, 0)),
                whole(5 * heads, HD),
            ],
            scratch_shapes=[
                pltpu.VMEM((heads, HD, INNER), F32),
                pltpu.VMEM((heads, 1, INNER), F32),
                pltpu.VMEM((heads, HD, INNER), F32),
                pltpu.VMEM((heads, 1, HD), F32),
                pltpu.VMEM((heads, CH, INNER), F32),
                pltpu.VMEM((heads, CH, CH), BF),
                pltpu.VMEM((heads, CH, HD), F32),
                pltpu.VMEM((heads, CH, HD), F32),
                pltpu.VMEM((heads, CH, INNER), BF),
                pltpu.VMEM((heads, CH, HD), BF),
                pltpu.VMEM((heads, CH, INNER), BF),
            ],
        ),
        out_shape=[
            sds((rows, heads * HD), F32),
            sds((rows, heads * INNER), BF),
            sds((rows, heads * INNER), BF),
            sds((rows, heads * INNER), BF),
            sds((heads, rows, HD), BF),
            sds((heads, rows, HD), BF),
            sds((chunks, heads, HD, INNER), BF),
            sds((chunks * STEPS, heads, HD, INNER), BF),
            sds((5 * heads, HD), F32),
        ],
        compiler_params=pltpu.CompilerParams(vmem_limit_bytes=56 * 2**20),
        cost_estimate=pl.CostEstimate(flops=65 * 10**9, bytes_accessed=25 * 10**6, transcendentals=0),
    )(place, pack, params)


def backward_kernel(
    heads, shares, place_ref, pack_ref, do_ref, z1_ref, a_ref, z1b_ref, c_ref, z2b_ref, w1s_ref, w2s_ref, small_ref, post_ref,
    dpack_ref, block_ref, dw1, db1, dw2, db2, dg_ref, dh_ref,
    dg1b, dg2b, dx2b, d1v, ad2, g2v, kkt, dz1buf, k1v, k2v, dyv, ecol, x2buf,
):
    H = range(heads)

    @pl.when(pl.program_id(0) == 0)
    def _():
        dw1[...] = jnp.zeros_like(dw1)
        db1[...] = jnp.zeros_like(db1)
        dw2[...] = jnp.zeros_like(dw2)
        db2[...] = jnp.zeros_like(db2)
        dg_ref[...] = jnp.zeros_like(dg_ref)
        dh_ref[...] = jnp.zeros_like(dh_ref)
        dz1buf[...] = jnp.zeros_like(dz1buf)

    coef, before = masks()
    xq, xk, xv, rrow, rcol = split_pack(pack_ref[...], heads)
    uv, yv, st = [], [], []
    dxq, dxk, dr_row = [], [], []
    dw1_out, db1_out, dw2_out, db2_out = [], [], [], []
    x2_all, g1_all, g2_all, ccv = [], [], [], []
    for h in H:
        wide = slice(INNER * h, INNER * (h + 1))
        g, sh = small_ref[heads + h : heads + h + 1], small_ref[2 * heads + h : 2 * heads + h + 1]
        a = g * g
        x2, d1, d2 = gelu_three(z1_ref[:, wide].astype(F32))
        av = a_ref[:, wide].astype(F32)
        d1v[h] = d1
        ad2[h] = av * d2
        x2 = x2.astype(BF)
        x2buf[h] = x2
        g1 = (av * d1).astype(BF)
        c = c_ref[h].astype(F32)
        cch = (sh - xv[h] + xk[h]) * g
        ca = c * a
        q1, q2, q3, q4 = mean(c * c), mean(ca), mean(ca * c), mean(c * cch)
        s = lax.rsqrt(q1 + EPS)
        m1 = s * q2 + mean(cch)
        m2 = s * (s * q3 + q4)
        u = c * s
        y = u * a + cch
        g2 = s * (y - m1 - u * m2)
        uv.append(u)
        yv.append(y)
        st.append((s, m2, s * q2, s * s * q3, mean(y), mean(a)))
        g2v[h] = g2
        x2_all.append(x2)
        g1_all.append(g1)
        g2_all.append(g2)
        ccv.append(cch)
        ecol[h] = jnp.broadcast_to(rcol[h] * (1.0 / CS), (CH, HD))
        do = do_ref[:, HD * h : HD * (h + 1)].astype(F32)
        z2b = z2b_ref[h].astype(F32)
        sb = lax.rsqrt(mean(z2b * z2b) + EPS)
        ub = z2b * sb
        dog = do * g
        dg_ref[h] += jnp.sum(do * ub, axis=0, keepdims=True)
        dh_ref[h] += jnp.sum(do, axis=0, keepdims=True)
        dz2b = sb * (dog - mean(dog) - ub * mean(dog * ub))
        x2q, d1b = gelu_two(z1b_ref[:, wide].astype(F32))
        x2q = x2q.astype(BF)
        w2_start, w1_start = w2s_ref[0, h], w1s_ref[0, h]
        mask = coef * rrow[h]
        p = nt(x2q, x2) + 1.0
        dm2 = -nt(dz2b, g2)
        dp = (mask * dm2).astype(BF)
        dg2b[h] = -tn(mask * p, dz2b)
        dx2b[h] = tn(dp, x2q)
        dx2q = nn(dz2b, w2_start) + nn(dp, x2)
        dz1b = dx2q * d1b
        sc = nt(xq[h], xk[h]) + 1.0
        dm1 = -nt(dz1b, g1)
        ds = (mask * dm1).astype(BF)
        kk = nt(xk[h], xk[h]) + 1.0
        kkt[h] = (kk * before.T).astype(BF)
        k1 = nn(xk[h], dw1[h]) + db1[h]
        k1v[h] = k1
        dg1b[h] = -tn(mask * sc, dz1b)
        dr_row.append(jnp.sum(coef * (sc * dm1 + p * dm2), axis=0, keepdims=True))
        dxq.append(do + nt(dz1b, w1_start) + nn(ds, xk[h]))
        dxk.append(tn(ds, xq[h]) - nt((rcol[h] * (1.0 / CS)) * g1.astype(F32), dw1[h]))
        dw1_out.append(tn(xq[h], dz1b))
        db1_out.append(jnp.sum(dz1b, axis=0, keepdims=True))
        dw2_out.append(tn(dz2b, x2q))
        db2_out.append(jnp.sum(dz2b, axis=0, keepdims=True))
    d2 = [dw2[h] for h in H]
    e2 = [db2[h] for h in H]
    for i in reversed(range(STEPS)):
        rows = slice(CS * i, CS * (i + 1))
        k1 = [k1v[h, rows, :] for h in H]
        if i < STEPS - 2:
            k1 = [k1[h] + nn(kkt[h, rows, :][:, CS * (i + 2) :], dz1buf[h, CS * (i + 2) :, :]) for h in H]
        if i < STEPS - 1:
            k1 = [k1[h] + nn(kkt[h, rows, :][:, CS * (i + 1) : CS * (i + 2)], dz1buf[h, CS * (i + 1) : CS * (i + 2), :]) for h in H]
        dg1 = [dg1b[h, rows, :] - ecol[h, rows, :][:, :1] * k1[h] for h in H]
        da = [(dg1[h] * d1v[h, rows, :]).astype(BF) for h in H]
        d2b = [d2[h].astype(BF) for h in H]
        w2i = [w2s_ref[i, h] for h in H]
        g2 = [g2v[h, rows, :] for h in H]
        k2 = [nt(x2buf[h, rows, :], d2b[h]) + e2[h] for h in H]
        dg2 = [dg2b[h, rows, :] - ecol[h, rows, :] * k2[h] + nt(da[h], w2i[h]) for h in H]
        l2 = [dx2b[h, rows, :] - nn(ecol[h, rows, :] * g2[h], d2b[h]) for h in H]
        dz2 = []
        for h in H:
            g = small_ref[heads + h : heads + h + 1]
            a = g * g
            s, m2, mau, mauu, my = (q[rows] for q in st[h][:5])
            ma = st[h][5]
            u, y = uv[h][rows], yv[h][rows]
            dv = dg2[h]
            dva = dv * a
            n1, n2, n3, n4, n5 = mean(dv), mean(dv * u), mean(dv * g2[h]), mean(dva * u), mean(dva)
            dy = s * (dv - n1 - u * n2)
            muu = s * (n4 - n1 * mau - n2 * (mauu + 2.0 * m2))
            mu = s * (n5 - n1 * (ma + m2) - n2 * (mau + my))
            dz2.append(s * (dy * a - (s * m2) * dv - (s * n2) * y - mu - u * (muu + n3)))
            dyv[h, rows, :] = dy
            k2v[h, rows, :] = k2[h]
        dx2 = [l2[h] + nn(dz2[h], w2i[h]) for h in H]
        dz1 = [dx2[h] * d1v[h, rows, :] + dg1[h] * ad2[h, rows, :] for h in H]
        for h in H:
            dz1buf[h, rows, :] = dz1[h].astype(BF)
            d2[h] = d2[h] + tn(
                jnp.concatenate([g2[h], dz2[h]], axis=0), jnp.concatenate([da[h], x2buf[h, rows, :]], axis=0)
            )
            e2[h] = e2[h] + jnp.sum(dz2[h], axis=0, keepdims=True)
    dq_out, dk_out, dv_out, de_col = [], [], [], []
    for h in H:
        g = small_ref[heads + h : heads + h + 1]
        dz1 = dz1buf[h]
        dy = dyv[h]
        g1, g2 = g1_all[h], g2_all[h]
        k1 = k1v[h] + nn(kkt[h], dz1)
        de_col.append(jnp.sum(g1.astype(F32) * k1, axis=1, keepdims=True) + jnp.sum(g2 * k2v[h], axis=1, keepdims=True))
        dkk = (-nt(dz1, g1) * (before * (rrow[h] * (1.0 / CS)))).astype(BF)
        dyg = dy * g
        dk = dxk[h] + nn(dkk, xk[h]) + tn(dkk, xk[h]) + nt(dz1, w1s_ref[0, h]) + dyg
        dg_ref[h] += jnp.sum(dy * (uv[h] * g * 2.0 + small_ref[2 * heads + h : 2 * heads + h + 1] - xv[h] + xk[h]), axis=0, keepdims=True)
        dh_ref[h] += jnp.sum(dyg, axis=0, keepdims=True)
        off = HD + HD * h
        dpack_ref[:, off : off + HD] = dxq[h].astype(dpack_ref.dtype)
        off += HD * heads
        dpack_ref[:, off : off + HD] = dk.astype(dpack_ref.dtype)
        off += HD * heads
        dpack_ref[:, off : off + HD] = (-dyg).astype(dpack_ref.dtype)
        dw1[h] = dw1[h] + dw1_out[h] + tn(xk[h], dz1)
        db1[h] = db1[h] + db1_out[h] + jnp.sum(dz1.astype(F32), axis=0, keepdims=True)
        dw2[h] = d2[h] + dw2_out[h]
        db2[h] = e2[h] + db2_out[h]
    sub = lax.broadcasted_iota(jnp.int32, (CH, CH), 0)
    lane = lax.broadcasted_iota(jnp.int32, (CH, CH), 1)
    stack = jnp.zeros((CH, CH), F32)
    cols = jnp.zeros((CH, CH), F32)
    for h in H:
        stack = stack + jnp.where(sub == h, dr_row[h], 0.0)
        slope = rcol[h] * (1.0 - HD * rcol[h])
        cols = cols + jnp.where(lane == h, slope, 0.0)
    turned = stack.T
    for h in H:
        turned = turned - jnp.where(lane == h, de_col[h] * (1.0 / CS), 0.0)
    dpack_ref[:, :HD] = (turned * cols)[:, :HD].astype(dpack_ref.dtype)

    @pl.when(pl.program_id(0) == pl.num_programs(0) - 1)
    def _():
        mine = heads * HD
        block_ref[...] = jnp.zeros_like(block_ref)
        for h in H:
            block_ref[:, HD * h : HD * (h + 1)] = dw1[h].T
            block_ref[:, mine + HD * h : mine + HD * (h + 1)] = dw2[h].T
        bias = jnp.concatenate([db1[h] for h in H] + [jnp.zeros((8 - heads, INNER), F32)], axis=0)
        block_ref[:, 2 * mine : 2 * mine + heads] = bias.T[:, :heads]
        lines = [db2[h] for h in H] + [dg_ref[h] for h in H] + [dh_ref[h] for h in H]
        lines += [post_ref[i : i + 1, HD * h : HD * (h + 1)] for i in range(2) for h in H]
        few, step = HD // shares, INNER // shares
        small = jnp.concatenate(lines + [jnp.zeros((16 - 5 * heads, HD), F32)], axis=0).T
        for d in range(shares):
            block_ref[step * d : step * d + few, 2 * mine + heads : 2 * mine + 6 * heads] = small[
                few * d : few * (d + 1), : 5 * heads
            ]


def backward_call(place, pack, do, saved, small, post, dp):
    z1, a, z1b, c, z2b, w1s, w2s = saved
    heads = small.shape[0] // 5
    rows = pack.shape[0]
    chunks = rows // CH
    last = chunks - 1
    per_block = chunks // 4

    def spot(c, place):
        return (((last - c) // per_block) ^ place[0]) * per_block + (last - c) % per_block

    def whole(*shape):
        return pl.BlockSpec(shape, lambda c, place: (0,) * len(shape))

    def moved(n):
        return pl.BlockSpec((CH, n), lambda c, place: (spot(c, place), 0))

    def kept(n):
        return pl.BlockSpec((CH, n), lambda c, place: (last - c, 0))

    by_head = pl.BlockSpec((heads, CH, HD), lambda c, place: (0, last - c, 0))
    sds = jax.ShapeDtypeStruct
    return pl.pallas_call(
        functools.partial(backward_kernel, heads, dp),
        grid_spec=pltpu.PrefetchScalarGridSpec(
            num_scalar_prefetch=1,
            grid=(chunks,),
            in_specs=[
                moved(PACK),
                moved(heads * HD),
                kept(heads * INNER),
                kept(heads * INNER),
                kept(heads * INNER),
                by_head,
                by_head,
                pl.BlockSpec((1, heads, HD, INNER), lambda c, place: (last - c, 0, 0, 0)),
                pl.BlockSpec((STEPS, heads, HD, INNER), lambda c, place: (last - c, 0, 0, 0)),
                whole(*small.shape),
                whole(*post.shape),
            ],
            out_specs=[moved(PACK), whole(INNER, PACK)],
            scratch_shapes=[
                pltpu.VMEM((heads, HD, INNER), F32),
                pltpu.VMEM((heads, 1, INNER), F32),
                pltpu.VMEM((heads, HD, INNER), F32),
                pltpu.VMEM((heads, 1, HD), F32),
                pltpu.VMEM((heads, 1, HD), F32),
                pltpu.VMEM((heads, 1, HD), F32),
                pltpu.VMEM((heads, CH, INNER), F32),
                pltpu.VMEM((heads, CH, HD), F32),
                pltpu.VMEM((heads, CH, INNER), F32),
                pltpu.VMEM((heads, CH, INNER), F32),
                pltpu.VMEM((heads, CH, INNER), F32),
                pltpu.VMEM((heads, CH, HD), F32),
                pltpu.VMEM((heads, CH, CH), BF),
                pltpu.VMEM((heads, CH, INNER), BF),
                pltpu.VMEM((heads, CH, INNER), F32),
                pltpu.VMEM((heads, CH, HD), F32),
                pltpu.VMEM((heads, CH, HD), F32),
                pltpu.VMEM((heads, CH, HD), F32),
                pltpu.VMEM((heads, CH, INNER), BF),
            ],
        ),
        out_shape=[
            sds((rows, PACK), BF),
            sds((INNER, PACK), F32),
        ],
        compiler_params=pltpu.CompilerParams(vmem_limit_bytes=56 * 2**20),
        cost_estimate=pl.CostEstimate(flops=70 * 10**9, bytes_accessed=25 * 10**6, transcendentals=0),
    )(place, pack, do, z1, a, z1b, c, z2b, w1s, w2s, small, post)


D = 768
DP = ("line", "near")


def swap(x, bit):
    size = lax.axis_size("tensor")
    return lax.ppermute(x, "tensor", [(i, i ^ bit) for i in range(size)])


def widen(x):
    far = swap(x, 2)
    return jnp.concatenate([x, swap(x, 1), far, swap(far, 1)], axis=0)


def narrow(total):
    quarter = total.shape[0] // 4
    near, pair, far, cross = [total[quarter * i : quarter * (i + 1)] for i in range(4)]
    far = (far + swap(cross.astype(BF), 1).astype(F32)).astype(BF)
    far = swap(far, 2)
    return near + swap(pair.astype(BF), 1).astype(F32) + far.astype(F32)


def dot(a, b):
    return lax.dot_general(a, b, (((1,), (0,)), ((), ())), preferred_element_type=F32)


def dot_t(a, b):
    return lax.dot_general(a, b, (((1,), (1,)), ((), ())), preferred_element_type=F32)


def t_dot(a, b):
    return lax.dot_general(a, b, (((0,), (0,)), ((), ())), preferred_element_type=F32)


def rms(x, gain):
    scale = lax.rsqrt(jnp.mean(x * x, axis=1, keepdims=True) + EPS)
    return (x * scale * gain).astype(BF), scale


def rms_back(x, scale, gain, grad):
    q = grad * gain
    back = scale * q - x * (scale * scale * scale) * jnp.mean(q * x, axis=1, keepdims=True)
    return back, jnp.sum(grad * (x * scale), axis=0)


def gather(x):
    return lax.all_gather(x, DP, axis=0, tiled=True)


def turned(x):
    return x.astype(F32).T.astype(BF)


def pack_kernel(
    q_ref, k_ref, v_ref, og_ref, r_ref, out_ref, i1_ref, i2_ref, gate_ref, up_ref, down_ref,
    mix_ref, early_ref, late_ref, inner_ref,
):
    heads = r_ref.shape[0]
    mine = heads * HD
    ff = gate_ref.shape[2]
    rest = 3 * ff + 2 * mine
    for l in range(2):
        mix, at = (mix_ref, 0) if l == 0 else (early_ref, rest)
        mix[:, at : at + HD] = jnp.zeros((mix.shape[0], HD), BF)
        mix[:, at : at + heads] = turned(r_ref[:, l])
        for i, ref in enumerate((q_ref, k_ref, v_ref)):
            mix[:, at + HD + mine * i : at + HD + mine * (i + 1)] = ref[l]
        group = early_ref if l == 0 else late_ref
        group[:, :ff] = gate_ref[l]
        group[:, ff : 2 * ff] = up_ref[l]
        group[:, 2 * ff : 3 * ff] = down_ref[l]
        group[:, 3 * ff : 3 * ff + mine] = og_ref[l]
        group[:, 3 * ff + mine : rest] = turned(out_ref[l])
        base = 2 * mine * l
        for h in range(heads):
            inner_ref[:, base + HD * h : base + HD * (h + 1)] = i1_ref[l, h]
            inner_ref[:, base + mine + HD * h : base + mine + HD * (h + 1)] = i2_ref[l, h]


def weight_grad_kernel(wide_ref, two_ref, branch_ref, other_ref, pre_ref, gate_ref, up_ref, hid_ref, ho_ref, out_ref):
    ff = gate_ref.shape[1]
    mine = pre_ref.shape[1]
    two = two_ref[...]
    out_ref[:, :ff] = tn(two, gate_ref[...]).astype(BF)
    out_ref[:, ff : 2 * ff] = tn(two, up_ref[...]).astype(BF)
    out_ref[:, 2 * ff : 3 * ff] = tn(branch_ref[...], hid_ref[...]).astype(BF)
    out_ref[:, 3 * ff : 3 * ff + mine] = tn(wide_ref[...], pre_ref[...]).astype(BF)
    out_ref[:, 3 * ff + mine :] = tn(other_ref[...], ho_ref[...]).astype(BF)


def weight_grads(wide, two, branch, other, pre, gate, up, hid, ho):
    rows, width = wide.shape
    step = 256
    left = pl.BlockSpec((rows, step), lambda i: (0, i))

    def whole(x):
        return pl.BlockSpec(x.shape, lambda i: (0, 0))

    cols = 3 * gate.shape[1] + 2 * pre.shape[1]
    return pl.pallas_call(
        weight_grad_kernel,
        grid=(width // step,),
        in_specs=[left] * 4 + [whole(x) for x in (pre, gate, up, hid, ho)],
        out_specs=pl.BlockSpec((step, cols), lambda i: (i, 0)),
        out_shape=jax.ShapeDtypeStruct((width, cols), BF),
        compiler_params=pltpu.CompilerParams(vmem_limit_bytes=32 * 2**20),
        cost_estimate=pl.CostEstimate(flops=2 * rows * width * cols, bytes_accessed=12 * 10**6, transcendentals=0),
    )(wide, two, branch, other, pre, gate, up, hid, ho)


def gather_small(x):
    size = lax.axis_size("line")
    other = lax.ppermute(x, "near", [(0, 1), (1, 0)])
    first = lax.axis_index("near") == 0
    pair = jnp.concatenate([jnp.where(first, x, other), jnp.where(first, other, x)], axis=0)
    if size > 4:
        return lax.all_gather(pair, "line", axis=0, tiled=True)
    parts = [pair] + [lax.ppermute(pair, "line", [(i, (i - k) % size) for i in range(size)]) for k in range(1, size)]
    start = lax.rem(size - lax.axis_index("line"), size) * pair.shape[0]
    return lax.dynamic_slice_in_dim(jnp.concatenate(parts + parts[:-1], axis=0), start, size * pair.shape[0], axis=0)


def scatter(x):
    return lax.psum_scatter(x, DP, scatter_dimension=0, tiled=True).astype(F32)


def exchange_sum(x):
    moved = lax.all_to_all(x, DP, split_axis=0, concat_axis=0, tiled=True)
    return jnp.sum(moved.astype(F32), axis=0)


def per_device(
    hidden_in, cotangent, w_query, w_key, w_value, w_outgate, w_rate, w_output, init_first, init_first_bias,
    init_second, init_second_bias, inner_gain, inner_shift, post_gain, post_shift, mixer_gain, mlp_gain,
    w_gate, w_up, w_down,
):
    layers, part, mine = w_query.shape
    heads = w_rate.shape[2]
    ff = w_gate.shape[2]
    inner_part = init_first.shape[3]
    small_part = inner_gain.shape[2]
    gain_part = mixer_gain.shape[1]
    dp = lax.axis_size("line") * lax.axis_size("near")
    tp = lax.axis_size("tensor")
    rows = hidden_in.shape[0]
    place = lax.axis_index("tensor").astype(jnp.int32).reshape(1)
    lead = HD - heads

    gains_here = jnp.concatenate([mixer_gain, mlp_gain], axis=0)
    gains_group = lax.all_gather(gains_here, "tensor", axis=1, tiled=True)
    span = 2 * mine + 6 * heads
    sds = jax.ShapeDtypeStruct
    rest_cols = 3 * ff + 2 * mine
    mix_here, early, late, inner_here = pl.pallas_call(
        pack_kernel,
        out_shape=[
            sds((part, PACK), BF),
            sds((part, rest_cols + PACK), BF),
            sds((part, rest_cols), BF),
            sds((inner_part, 2 * mine * layers), BF),
        ],
    )(
        w_query, w_key, w_value, w_outgate, w_rate.transpose(2, 0, 1), w_output, init_first.transpose(0, 1, 3, 2),
        init_second, w_gate, w_up, w_down.transpose(0, 2, 1),
    )
    smalls = jnp.concatenate([init_second_bias, inner_gain, inner_shift, post_gain, post_shift], axis=1)
    smalls = jnp.pad(smalls.reshape(layers * 5 * heads, small_part), ((0, 0), (0, inner_part - small_part)))
    biases = init_first_bias.reshape(layers * heads, inner_part)
    thin = jnp.concatenate([biases, smalls], axis=0).T
    inner_all = gather_small(jnp.concatenate([inner_here, thin, gains_group.reshape(inner_part, -1)], axis=1))
    mix_w = [gather(mix_here)]
    first_group, last_group = gather(early), gather(late)
    mix_w.append(first_group[:, rest_cols:])
    rest_w = [first_group[:, :rest_cols], last_group]
    states = 2 * mine * layers
    inner_in = []
    for l in range(layers):
        at = states + heads * layers + 5 * heads * l
        bias_at = states + heads * l
        inner_in.append(
            jnp.concatenate(
                [inner_all[:, 2 * mine * l : 2 * mine * (l + 1)], inner_all[:, bias_at : bias_at + heads],
                 inner_all[:, at : at + 5 * heads]],
                axis=1,
            )
        )
    gains = inner_all[:, layers * span :].reshape(dp, 2 * layers, tp * gain_part)
    gains = gains.transpose(1, 0, 2).reshape(2 * layers, D).astype(F32)
    edges = [0, ff, 2 * ff, 3 * ff, 3 * ff + mine, 3 * ff + 2 * mine]

    def piece(l, i):
        return rest_w[l][:, edges[i] : edges[i + 1]]

    residual = hidden_in.astype(F32)
    raw_wide = widen(hidden_in)
    kept = []
    for l in range(layers):
        gain_one, gain_two = gains[l], gains[layers + l]
        res_one = residual
        if l == 0:
            wide_res = raw_wide.astype(F32)
            wide, wide_scale = rms(wide_res, gain_one)
            wide_unit = wide_res * wide_scale
            scale_one = lax.rsqrt(jnp.mean(residual * residual, axis=1, keepdims=True) + EPS)
        else:
            normed, scale_one = rms(residual, gain_one)
            wide = widen(normed)
        pack = dot(wide, mix_w[l]).astype(BF)
        outs = forward_call(place, pack, inner_in[l], heads, dp)
        inner_out, saved, small = outs[0], outs[1:-1], outs[-1]
        pg = small[3 * heads : 4 * heads].reshape(-1)
        ps = small[4 * heads : 5 * heads].reshape(-1)
        gate_pre = dot(wide, piece(l, 3))
        sums = jnp.stack([jnp.sum(inner_out, axis=1), jnp.sum(inner_out * inner_out, axis=1)])
        sums = order_sum(sums)
        mean_all = sums[0] / D
        inv = lax.rsqrt(sums[1] / D - mean_all * mean_all + EPS)[:, None]
        unit = (inner_out - mean_all[:, None]) * inv
        post = unit * pg + ps
        heads_out = (jax.nn.gelu(gate_pre, approximate=True) * post).astype(BF)
        residual = residual + narrow(dot_t(heads_out, piece(l, 4)))
        res_two = residual
        normed, scale_two = rms(residual, gain_two)
        wide_two = widen(normed)
        gate = dot(wide_two, piece(l, 0))
        up = dot(wide_two, piece(l, 1))
        hidden = (jax.nn.silu(gate) * up).astype(BF)
        residual = residual + narrow(dot_t(hidden, piece(l, 2)))
        kept.append(
            (res_one, scale_one, wide, pack, saved, gate_pre, unit, inv, heads_out, res_two, scale_two, wide_two,
             gate, up, hidden, small, pg, ps)
        )
    block_out = residual.astype(BF)

    grad = cotangent.astype(F32)
    mix_grads, rest_grads = [None] * layers, [None] * layers
    gain_grads = [None] * (2 * layers)
    for l in reversed(range(layers)):
        gain_one, gain_two = gains[l], gains[layers + l]
        (res_one, scale_one, wide, pack, saved, gate_pre, unit, inv, heads_out, res_two, scale_two, wide_two,
         gate, up, hidden, small, pg, ps) = kept[l]
        branch = widen(cotangent if l == layers - 1 else grad.astype(BF))
        d_hidden = dot(branch, piece(l, 2))
        q = jax.nn.sigmoid(gate)
        swish = gate * q
        d_gate = (d_hidden * up * (q + swish * (1.0 - q))).astype(BF)
        d_up = (d_hidden * swish).astype(BF)
        d_norm = narrow(dot_t(d_gate, piece(l, 0)) + dot_t(d_up, piece(l, 1)))
        back, gain_grads[layers + l] = rms_back(res_two, scale_two, gain_two, d_norm)
        grad = grad + back
        branch_two = widen(grad.astype(BF))
        d_heads = dot(branch_two, piece(l, 4))
        post = unit * pg + ps
        ge, slope = gelu_two(gate_pre)
        d_pre = (d_heads * post * slope).astype(BF)
        d_post = d_heads * ge
        d_pg = jnp.sum(d_post * unit, axis=0)
        d_ps = jnp.sum(d_post, axis=0)
        p = d_post * pg
        sums = order_sum(jnp.stack([jnp.sum(p, axis=1), jnp.sum(p * unit, axis=1)])) / D
        d_inner = inv * (p - sums[0][:, None] - unit * sums[1][:, None])
        rest_sum = weight_grads(wide, wide_two, branch, branch_two, d_pre, d_gate, d_up, hidden, heads_out)
        rest_sum, d_inner = lax.optimization_barrier((rest_sum, d_inner))
        rest_grads[l] = scatter(rest_sum)
        d_pack, block = backward_call(place, pack, d_inner, saved, small, jnp.stack([d_pg, d_ps]), dp)
        d_wide = dot_t(d_pack, mix_w[l]) + dot_t(d_pre, piece(l, 3))
        d_norm = narrow(d_wide)
        back, gain_grads[l] = rms_back(res_one, scale_one, gain_one, d_norm)
        if l == 0:
            gain_grads[l] = jnp.sum(d_wide * wide_unit, axis=0)
        grad = grad + back
        if l > 0:
            grad, rest_grads[l] = lax.optimization_barrier((grad, rest_grads[l]))
        mats = t_dot(wide, d_pack)
        if l == 0:
            mats = mats + jnp.pad(jnp.stack(gain_grads).T, ((0, 0), (heads, PACK - heads - 2 * layers)))
        mixed = jnp.concatenate([mats.reshape(dp, part, PACK), block.reshape(dp, inner_part, PACK)], axis=1)
        mix_grads[l] = exchange_sum(mixed.astype(BF))
    grad_in = grad

    both = jnp.stack(mix_grads)
    mats, block = both[:, :part], both[:, part:]
    rest = jnp.stack(rest_grads)
    d_gains = lax.psum(mix_grads[0][:part, heads : heads + 2 * layers].T, "tensor")
    d_gains = lax.dynamic_slice_in_dim(d_gains, lax.axis_index("tensor") * gain_part, gain_part, axis=1)
    small = block[:, :small_part, 2 * mine + heads : span].transpose(0, 2, 1).reshape(layers, 5, heads, small_part)

    def matrix(i):
        return mats[:, :, HD + mine * i : HD + mine * (i + 1)]

    def tail_piece(i):
        return rest[:, :, edges[i] : edges[i + 1]]

    def state_part(i):
        return block[:, :, mine * i : mine * (i + 1)].reshape(layers, inner_part, heads, HD)

    return (
        block_out,
        grad_in,
        matrix(0),
        matrix(1),
        matrix(2),
        tail_piece(3),
        mats[:, :, :heads],
        tail_piece(4).transpose(0, 2, 1),
        state_part(0).transpose(0, 2, 3, 1),
        block[:, :, 2 * mine : 2 * mine + heads].transpose(0, 2, 1),
        state_part(1).transpose(0, 2, 1, 3),
        small[:, 0],
        small[:, 1],
        small[:, 2],
        small[:, 3],
        small[:, 4],
        d_gains[:layers],
        d_gains[layers:],
        tail_piece(0),
        tail_piece(1),
        tail_piece(2).transpose(0, 2, 1),
    )


def order_sum(sums):
    def turn(x, bit):
        parts = jnp.split(x, 4, axis=1)
        return jnp.concatenate([parts[i ^ bit] for i in range(4)], axis=1)

    sums = sums + turn(swap(sums, 1), 1)
    return sums + turn(swap(sums, 2), 2)


def solution(mesh):
    shape = (mesh.shape["dp"] // 2, 2, mesh.shape["tensor"])
    mesh = jax.sharding.Mesh(mesh.devices.reshape(shape), ("line", "near", "tensor"))
    placed = (
        P(("line", "near", "tensor"), None),
        P(("line", "near", "tensor"), None),
        P(None, DP, "tensor"),
        P(None, DP, "tensor"),
        P(None, DP, "tensor"),
        P(None, DP, "tensor"),
        P(None, DP, "tensor"),
        P(None, "tensor", DP),
        P(None, "tensor", None, DP),
        P(None, "tensor", DP),
        P(None, "tensor", DP, None),
        P(None, "tensor", DP),
        P(None, "tensor", DP),
        P(None, "tensor", DP),
        P(None, "tensor", DP),
        P(None, "tensor", DP),
        P(None, ("line", "near", "tensor")),
        P(None, ("line", "near", "tensor")),
        P(None, DP, "tensor"),
        P(None, DP, "tensor"),
        P(None, "tensor", DP),
    )
    return jax.shard_map(
        per_device,
        mesh=mesh,
        in_specs=placed,
        out_specs=(
            P(("line", "near", "tensor"), None),
            P(("line", "near", "tensor"), None),
            P(None, DP, "tensor"),
            P(None, DP, "tensor"),
            P(None, DP, "tensor"),
            P(None, DP, "tensor"),
            P(None, DP, "tensor"),
            P(None, "tensor", DP),
            P(None, "tensor", None, DP),
            P(None, "tensor", DP),
            P(None, "tensor", DP, None),
            P(None, "tensor", DP),
            P(None, "tensor", DP),
            P(None, "tensor", DP),
            P(None, "tensor", DP),
            P(None, "tensor", DP),
            P(None, ("line", "near", "tensor")),
            P(None, ("line", "near", "tensor")),
            P(None, DP, "tensor"),
            P(None, DP, "tensor"),
            P(None, "tensor", DP),
        ),
        check_vma=False,
    )
```

```python
import functools

import jax
import jax.numpy as jnp
from jax import lax
from jax.experimental import pallas as pl
from jax.sharding import PartitionSpec as P
from jax.experimental.pallas import tpu as pltpu

F32 = jnp.float32
BF = jnp.bfloat16
HD = 64
INNER = 256
CS = 16
CH = 128
STEPS = CH // CS
UNIT = 128
PACK = 640
EPS = 1e-6
K0 = 0.7978845608028654
K1 = 0.7978845608028654 * 0.044715


def mm(a, b, ca, cb):
    return lax.dot_general(
        a.astype(BF), b.astype(BF), (((ca,), (cb,)), ((), ())), preferred_element_type=F32
    )


def nn(a, b):
    return mm(a, b, 1, 0)


def nt(a, b):
    return mm(a, b, 1, 1)


def tn(a, b):
    return mm(a, b, 0, 0)


def gelu_two(z):
    zz = z * z
    t = jnp.tanh(z * (K0 + K1 * zz))
    half = 0.5 + 0.5 * t
    return z * half, half + 0.5 * z * (1.0 - t * t) * (K0 + 3.0 * K1 * zz)


def gelu_three(z):
    zz = z * z
    t = jnp.tanh(z * (K0 + K1 * zz))
    half = 0.5 + 0.5 * t
    rest = 1.0 - t * t
    p = K0 + 3.0 * K1 * zz
    return z * half, half + 0.5 * z * rest * p, rest * (p + 3.0 * K1 * zz - z * t * p * p)


def mean(x):
    return jnp.sum(x, axis=1, keepdims=True) * (1.0 / HD)


def masks():
    row = lax.broadcasted_iota(jnp.int32, (CH, CH), 0)
    col = lax.broadcasted_iota(jnp.int32, (CH, CH), 1)
    row_block, col_block = row >> 4, col >> 4
    inside = (row_block == col_block) & (col <= row)
    earlier = col_block < row_block
    own = 1.0 / ((row & (CS - 1)) + 1).astype(F32)
    coef = jnp.where(earlier, 1.0 / CS, jnp.where(inside, own, 0.0))
    return coef, jnp.where(earlier, 1.0, 0.0)


def split_pack(pack, heads):
    wide = pack.astype(F32)
    first = wide[:, :CH]
    turned = first.T
    rates_row = [jax.nn.sigmoid(turned[h : h + 1]) * (1.0 / HD) for h in range(heads)]
    rates_col = [jax.nn.sigmoid(first[:, h : h + 1]) * (1.0 / HD) for h in range(heads)]
    off = HD
    xq = [wide[:, off + HD * h : off + HD * (h + 1)] for h in range(heads)]
    off += HD * heads
    xk = [wide[:, off + HD * h : off + HD * (h + 1)] for h in range(heads)]
    off += HD * heads
    xv = [wide[:, off + HD * h : off + HD * (h + 1)] for h in range(heads)]
    return xq, xk, xv, rates_row, rates_col


def forward_kernel(
    heads, dp, place_ref, pack_ref, in_ref,
    o_ref, z1_ref, a_ref, z1b_ref, c_ref, z2b_ref, w1s_ref, w2s_ref, small_ref,
    w1, b1, w2, b2, pre, kke, cc, ecol, g1buf, g2buf, x2buf,
):
    H = range(heads)

    @pl.when(pl.program_id(0) == 0)
    def _():
        mine = heads * HD
        params = in_ref[...].astype(F32)
        first, second, rest = params[:, :mine].T, params[:, mine : 2 * mine].T, params[:, 2 * mine :]
        biases = rest.T
        few, step = HD // dp, INNER // dp
        small = jnp.concatenate([rest[step * d : step * d + few] for d in range(dp)], axis=0).T
        small_ref[...] = small[heads:]
        for h in H:
            w1[h] = first[HD * h : HD * (h + 1)]
            w2_own = second[HD * h : HD * (h + 1)]
            w2[h] = w2_own - jnp.mean(w2_own, axis=0, keepdims=True)
            b1[h] = biases[h : h + 1]
            b2_own = small[heads + h : heads + h + 1]
            b2[h] = b2_own - mean(b2_own)
        g1buf[...] = jnp.zeros_like(g1buf)

    coef, before = masks()
    xq, xk, xv, rrow, rcol = split_pack(pack_ref[...], heads)
    b2_start = [b2[h] for h in H]
    mcc = []
    for h in H:
        pre[h] = nn(xk[h], w1[h]) + b1[h]
        kke[h] = ((nt(xk[h], xk[h]) + 1.0) * (before * (rrow[h] * (1.0 / CS)))).astype(BF)
        g, sh = small_ref[heads + h : heads + h + 1], small_ref[2 * heads + h : 2 * heads + h + 1]
        cval = (sh - xv[h] + xk[h]) * g
        cc[h] = cval
        mcc.append(mean(cval))
        ecol[h] = jnp.broadcast_to(rcol[h] * (1.0 / CS), (CH, HD))
        w1s_ref[0, h] = w1[h].astype(w1s_ref.dtype)
    w1_start = [w1[h].astype(BF) for h in H]
    w2_start = [w2[h].astype(BF) for h in H]
    b1_start = [b1[h] for h in H]

    def finish(k):
        part, upto = slice(UNIT * k, UNIT * (k + 1)), UNIT * (k + 1)
        mask = [coef[part, :upto] * rrow[h][:, :upto] for h in H]
        score = [nt(xq[h][part], xk[h][:upto]) + 1.0 for h in H]
        z1b = [nn(xq[h][part], w1_start[h]) + b1_start[h] - nn(score[h] * mask[h], g1buf[h, :upto, :]) for h in H]
        x2q = [jax.nn.gelu(z1b[h], approximate=True).astype(BF) for h in H]
        p = [nt(x2q[h], x2buf[h, :upto, :]) + 1.0 for h in H]
        z2b = [nt(x2q[h], w2_start[h]) + b2_start[h] - nn(p[h] * mask[h], g2buf[h, :upto, :]) for h in H]
        for h in H:
            z1b_ref[part, INNER * h : INNER * (h + 1)] = z1b[h].astype(BF)
            centred = z2b[h] - mean(z2b[h])
            z2b_ref[h, part, :] = centred.astype(BF)
            unit = centred * lax.rsqrt(mean(centred * centred) + EPS)
            o_ref[part, HD * h : HD * (h + 1)] = (
                xq[h][part] + unit * small_ref[heads + h : heads + h + 1] + small_ref[2 * heads + h : 2 * heads + h + 1]
            )

    ma = [mean(small_ref[heads + h : heads + h + 1] * small_ref[heads + h : heads + h + 1]) for h in H]
    w2v = [w2[h] for h in H]
    b2v = list(b2_start)
    for i in range(STEPS):
        rows = slice(CS * i, CS * (i + 1))
        z1 = [pre[h, rows, :] for h in H]
        if i >= 2:
            z1 = [z1[h] - nn(kke[h, rows, : CS * (i - 1)], g1buf[h, : CS * (i - 1), :]) for h in H]
        if i >= 1:
            z1 = [z1[h] - nn(kke[h, rows, :][:, CS * (i - 1) : CS * i], g1buf[h, CS * (i - 1) : CS * i, :]) for h in H]
        xd = [gelu_two(z1[h]) for h in H]
        x2b = [xd[h][0].astype(BF) for h in H]
        w2b = [w2v[h].astype(BF) for h in H]
        c = [nt(x2b[h], w2b[h]) + b2v[h] for h in H]
        g2 = []
        for h in H:
            g = small_ref[heads + h : heads + h + 1]
            a = g * g
            ca = c[h] * a
            cch = cc[h, rows, :]
            mc = mcc[h][rows]
            mu, q1, q2, q3, q4 = mean(c[h]), mean(c[h] * c[h]), mean(ca), mean(ca * c[h]), mean(c[h] * cch)
            s = lax.rsqrt(q1 - mu * mu + EPS)
            m1 = s * (q2 - mu * ma[h]) + mc
            m2 = s * (s * (q3 - mu * (2.0 * q2 - mu * ma[h])) + (q4 - mu * mc))
            c[h] = c[h] - mu
            g2.append(s * (c[h] * (s * (a - m2)) + cch - m1))
        av = [nn(g2[h], w2b[h]) for h in H]
        g1 = [av[h] * xd[h][1] for h in H]
        for h in H:
            g1buf[h, rows, :] = g1[h].astype(BF)
            g2buf[h, rows, :] = g2[h].astype(BF)
            x2buf[h, rows, :] = x2b[h]
            w2s_ref[i, h] = w2b[h].astype(w2s_ref.dtype)
            z1_ref[rows, INNER * h : INNER * (h + 1)] = z1[h].astype(BF)
            a_ref[rows, INNER * h : INNER * (h + 1)] = av[h].astype(BF)
            c_ref[h, rows, :] = c[h].astype(BF)
            eg2 = ecol[h, rows, :] * g2[h]
            w2v[h] = w2v[h] - tn(eg2, x2b[h])
            b2v[h] = b2v[h] - jnp.sum(eg2, axis=0, keepdims=True)
        if (i + 1) % (UNIT // CS) == 0:
            finish(i // (UNIT // CS))
    for h in H:
        g1 = g1buf[h]
        w1[h] = w1[h] - tn(ecol[h] * xk[h], g1)
        b1[h] = b1[h] - jnp.sum(ecol[h][:, :1] * g1.astype(F32), axis=0, keepdims=True)
        w2[h] = w2v[h]
        b2[h] = b2v[h]


def forward_call(place, pack, params, heads, dp):
    rows = pack.shape[0]
    chunks = rows // CH
    per_block = chunks // 4

    def spot(c, place):
        return ((c // per_block) ^ place[0]) * per_block + c % per_block

    def whole(*shape):
        return pl.BlockSpec(shape, lambda c, place: (0,) * len(shape))

    def moved(n):
        return pl.BlockSpec((CH, n), lambda c, place: (spot(c, place), 0))

    def kept(n):
        return pl.BlockSpec((CH, n), lambda c, place: (c, 0))

    by_head = pl.BlockSpec((heads, CH, HD), lambda c, place: (0, c, 0))
    sds = jax.ShapeDtypeStruct
    return pl.pallas_call(
        functools.partial(forward_kernel, heads, dp),
        grid_spec=pltpu.PrefetchScalarGridSpec(
            num_scalar_prefetch=1,
            grid=(chunks,),
            in_specs=[
                moved(PACK),
                whole(*params.shape),
            ],
            out_specs=[
                moved(heads * HD),
                kept(heads * INNER),
                kept(heads * INNER),
                kept(heads * INNER),
                by_head,
                by_head,
                pl.BlockSpec((1, heads, HD, INNER), lambda c, place: (c, 0, 0, 0)),
                pl.BlockSpec((STEPS, heads, HD, INNER), lambda c, place: (c, 0, 0, 0)),
                whole(5 * heads, HD),
            ],
            scratch_shapes=[
                pltpu.VMEM((heads, HD, INNER), F32),
                pltpu.VMEM((heads, 1, INNER), F32),
                pltpu.VMEM((heads, HD, INNER), F32),
                pltpu.VMEM((heads, 1, HD), F32),
                pltpu.VMEM((heads, CH, INNER), F32),
                pltpu.VMEM((heads, CH, CH), BF),
                pltpu.VMEM((heads, CH, HD), F32),
                pltpu.VMEM((heads, CH, HD), F32),
                pltpu.VMEM((heads, CH, INNER), BF),
                pltpu.VMEM((heads, CH, HD), BF),
                pltpu.VMEM((heads, CH, INNER), BF),
            ],
        ),
        out_shape=[
            sds((rows, heads * HD), F32),
            sds((rows, heads * INNER), BF),
            sds((rows, heads * INNER), BF),
            sds((rows, heads * INNER), BF),
            sds((heads, rows, HD), BF),
            sds((heads, rows, HD), BF),
            sds((chunks, heads, HD, INNER), BF),
            sds((chunks * STEPS, heads, HD, INNER), BF),
            sds((5 * heads, HD), F32),
        ],
        compiler_params=pltpu.CompilerParams(vmem_limit_bytes=56 * 2**20),
        cost_estimate=pl.CostEstimate(flops=65 * 10**9, bytes_accessed=25 * 10**6, transcendentals=0),
    )(place, pack, params)


def backward_kernel(
    heads, shares, place_ref, pack_ref, do_ref, z1_ref, a_ref, z1b_ref, c_ref, z2b_ref, w1s_ref, w2s_ref, small_ref, post_ref,
    dpack_ref, block_ref, dw1, db1, dw2, db2, dg_ref, dh_ref,
    dg1b, dg2b, dx2b, d1v, ad2, g2v, kkt, dz1buf, k1v, k2v, dyv, ecol, x2buf,
):
    H = range(heads)

    @pl.when(pl.program_id(0) == 0)
    def _():
        dw1[...] = jnp.zeros_like(dw1)
        db1[...] = jnp.zeros_like(db1)
        dw2[...] = jnp.zeros_like(dw2)
        db2[...] = jnp.zeros_like(db2)
        dg_ref[...] = jnp.zeros_like(dg_ref)
        dh_ref[...] = jnp.zeros_like(dh_ref)
        dz1buf[...] = jnp.zeros_like(dz1buf)

    coef, before = masks()
    xq, xk, xv, rrow, rcol = split_pack(pack_ref[...], heads)
    wides = [slice(INNER * h, INNER * (h + 1)) for h in H]
    gains = [small_ref[heads + h : heads + h + 1] for h in H]
    shifts = [small_ref[2 * heads + h : 2 * heads + h + 1] for h in H]
    w1_start = [w1s_ref[0, h] for h in H]
    w2_start = [w2s_ref[0, h] for h in H]
    mask = [coef * rrow[h] for h in H]
    do = [do_ref[:, HD * h : HD * (h + 1)].astype(F32) for h in H]
    dz2b = []
    for h in H:
        z2b = z2b_ref[h].astype(F32)
        sb = lax.rsqrt(mean(z2b * z2b) + EPS)
        ub = z2b * sb
        dog = do[h] * gains[h]
        dg_ref[h] += jnp.sum(do[h] * ub, axis=0, keepdims=True)
        dh_ref[h] += jnp.sum(do[h], axis=0, keepdims=True)
        dz2b.append(sb * (dog - mean(dog) - ub * mean(dog * ub)))
    uv, yv, st, g2_all = [], [], [], []
    for h in H:
        a = gains[h] * gains[h]
        c = c_ref[h].astype(F32)
        cch = (shifts[h] - xv[h] + xk[h]) * gains[h]
        ca = c * a
        q1, q2, q3, q4 = mean(c * c), mean(ca), mean(ca * c), mean(c * cch)
        s = lax.rsqrt(q1 + EPS)
        m1 = s * q2 + mean(cch)
        m2 = s * (s * q3 + q4)
        u = c * s
        y = u * a + cch
        g2 = s * (y - m1 - u * m2)
        uv.append(u)
        yv.append(y)
        st.append((s, m2, s * q2, s * s * q3, mean(y), mean(a)))
        g2v[h] = g2
        g2_all.append(g2.astype(BF))
        ecol[h] = jnp.broadcast_to(rcol[h] * (1.0 / CS), (CH, HD))
    x2_all, g1_all, x2q, d1b = [], [], [], []
    for h in H:
        x2, d1, slope2 = gelu_three(z1_ref[:, wides[h]].astype(F32))
        av = a_ref[:, wides[h]].astype(F32)
        d1v[h] = d1
        ad2[h] = av * slope2
        x2_all.append(x2.astype(BF))
        x2buf[h] = x2_all[h]
        g1_all.append((av * d1).astype(BF))
    for h in H:
        value, slope = gelu_two(z1b_ref[:, wides[h]].astype(F32))
        x2q.append(value.astype(BF))
        d1b.append(slope)
    before_t = before.T
    sc = [nt(xq[h], xk[h]) + 1.0 for h in H]
    for h in H:
        kkt[h] = ((nt(xk[h], xk[h]) + 1.0) * before_t).astype(BF)
    p = [nt(x2q[h], x2_all[h]) + 1.0 for h in H]
    dm2 = [-nt(dz2b[h], g2_all[h]) for h in H]
    dpv = [(mask[h] * dm2[h]).astype(BF) for h in H]
    dz1b = [(nn(dz2b[h], w2_start[h]) + nn(dpv[h], x2_all[h])) * d1b[h] for h in H]
    for h in H:
        dg2b[h] = -tn(mask[h] * p[h], dz2b[h])
    for h in H:
        dx2b[h] = tn(dpv[h], x2q[h])
    dw2_out = [tn(dz2b[h], x2q[h]) for h in H]
    db2_out = [jnp.sum(dz2b[h], axis=0, keepdims=True) for h in H]
    db1_out = [jnp.sum(dz1b[h], axis=0, keepdims=True) for h in H]
    dz1c = [dz1b[h].astype(BF) for h in H]
    dm1 = [-nt(dz1c[h], g1_all[h]) for h in H]
    dsv = [(mask[h] * dm1[h]).astype(BF) for h in H]
    for h in H:
        dg1b[h] = -tn(mask[h] * sc[h], dz1c[h])
    for h in H:
        k1v[h] = nn(xk[h], dw1[h]) + db1[h]
    dr_row = [jnp.sum(coef * (sc[h] * dm1[h] + p[h] * dm2[h]), axis=0, keepdims=True) for h in H]
    dxq = [do[h] + nt(dz1c[h], w1_start[h]) + nn(dsv[h], xk[h]) for h in H]
    dxk = [tn(dsv[h], xq[h]) - nt((rcol[h] * (1.0 / CS)) * g1_all[h].astype(F32), dw1[h]) for h in H]
    dw1_out = [tn(xq[h], dz1c[h]) for h in H]
    d2 = [dw2[h] for h in H]
    e2 = [db2[h] for h in H]
    for i in reversed(range(STEPS)):
        rows = slice(CS * i, CS * (i + 1))
        k1 = [k1v[h, rows, :] for h in H]
        if i < STEPS - 2:
            k1 = [k1[h] + nn(kkt[h, rows, :][:, CS * (i + 2) :], dz1buf[h, CS * (i + 2) :, :]) for h in H]
        if i < STEPS - 1:
            k1 = [k1[h] + nn(kkt[h, rows, :][:, CS * (i + 1) : CS * (i + 2)], dz1buf[h, CS * (i + 1) : CS * (i + 2), :]) for h in H]
        dg1 = [dg1b[h, rows, :] - ecol[h, rows, :][:, :1] * k1[h] for h in H]
        da = [(dg1[h] * d1v[h, rows, :]).astype(BF) for h in H]
        d2b = [d2[h].astype(BF) for h in H]
        w2i = [w2s_ref[i, h] for h in H]
        g2 = [g2v[h, rows, :] for h in H]
        k2 = [nt(x2buf[h, rows, :], d2b[h]) + e2[h] for h in H]
        dg2 = [dg2b[h, rows, :] - ecol[h, rows, :] * k2[h] + nt(da[h], w2i[h]) for h in H]
        l2 = [dx2b[h, rows, :] - nn(ecol[h, rows, :] * g2[h], d2b[h]) for h in H]
        dz2 = []
        for h in H:
            g = small_ref[heads + h : heads + h + 1]
            a = g * g
            s, m2, mau, mauu, my = (q[rows] for q in st[h][:5])
            ma = st[h][5]
            u, y = uv[h][rows], yv[h][rows]
            dv = dg2[h]
            dva = dv * a
            n1, n2, n3, n4, n5 = mean(dv), mean(dv * u), mean(dv * g2[h]), mean(dva * u), mean(dva)
            dy = s * (dv - n1 - u * n2)
            muu = s * (n4 - n1 * mau - n2 * (mauu + 2.0 * m2))
            mu = s * (n5 - n1 * (ma + m2) - n2 * (mau + my))
            dz2.append(s * (dy * a - (s * m2) * dv - (s * n2) * y - mu - u * (muu + n3)))
            dyv[h, rows, :] = dy
            k2v[h, rows, :] = k2[h]
        dx2 = [l2[h] + nn(dz2[h], w2i[h]) for h in H]
        dz1 = [dx2[h] * d1v[h, rows, :] + dg1[h] * ad2[h, rows, :] for h in H]
        for h in H:
            dz1buf[h, rows, :] = dz1[h].astype(BF)
            d2[h] = d2[h] + tn(
                jnp.concatenate([g2[h], dz2[h]], axis=0), jnp.concatenate([da[h], x2buf[h, rows, :]], axis=0)
            )
            e2[h] = e2[h] + jnp.sum(dz2[h], axis=0, keepdims=True)
    dz1 = [dz1buf[h] for h in H]
    k1 = [k1v[h] + nn(kkt[h], dz1[h]) for h in H]
    dkk = [(-nt(dz1[h], g1_all[h]) * (before * (rrow[h] * (1.0 / CS)))).astype(BF) for h in H]
    dyg = [dyv[h] * gains[h] for h in H]
    dk = [dxk[h] + nt(dz1[h], w1_start[h]) + dyg[h] for h in H]
    dk = [dk[h] + nn(dkk[h], xk[h]) + tn(dkk[h], xk[h]) for h in H]
    de_col = [
        jnp.sum(g1_all[h].astype(F32) * k1[h], axis=1, keepdims=True)
        + jnp.sum(g2v[h] * k2v[h], axis=1, keepdims=True)
        for h in H
    ]
    for h in H:
        dg_ref[h] += jnp.sum(dyv[h] * (uv[h] * gains[h] * 2.0 + shifts[h] - xv[h] + xk[h]), axis=0, keepdims=True)
        dh_ref[h] += jnp.sum(dyg[h], axis=0, keepdims=True)
        off = HD + HD * h
        dpack_ref[:, off : off + HD] = dxq[h].astype(BF)
        off += HD * heads
        dpack_ref[:, off : off + HD] = dk[h].astype(BF)
        off += HD * heads
        dpack_ref[:, off : off + HD] = (-dyg[h]).astype(BF)
    for h in H:
        dw1[h] = dw1[h] + dw1_out[h] + tn(xk[h], dz1[h])
        db1[h] = db1[h] + db1_out[h] + jnp.sum(dz1[h].astype(F32), axis=0, keepdims=True)
        dw2[h] = d2[h] + dw2_out[h]
        db2[h] = e2[h] + db2_out[h]
    sub = lax.broadcasted_iota(jnp.int32, (CH, CH), 0)
    lane = lax.broadcasted_iota(jnp.int32, (CH, CH), 1)
    stack = jnp.zeros((CH, CH), F32)
    cols = jnp.zeros((CH, CH), F32)
    for h in H:
        stack = stack + jnp.where(sub == h, dr_row[h], 0.0)
        slope = rcol[h] * (1.0 - HD * rcol[h])
        cols = cols + jnp.where(lane == h, slope, 0.0)
    turned = stack.T
    for h in H:
        turned = turned - jnp.where(lane == h, de_col[h] * (1.0 / CS), 0.0)
    dpack_ref[:, :HD] = (turned * cols)[:, :HD].astype(dpack_ref.dtype)

    @pl.when(pl.program_id(0) == pl.num_programs(0) - 1)
    def _():
        mine = heads * HD
        block_ref[...] = jnp.zeros_like(block_ref)
        for h in H:
            block_ref[:, HD * h : HD * (h + 1)] = dw1[h].T
            block_ref[:, mine + HD * h : mine + HD * (h + 1)] = dw2[h].T
        bias = jnp.concatenate([db1[h] for h in H] + [jnp.zeros((8 - heads, INNER), F32)], axis=0)
        block_ref[:, 2 * mine : 2 * mine + heads] = bias.T[:, :heads]
        lines = [db2[h] for h in H] + [dg_ref[h] for h in H] + [dh_ref[h] for h in H]
        lines += [post_ref[i : i + 1, HD * h : HD * (h + 1)] for i in range(2) for h in H]
        few, step = HD // shares, INNER // shares
        small = jnp.concatenate(lines + [jnp.zeros((16 - 5 * heads, HD), F32)], axis=0).T
        for d in range(shares):
            block_ref[step * d : step * d + few, 2 * mine + heads : 2 * mine + 6 * heads] = small[
                few * d : few * (d + 1), : 5 * heads
            ]


def backward_call(place, pack, do, saved, small, post, dp):
    z1, a, z1b, c, z2b, w1s, w2s = saved
    heads = small.shape[0] // 5
    rows = pack.shape[0]
    chunks = rows // CH
    last = chunks - 1
    per_block = chunks // 4

    def spot(c, place):
        return (((last - c) // per_block) ^ place[0]) * per_block + (last - c) % per_block

    def whole(*shape):
        return pl.BlockSpec(shape, lambda c, place: (0,) * len(shape))

    def moved(n):
        return pl.BlockSpec((CH, n), lambda c, place: (spot(c, place), 0))

    def kept(n):
        return pl.BlockSpec((CH, n), lambda c, place: (last - c, 0))

    by_head = pl.BlockSpec((heads, CH, HD), lambda c, place: (0, last - c, 0))
    sds = jax.ShapeDtypeStruct
    return pl.pallas_call(
        functools.partial(backward_kernel, heads, dp),
        grid_spec=pltpu.PrefetchScalarGridSpec(
            num_scalar_prefetch=1,
            grid=(chunks,),
            in_specs=[
                moved(PACK),
                moved(heads * HD),
                kept(heads * INNER),
                kept(heads * INNER),
                kept(heads * INNER),
                by_head,
                by_head,
                pl.BlockSpec((1, heads, HD, INNER), lambda c, place: (last - c, 0, 0, 0)),
                pl.BlockSpec((STEPS, heads, HD, INNER), lambda c, place: (last - c, 0, 0, 0)),
                whole(*small.shape),
                whole(*post.shape),
            ],
            out_specs=[moved(PACK), whole(INNER, PACK)],
            scratch_shapes=[
                pltpu.VMEM((heads, HD, INNER), F32),
                pltpu.VMEM((heads, 1, INNER), F32),
                pltpu.VMEM((heads, HD, INNER), F32),
                pltpu.VMEM((heads, 1, HD), F32),
                pltpu.VMEM((heads, 1, HD), F32),
                pltpu.VMEM((heads, 1, HD), F32),
                pltpu.VMEM((heads, CH, INNER), F32),
                pltpu.VMEM((heads, CH, HD), F32),
                pltpu.VMEM((heads, CH, INNER), F32),
                pltpu.VMEM((heads, CH, INNER), F32),
                pltpu.VMEM((heads, CH, INNER), F32),
                pltpu.VMEM((heads, CH, HD), F32),
                pltpu.VMEM((heads, CH, CH), BF),
                pltpu.VMEM((heads, CH, INNER), BF),
                pltpu.VMEM((heads, CH, INNER), F32),
                pltpu.VMEM((heads, CH, HD), F32),
                pltpu.VMEM((heads, CH, HD), F32),
                pltpu.VMEM((heads, CH, HD), F32),
                pltpu.VMEM((heads, CH, INNER), BF),
            ],
        ),
        out_shape=[
            sds((rows, PACK), BF),
            sds((INNER, PACK), F32),
        ],
        compiler_params=pltpu.CompilerParams(vmem_limit_bytes=56 * 2**20),
        cost_estimate=pl.CostEstimate(flops=70 * 10**9, bytes_accessed=25 * 10**6, transcendentals=0),
    )(place, pack, do, z1, a, z1b, c, z2b, w1s, w2s, small, post)


D = 768
DP = ("line", "near")


def swap(x, bit):
    size = lax.axis_size("tensor")
    return lax.ppermute(x, "tensor", [(i, i ^ bit) for i in range(size)])


def widen(x):
    far = swap(x, 2)
    return jnp.concatenate([x, swap(x, 1), far, swap(far, 1)], axis=0)


def narrow_start(total):
    quarter = total.shape[0] // 4
    near, pair, far, cross = [total[quarter * i : quarter * (i + 1)] for i in range(4)]
    far = (far + swap(cross.astype(BF), 1).astype(F32)).astype(BF)
    return near + swap(pair.astype(BF), 1).astype(F32), far


def narrow(total):
    near, far = narrow_start(total)
    return near + swap(far, 2).astype(F32)


def sum_all(x):
    for axis in ("tensor", "near", "line"):
        size, bit = lax.axis_size(axis), 1
        while bit < size:
            x = x + lax.ppermute(x, axis, [(i, i ^ bit) for i in range(size)])
            bit *= 2
    return x


def dot(a, b):
    return lax.dot_general(a, b, (((1,), (0,)), ((), ())), preferred_element_type=F32)


def dot_t(a, b):
    return lax.dot_general(a, b, (((1,), (1,)), ((), ())), preferred_element_type=F32)


def t_dot(a, b):
    return lax.dot_general(a, b, (((0,), (0,)), ((), ())), preferred_element_type=F32)


def rms(x, gain):
    scale = lax.rsqrt(jnp.mean(x * x, axis=1, keepdims=True) + EPS)
    return (x * scale * gain).astype(BF), scale


def rms_back(x, scale, gain, grad):
    q = grad * gain
    back = scale * q - x * (scale * scale * scale) * jnp.mean(q * x, axis=1, keepdims=True)
    return back, jnp.sum(grad * (x * scale), axis=0)


def gather(x):
    return lax.all_gather(x, DP, axis=0, tiled=True)


def turned(x):
    return x.astype(F32).T.astype(BF)


def pack_kernel(
    q_ref, k_ref, v_ref, og_ref, r_ref, out_ref, i1_ref, i2_ref, gate_ref, up_ref, down_ref,
    mix_ref, early_ref, late_ref, inner_ref,
):
    heads = r_ref.shape[0]
    mine = heads * HD
    ff = gate_ref.shape[2]
    rest = 3 * ff + 2 * mine
    for l in range(2):
        mix, at = (mix_ref, 0) if l == 0 else (early_ref, rest)
        mix[:, at : at + HD] = jnp.zeros((mix.shape[0], HD), BF)
        mix[:, at : at + heads] = turned(r_ref[:, l])
        for i, ref in enumerate((q_ref, k_ref, v_ref)):
            mix[:, at + HD + mine * i : at + HD + mine * (i + 1)] = ref[l]
        group = early_ref if l == 0 else late_ref
        group[:, :ff] = gate_ref[l]
        group[:, ff : 2 * ff] = up_ref[l]
        group[:, 2 * ff : 3 * ff] = down_ref[l]
        group[:, 3 * ff : 3 * ff + mine] = og_ref[l]
        group[:, 3 * ff + mine : rest] = turned(out_ref[l])
        base = 2 * mine * l
        for h in range(heads):
            inner_ref[:, base + HD * h : base + HD * (h + 1)] = i1_ref[l, h]
            inner_ref[:, base + mine + HD * h : base + mine + HD * (h + 1)] = i2_ref[l, h]


def weight_grad_kernel(wide_ref, two_ref, branch_ref, other_ref, pre_ref, gate_ref, up_ref, hid_ref, ho_ref, out_ref):
    ff = gate_ref.shape[1]
    mine = pre_ref.shape[1]
    two = two_ref[...]
    out_ref[:, :ff] = tn(two, gate_ref[...]).astype(BF)
    out_ref[:, ff : 2 * ff] = tn(two, up_ref[...]).astype(BF)
    out_ref[:, 2 * ff : 3 * ff] = tn(branch_ref[...], hid_ref[...]).astype(BF)
    out_ref[:, 3 * ff : 3 * ff + mine] = tn(wide_ref[...], pre_ref[...]).astype(BF)
    out_ref[:, 3 * ff + mine :] = tn(other_ref[...], ho_ref[...]).astype(BF)


def weight_grads(wide, two, branch, other, pre, gate, up, hid, ho):
    rows, width = wide.shape
    step = 256
    left = pl.BlockSpec((rows, step), lambda i: (0, i))

    def whole(x):
        return pl.BlockSpec(x.shape, lambda i: (0, 0))

    cols = 3 * gate.shape[1] + 2 * pre.shape[1]
    return pl.pallas_call(
        weight_grad_kernel,
        grid=(width // step,),
        in_specs=[left] * 4 + [whole(x) for x in (pre, gate, up, hid, ho)],
        out_specs=pl.BlockSpec((step, cols), lambda i: (i, 0)),
        out_shape=jax.ShapeDtypeStruct((width, cols), BF),
        compiler_params=pltpu.CompilerParams(vmem_limit_bytes=32 * 2**20),
        cost_estimate=pl.CostEstimate(flops=2 * rows * width * cols, bytes_accessed=12 * 10**6, transcendentals=0),
    )(wide, two, branch, other, pre, gate, up, hid, ho)


def gather_small(x):
    size = lax.axis_size("line")
    other = lax.ppermute(x, "near", [(0, 1), (1, 0)])
    first = lax.axis_index("near") == 0
    pair = jnp.concatenate([jnp.where(first, x, other), jnp.where(first, other, x)], axis=0)
    if size > 4:
        return lax.all_gather(pair, "line", axis=0, tiled=True)
    parts = [pair] + [lax.ppermute(pair, "line", [(i, (i - k) % size) for i in range(size)]) for k in range(1, size)]
    start = lax.rem(size - lax.axis_index("line"), size) * pair.shape[0]
    return lax.dynamic_slice_in_dim(jnp.concatenate(parts + parts[:-1], axis=0), start, size * pair.shape[0], axis=0)


def scatter(x):
    return lax.psum_scatter(x, DP, scatter_dimension=0, tiled=True).astype(F32)


def exchange_sum(x):
    moved = lax.all_to_all(x, DP, split_axis=0, concat_axis=0, tiled=True)
    return jnp.sum(moved.astype(F32), axis=0)


def per_device(
    hidden_in, cotangent, w_query, w_key, w_value, w_outgate, w_rate, w_output, init_first, init_first_bias,
    init_second, init_second_bias, inner_gain, inner_shift, post_gain, post_shift, mixer_gain, mlp_gain,
    w_gate, w_up, w_down,
):
    layers, part, mine = w_query.shape
    heads = w_rate.shape[2]
    ff = w_gate.shape[2]
    inner_part = init_first.shape[3]
    small_part = inner_gain.shape[2]
    gain_part = mixer_gain.shape[1]
    dp = lax.axis_size("line") * lax.axis_size("near")
    tp = lax.axis_size("tensor")
    rows = hidden_in.shape[0]
    place = lax.axis_index("tensor").astype(jnp.int32).reshape(1)
    lead = HD - heads

    gains_here = jnp.concatenate([mixer_gain, mlp_gain], axis=0)
    gains_group = lax.all_gather(gains_here, "tensor", axis=1, tiled=True)
    span = 2 * mine + 6 * heads
    sds = jax.ShapeDtypeStruct
    rest_cols = 3 * ff + 2 * mine
    mix_here, early, late, inner_here = pl.pallas_call(
        pack_kernel,
        out_shape=[
            sds((part, PACK), BF),
            sds((part, rest_cols + PACK), BF),
            sds((part, rest_cols), BF),
            sds((inner_part, 2 * mine * layers), BF),
        ],
    )(
        w_query, w_key, w_value, w_outgate, w_rate.transpose(2, 0, 1), w_output, init_first.transpose(0, 1, 3, 2),
        init_second, w_gate, w_up, w_down.transpose(0, 2, 1),
    )
    smalls = jnp.concatenate([init_second_bias, inner_gain, inner_shift, post_gain, post_shift], axis=1)
    smalls = jnp.pad(smalls.reshape(layers * 5 * heads, small_part), ((0, 0), (0, inner_part - small_part)))
    biases = init_first_bias.reshape(layers * heads, inner_part)
    thin = jnp.concatenate([biases, smalls], axis=0).T
    raw_near, raw_far = swap(hidden_in, 1), swap(hidden_in, 2)
    thin, raw_near, raw_far = lax.optimization_barrier((thin, raw_near, raw_far))
    inner_all = gather_small(jnp.concatenate([inner_here, thin, gains_group.reshape(inner_part, -1)], axis=1))
    mix_here, early, inner_all = lax.optimization_barrier((mix_here, early, inner_all))
    mix_w = [gather(mix_here)]
    first_group, last_group = gather(early), gather(late)
    mix_w.append(first_group[:, rest_cols:])
    rest_w = [first_group[:, :rest_cols], last_group]
    states = 2 * mine * layers
    inner_in = []
    for l in range(layers):
        at = states + heads * layers + 5 * heads * l
        bias_at = states + heads * l
        inner_in.append(
            jnp.concatenate(
                [inner_all[:, 2 * mine * l : 2 * mine * (l + 1)], inner_all[:, bias_at : bias_at + heads],
                 inner_all[:, at : at + 5 * heads]],
                axis=1,
            )
        )
    gains = inner_all[:, layers * span :].reshape(dp, 2 * layers, tp * gain_part)
    gains = gains.transpose(1, 0, 2).reshape(2 * layers, D).astype(F32)
    edges = [0, ff, 2 * ff, 3 * ff, 3 * ff + mine, 3 * ff + 2 * mine]

    def piece(l, i):
        return rest_w[l][:, edges[i] : edges[i + 1]]

    residual = hidden_in.astype(F32)
    raw_wide = jnp.concatenate([hidden_in, raw_near, raw_far, swap(raw_far, 1)], axis=0)
    top_near, top_far = swap(cotangent, 1), swap(cotangent, 2)
    kept = []
    for l in range(layers):
        gain_one, gain_two = gains[l], gains[layers + l]
        res_one = residual
        if l == 0:
            wide_res = raw_wide.astype(F32)
            wide, wide_scale = rms(wide_res, gain_one)
            wide_unit = wide_res * wide_scale
            scale_one = lax.rsqrt(jnp.mean(residual * residual, axis=1, keepdims=True) + EPS)
        else:
            normed, scale_one = rms(residual, gain_one)
            wide = widen(normed)
        pack = dot(wide, mix_w[l]).astype(BF)
        outs = forward_call(place, pack, inner_in[l], heads, dp)
        inner_out, saved, small = outs[0], outs[1:-1], outs[-1]
        if l == 0:
            inner_out, top_near, top_far = lax.optimization_barrier((inner_out, top_near, top_far))
        pg = small[3 * heads : 4 * heads].reshape(-1)
        ps = small[4 * heads : 5 * heads].reshape(-1)
        gate_pre = dot(wide, piece(l, 3))
        sums = jnp.stack([jnp.sum(inner_out, axis=1), jnp.sum(inner_out * inner_out, axis=1)])
        sums = order_sum(sums)
        mean_all = sums[0] / D
        inv = lax.rsqrt(sums[1] / D - mean_all * mean_all + EPS)[:, None]
        unit = (inner_out - mean_all[:, None]) * inv
        post = unit * pg + ps
        heads_out = (jax.nn.gelu(gate_pre, approximate=True) * post).astype(BF)
        residual = residual + narrow(dot_t(heads_out, piece(l, 4)))
        res_two = residual
        normed, scale_two = rms(residual, gain_two)
        wide_two = widen(normed)
        gate = dot(wide_two, piece(l, 0))
        up = dot(wide_two, piece(l, 1))
        hidden = (jax.nn.silu(gate) * up).astype(BF)
        near, far = narrow_start(dot_t(hidden, piece(l, 2)))
        if l < layers - 1:
            residual = residual + near + swap(far, 2).astype(F32)
        kept.append(
            (res_one, scale_one, wide, pack, saved, gate_pre, unit, inv, heads_out, res_two, scale_two, wide_two,
             gate, up, hidden, small, pg, ps)
        )
    grad = cotangent.astype(F32)
    mix_grads, rest_grads = [None] * layers, [None] * layers
    gain_grads = [None] * (2 * layers)
    for l in reversed(range(layers)):
        gain_one, gain_two = gains[l], gains[layers + l]
        (res_one, scale_one, wide, pack, saved, gate_pre, unit, inv, heads_out, res_two, scale_two, wide_two,
         gate, up, hidden, small, pg, ps) = kept[l]
        if l == layers - 1:
            branch = jnp.concatenate([cotangent, top_near, top_far, swap(top_far, 1)], axis=0)
        else:
            branch = widen(grad.astype(BF))
        d_hidden = dot(branch, piece(l, 2))
        q = jax.nn.sigmoid(gate)
        swish = gate * q
        d_gate = (d_hidden * up * (q + swish * (1.0 - q))).astype(BF)
        d_up = (d_hidden * swish).astype(BF)
        d_norm = narrow(dot_t(d_gate, piece(l, 0)) + dot_t(d_up, piece(l, 1)))
        back, gain_grads[layers + l] = rms_back(res_two, scale_two, gain_two, d_norm)
        grad = grad + back
        branch_two = widen(grad.astype(BF))
        d_heads = dot(branch_two, piece(l, 4))
        post = unit * pg + ps
        ge, slope = gelu_two(gate_pre)
        d_pre = (d_heads * post * slope).astype(BF)
        d_post = d_heads * ge
        d_pg = jnp.sum(d_post * unit, axis=0)
        d_ps = jnp.sum(d_post, axis=0)
        p = d_post * pg
        sums = order_sum(jnp.stack([jnp.sum(p, axis=1), jnp.sum(p * unit, axis=1)])) / D
        d_inner = inv * (p - sums[0][:, None] - unit * sums[1][:, None])
        rest_sum = weight_grads(wide, wide_two, branch, branch_two, d_pre, d_gate, d_up, hidden, heads_out)
        rest_sum, d_inner = lax.optimization_barrier((rest_sum, d_inner))
        rest_grads[l] = scatter(rest_sum)
        if l == layers - 1:
            near, far, d_inner = lax.optimization_barrier((near, far, d_inner))
            moved = swap(far, 2)
        d_pack, block = backward_call(place, pack, d_inner, saved, small, jnp.stack([d_pg, d_ps]), dp)
        if l == layers - 1:
            d_pack, moved = lax.optimization_barrier((d_pack, moved))
            residual = residual + near + moved.astype(F32)
        mats = t_dot(wide, d_pack)
        mixed = jnp.concatenate([mats.reshape(dp, part, PACK), block.reshape(dp, inner_part, PACK)], axis=1).astype(BF)
        mixed, d_pack = lax.optimization_barrier((mixed, d_pack))
        mix_grads[l] = exchange_sum(mixed)
        d_wide = dot_t(d_pack, mix_w[l]) + dot_t(d_pre, piece(l, 3))
        near, far = narrow_start(d_wide)
        if l == 0:
            first_gain = jnp.sum(d_wide * wide_unit, axis=0)
            far, first_gain = lax.optimization_barrier((far, first_gain))
        d_norm = near + swap(far, 2).astype(F32)
        back, gain_grads[l] = rms_back(res_one, scale_one, gain_one, d_norm)
        if l == 0:
            gain_grads[l] = first_gain
        grad = grad + back
        if l > 0:
            grad, rest_grads[l], residual = lax.optimization_barrier((grad, rest_grads[l], residual))
    grad_in = grad
    block_out = residual.astype(BF)

    both = jnp.stack(mix_grads)
    mats, block = both[:, :part], both[:, part:]
    rest = jnp.stack(rest_grads)
    d_gains = sum_all(jnp.stack(gain_grads))
    spot = lax.axis_index(DP) * tp + lax.axis_index("tensor")
    d_gains = lax.dynamic_slice_in_dim(d_gains, spot * gain_part, gain_part, axis=1)
    small = block[:, :small_part, 2 * mine + heads : span].transpose(0, 2, 1).reshape(layers, 5, heads, small_part)

    def matrix(i):
        return mats[:, :, HD + mine * i : HD + mine * (i + 1)]

    def tail_piece(i):
        return rest[:, :, edges[i] : edges[i + 1]]

    def state_part(i):
        return block[:, :, mine * i : mine * (i + 1)].reshape(layers, inner_part, heads, HD)

    return (
        block_out,
        grad_in,
        matrix(0),
        matrix(1),
        matrix(2),
        tail_piece(3),
        mats[:, :, :heads],
        tail_piece(4).transpose(0, 2, 1),
        state_part(0).transpose(0, 2, 3, 1),
        block[:, :, 2 * mine : 2 * mine + heads].transpose(0, 2, 1),
        state_part(1).transpose(0, 2, 1, 3),
        small[:, 0],
        small[:, 1],
        small[:, 2],
        small[:, 3],
        small[:, 4],
        d_gains[:layers],
        d_gains[layers:],
        tail_piece(0),
        tail_piece(1),
        tail_piece(2).transpose(0, 2, 1),
    )


def order_sum(sums):
    def turn(x, bit):
        parts = jnp.split(x, 4, axis=1)
        return jnp.concatenate([parts[i ^ bit] for i in range(4)], axis=1)

    sums = sums + turn(swap(sums, 1), 1)
    return sums + turn(swap(sums, 2), 2)


def solution(mesh):
    shape = (mesh.shape["dp"] // 2, 2, mesh.shape["tensor"])
    mesh = jax.sharding.Mesh(mesh.devices.reshape(shape), ("line", "near", "tensor"))
    placed = (
        P(("line", "near", "tensor"), None),
        P(("line", "near", "tensor"), None),
        P(None, DP, "tensor"),
        P(None, DP, "tensor"),
        P(None, DP, "tensor"),
        P(None, DP, "tensor"),
        P(None, DP, "tensor"),
        P(None, "tensor", DP),
        P(None, "tensor", None, DP),
        P(None, "tensor", DP),
        P(None, "tensor", DP, None),
        P(None, "tensor", DP),
        P(None, "tensor", DP),
        P(None, "tensor", DP),
        P(None, "tensor", DP),
        P(None, "tensor", DP),
        P(None, ("line", "near", "tensor")),
        P(None, ("line", "near", "tensor")),
        P(None, DP, "tensor"),
        P(None, DP, "tensor"),
        P(None, "tensor", DP),
    )
    return jax.shard_map(
        per_device,
        mesh=mesh,
        in_specs=placed,
        out_specs=(
            P(("line", "near", "tensor"), None),
            P(("line", "near", "tensor"), None),
            P(None, DP, "tensor"),
            P(None, DP, "tensor"),
            P(None, DP, "tensor"),
            P(None, DP, "tensor"),
            P(None, DP, "tensor"),
            P(None, "tensor", DP),
            P(None, "tensor", None, DP),
            P(None, "tensor", DP),
            P(None, "tensor", DP, None),
            P(None, "tensor", DP),
            P(None, "tensor", DP),
            P(None, "tensor", DP),
            P(None, "tensor", DP),
            P(None, "tensor", DP),
            P(None, ("line", "near", "tensor")),
            P(None, ("line", "near", "tensor")),
            P(None, DP, "tensor"),
            P(None, DP, "tensor"),
            P(None, "tensor", DP),
        ),
        check_vma=False,
    )
```

```python
import functools

import jax
import jax.numpy as jnp
from jax import lax
from jax.experimental import pallas as pl
from jax.sharding import PartitionSpec as P
from jax.experimental.pallas import tpu as pltpu

F32 = jnp.float32
BF = jnp.bfloat16
HD = 64
INNER = 256
CS = 16
CH = 128
STEPS = CH // CS
UNIT = 128
PACK = 640
EPS = 1e-6
K0 = 0.7978845608028654
K1 = 0.7978845608028654 * 0.044715


def mm(a, b, ca, cb):
    return lax.dot_general(
        a.astype(BF), b.astype(BF), (((ca,), (cb,)), ((), ())), preferred_element_type=F32
    )


def nn(a, b):
    return mm(a, b, 1, 0)


def nt(a, b):
    return mm(a, b, 1, 1)


def tn(a, b):
    return mm(a, b, 0, 0)


def gelu_two(z):
    zz = z * z
    t = jnp.tanh(z * (K0 + K1 * zz))
    half = 0.5 + 0.5 * t
    return z * half, half + 0.5 * z * (1.0 - t * t) * (K0 + 3.0 * K1 * zz)


def gelu_three(z):
    zz = z * z
    t = jnp.tanh(z * (K0 + K1 * zz))
    half = 0.5 + 0.5 * t
    rest = 1.0 - t * t
    p = K0 + 3.0 * K1 * zz
    return z * half, half + 0.5 * z * rest * p, rest * (p + 3.0 * K1 * zz - z * t * p * p)


def mean(x):
    return jnp.sum(x, axis=1, keepdims=True) * (1.0 / HD)


def masks():
    row = lax.broadcasted_iota(jnp.int32, (CH, CH), 0)
    col = lax.broadcasted_iota(jnp.int32, (CH, CH), 1)
    row_block, col_block = row >> 4, col >> 4
    inside = (row_block == col_block) & (col <= row)
    earlier = col_block < row_block
    own = 1.0 / ((row & (CS - 1)) + 1).astype(F32)
    coef = jnp.where(earlier, 1.0 / CS, jnp.where(inside, own, 0.0))
    return coef, jnp.where(earlier, 1.0, 0.0)


def split_pack(pack, heads):
    wide = pack.astype(F32)
    first = wide[:, :CH]
    turned = first.T
    rates_row = [jax.nn.sigmoid(turned[h : h + 1]) * (1.0 / HD) for h in range(heads)]
    rates_col = [jax.nn.sigmoid(first[:, h : h + 1]) * (1.0 / HD) for h in range(heads)]
    off = HD
    xq = [wide[:, off + HD * h : off + HD * (h + 1)] for h in range(heads)]
    off += HD * heads
    xk = [wide[:, off + HD * h : off + HD * (h + 1)] for h in range(heads)]
    off += HD * heads
    xv = [wide[:, off + HD * h : off + HD * (h + 1)] for h in range(heads)]
    return xq, xk, xv, rates_row, rates_col


def forward_kernel(
    heads, dp, place_ref, pack_ref, in_ref,
    o_ref, z1_ref, a_ref, z1b_ref, c_ref, z2b_ref, w1s_ref, w2s_ref, small_ref,
    w1, b1, w2, b2, pre, kke, cc, ecol, g1buf, g2buf, x2buf,
):
    H = range(heads)

    @pl.when(pl.program_id(0) == 0)
    def _():
        mine = heads * HD
        params = in_ref[...].astype(F32)
        first, second, rest = params[:, :mine].T, params[:, mine : 2 * mine].T, params[:, 2 * mine :]
        biases = rest.T
        few, step = HD // dp, INNER // dp
        small = jnp.concatenate([rest[step * d : step * d + few] for d in range(dp)], axis=0).T
        small_ref[...] = small[heads:]
        for h in H:
            w1[h] = first[HD * h : HD * (h + 1)]
            w2_own = second[HD * h : HD * (h + 1)]
            w2[h] = w2_own - jnp.mean(w2_own, axis=0, keepdims=True)
            b1[h] = biases[h : h + 1]
            b2_own = small[heads + h : heads + h + 1]
            b2[h] = b2_own - mean(b2_own)
        g1buf[...] = jnp.zeros_like(g1buf)

    coef, before = masks()
    xq, xk, xv, rrow, rcol = split_pack(pack_ref[...], heads)
    b2_start = [b2[h] for h in H]
    mcc = []
    for h in H:
        pre[h] = nn(xk[h], w1[h]) + b1[h]
        kke[h] = ((nt(xk[h], xk[h]) + 1.0) * (before * (rrow[h] * (1.0 / CS)))).astype(BF)
        g, sh = small_ref[heads + h : heads + h + 1], small_ref[2 * heads + h : 2 * heads + h + 1]
        cval = (sh - xv[h] + xk[h]) * g
        cc[h] = cval
        mcc.append(mean(cval))
        ecol[h] = jnp.broadcast_to(rcol[h] * (1.0 / CS), (CH, HD))
        w1s_ref[0, h] = w1[h].astype(w1s_ref.dtype)
    w1_start = [w1[h].astype(BF) for h in H]
    w2_start = [w2[h].astype(BF) for h in H]
    b1_start = [b1[h] for h in H]

    def finish(k):
        part, upto = slice(UNIT * k, UNIT * (k + 1)), UNIT * (k + 1)
        mask = [coef[part, :upto] * rrow[h][:, :upto] for h in H]
        score = [nt(xq[h][part], xk[h][:upto]) + 1.0 for h in H]
        z1b = [nn(xq[h][part], w1_start[h]) + b1_start[h] - nn(score[h] * mask[h], g1buf[h, :upto, :]) for h in H]
        x2q = [jax.nn.gelu(z1b[h], approximate=True).astype(BF) for h in H]
        p = [nt(x2q[h], x2buf[h, :upto, :]) + 1.0 for h in H]
        z2b = [nt(x2q[h], w2_start[h]) + b2_start[h] - nn(p[h] * mask[h], g2buf[h, :upto, :]) for h in H]
        for h in H:
            z1b_ref[part, INNER * h : INNER * (h + 1)] = z1b[h].astype(BF)
            centred = z2b[h] - mean(z2b[h])
            z2b_ref[h, part, :] = centred.astype(BF)
            unit = centred * lax.rsqrt(mean(centred * centred) + EPS)
            o_ref[part, HD * h : HD * (h + 1)] = (
                xq[h][part] + unit * small_ref[heads + h : heads + h + 1] + small_ref[2 * heads + h : 2 * heads + h + 1]
            )

    ma = [mean(small_ref[heads + h : heads + h + 1] * small_ref[heads + h : heads + h + 1]) for h in H]
    w2v = [w2[h] for h in H]
    b2v = list(b2_start)
    for i in range(STEPS):
        rows = slice(CS * i, CS * (i + 1))
        z1 = [pre[h, rows, :] for h in H]
        if i >= 2:
            z1 = [z1[h] - nn(kke[h, rows, : CS * (i - 1)], g1buf[h, : CS * (i - 1), :]) for h in H]
        if i >= 1:
            z1 = [z1[h] - nn(kke[h, rows, :][:, CS * (i - 1) : CS * i], g1buf[h, CS * (i - 1) : CS * i, :]) for h in H]
        xd = [gelu_two(z1[h]) for h in H]
        x2b = [xd[h][0].astype(BF) for h in H]
        w2b = [w2v[h].astype(BF) for h in H]
        c = [nt(x2b[h], w2b[h]) + b2v[h] for h in H]
        g2 = []
        for h in H:
            g = small_ref[heads + h : heads + h + 1]
            a = g * g
            ca = c[h] * a
            cch = cc[h, rows, :]
            mc = mcc[h][rows]
            mu, q1, q2, q3, q4 = mean(c[h]), mean(c[h] * c[h]), mean(ca), mean(ca * c[h]), mean(c[h] * cch)
            s = lax.rsqrt(q1 - mu * mu + EPS)
            m1 = s * (q2 - mu * ma[h]) + mc
            m2 = s * (s * (q3 - mu * (2.0 * q2 - mu * ma[h])) + (q4 - mu * mc))
            c[h] = c[h] - mu
            g2.append(s * (c[h] * (s * (a - m2)) + cch - m1))
        av = [nn(g2[h], w2b[h]) for h in H]
        g1 = [av[h] * xd[h][1] for h in H]
        for h in H:
            g1buf[h, rows, :] = g1[h].astype(BF)
            g2buf[h, rows, :] = g2[h].astype(BF)
            x2buf[h, rows, :] = x2b[h]
            w2s_ref[i, h] = w2b[h].astype(w2s_ref.dtype)
            z1_ref[rows, INNER * h : INNER * (h + 1)] = z1[h].astype(BF)
            a_ref[rows, INNER * h : INNER * (h + 1)] = av[h].astype(BF)
            c_ref[h, rows, :] = c[h].astype(BF)
            eg2 = ecol[h, rows, :] * g2[h]
            w2v[h] = w2v[h] - tn(eg2, x2b[h])
            b2v[h] = b2v[h] - jnp.sum(eg2, axis=0, keepdims=True)
        if (i + 1) % (UNIT // CS) == 0:
            finish(i // (UNIT // CS))
    for h in H:
        g1 = g1buf[h]
        w1[h] = w1[h] - tn(ecol[h] * xk[h], g1)
        b1[h] = b1[h] - jnp.sum(ecol[h][:, :1] * g1.astype(F32), axis=0, keepdims=True)
        w2[h] = w2v[h]
        b2[h] = b2v[h]


def forward_call(place, pack, params, heads, dp):
    rows = pack.shape[0]
    chunks = rows // CH
    per_block = chunks // 4

    def spot(c, place):
        return ((c // per_block) ^ place[0]) * per_block + c % per_block

    def whole(*shape):
        return pl.BlockSpec(shape, lambda c, place: (0,) * len(shape))

    def moved(n):
        return pl.BlockSpec((CH, n), lambda c, place: (spot(c, place), 0))

    def kept(n):
        return pl.BlockSpec((CH, n), lambda c, place: (c, 0))

    by_head = pl.BlockSpec((heads, CH, HD), lambda c, place: (0, c, 0))
    sds = jax.ShapeDtypeStruct
    return pl.pallas_call(
        functools.partial(forward_kernel, heads, dp),
        grid_spec=pltpu.PrefetchScalarGridSpec(
            num_scalar_prefetch=1,
            grid=(chunks,),
            in_specs=[
                moved(PACK),
                whole(*params.shape),
            ],
            out_specs=[
                moved(heads * HD),
                kept(heads * INNER),
                kept(heads * INNER),
                kept(heads * INNER),
                by_head,
                by_head,
                pl.BlockSpec((1, heads, HD, INNER), lambda c, place: (c, 0, 0, 0)),
                pl.BlockSpec((STEPS, heads, HD, INNER), lambda c, place: (c, 0, 0, 0)),
                whole(5 * heads, HD),
            ],
            scratch_shapes=[
                pltpu.VMEM((heads, HD, INNER), F32),
                pltpu.VMEM((heads, 1, INNER), F32),
                pltpu.VMEM((heads, HD, INNER), F32),
                pltpu.VMEM((heads, 1, HD), F32),
                pltpu.VMEM((heads, CH, INNER), F32),
                pltpu.VMEM((heads, CH, CH), BF),
                pltpu.VMEM((heads, CH, HD), F32),
                pltpu.VMEM((heads, CH, HD), F32),
                pltpu.VMEM((heads, CH, INNER), BF),
                pltpu.VMEM((heads, CH, HD), BF),
                pltpu.VMEM((heads, CH, INNER), BF),
            ],
        ),
        out_shape=[
            sds((rows, heads * HD), F32),
            sds((rows, heads * INNER), BF),
            sds((rows, heads * INNER), BF),
            sds((rows, heads * INNER), BF),
            sds((heads, rows, HD), BF),
            sds((heads, rows, HD), BF),
            sds((chunks, heads, HD, INNER), BF),
            sds((chunks * STEPS, heads, HD, INNER), BF),
            sds((5 * heads, HD), F32),
        ],
        compiler_params=pltpu.CompilerParams(vmem_limit_bytes=56 * 2**20),
        cost_estimate=pl.CostEstimate(flops=65 * 10**9, bytes_accessed=25 * 10**6, transcendentals=0),
    )(place, pack, params)


def backward_kernel(
    heads, shares, place_ref, pack_ref, do_ref, z1_ref, a_ref, z1b_ref, c_ref, z2b_ref, w1s_ref, w2s_ref, small_ref, post_ref,
    dpack_ref, block_ref, dw1, db1, dw2, db2, dg_ref, dh_ref,
    dg1b, dg2b, dx2b, d1v, ad2, g2v, kkt, dz1buf, k1v, k2v, dyv, ecol, x2buf,
):
    H = range(heads)

    @pl.when(pl.program_id(0) == 0)
    def _():
        dw1[...] = jnp.zeros_like(dw1)
        db1[...] = jnp.zeros_like(db1)
        dw2[...] = jnp.zeros_like(dw2)
        db2[...] = jnp.zeros_like(db2)
        dg_ref[...] = jnp.zeros_like(dg_ref)
        dh_ref[...] = jnp.zeros_like(dh_ref)
        dz1buf[...] = jnp.zeros_like(dz1buf)

    coef, before = masks()
    xq, xk, xv, rrow, rcol = split_pack(pack_ref[...], heads)
    wides = [slice(INNER * h, INNER * (h + 1)) for h in H]
    gains = [small_ref[heads + h : heads + h + 1] for h in H]
    shifts = [small_ref[2 * heads + h : 2 * heads + h + 1] for h in H]
    w1_start = [w1s_ref[0, h] for h in H]
    w2_start = [w2s_ref[0, h] for h in H]
    mask = [coef * rrow[h] for h in H]
    do = [do_ref[:, HD * h : HD * (h + 1)].astype(F32) for h in H]
    dz2b = []
    for h in H:
        z2b = z2b_ref[h].astype(F32)
        sb = lax.rsqrt(mean(z2b * z2b) + EPS)
        ub = z2b * sb
        dog = do[h] * gains[h]
        dg_ref[h] += jnp.sum(do[h] * ub, axis=0, keepdims=True)
        dh_ref[h] += jnp.sum(do[h], axis=0, keepdims=True)
        dz2b.append(sb * (dog - mean(dog) - ub * mean(dog * ub)))
    uv, yv, st, g2_all = [], [], [], []
    for h in H:
        a = gains[h] * gains[h]
        c = c_ref[h].astype(F32)
        cch = (shifts[h] - xv[h] + xk[h]) * gains[h]
        ca = c * a
        q1, q2, q3, q4 = mean(c * c), mean(ca), mean(ca * c), mean(c * cch)
        s = lax.rsqrt(q1 + EPS)
        m1 = s * q2 + mean(cch)
        m2 = s * (s * q3 + q4)
        u = c * s
        y = u * a + cch
        g2 = s * (y - m1 - u * m2)
        uv.append(u)
        yv.append(y)
        st.append((s, m2, s * q2, s * s * q3, mean(y), mean(a)))
        g2v[h] = g2
        g2_all.append(g2.astype(BF))
        ecol[h] = jnp.broadcast_to(rcol[h] * (1.0 / CS), (CH, HD))
    x2_all, g1_all, x2q, d1b = [], [], [], []
    for h in H:
        x2, d1, slope2 = gelu_three(z1_ref[:, wides[h]].astype(F32))
        av = a_ref[:, wides[h]].astype(F32)
        d1v[h] = d1
        ad2[h] = av * slope2
        x2_all.append(x2.astype(BF))
        x2buf[h] = x2_all[h]
        g1_all.append((av * d1).astype(BF))
    for h in H:
        value, slope = gelu_two(z1b_ref[:, wides[h]].astype(F32))
        x2q.append(value.astype(BF))
        d1b.append(slope)
    before_t = before.T
    sc = [nt(xq[h], xk[h]) + 1.0 for h in H]
    for h in H:
        kkt[h] = ((nt(xk[h], xk[h]) + 1.0) * before_t).astype(BF)
    p = [nt(x2q[h], x2_all[h]) + 1.0 for h in H]
    dm2 = [-nt(dz2b[h], g2_all[h]) for h in H]
    dpv = [(mask[h] * dm2[h]).astype(BF) for h in H]
    dz1b = [(nn(dz2b[h], w2_start[h]) + nn(dpv[h], x2_all[h])) * d1b[h] for h in H]
    for h in H:
        dg2b[h] = -tn(mask[h] * p[h], dz2b[h])
    for h in H:
        dx2b[h] = tn(dpv[h], x2q[h])
    dw2_out = [tn(dz2b[h], x2q[h]) for h in H]
    db2_out = [jnp.sum(dz2b[h], axis=0, keepdims=True) for h in H]
    db1_out = [jnp.sum(dz1b[h], axis=0, keepdims=True) for h in H]
    dz1c = [dz1b[h].astype(BF) for h in H]
    dm1 = [-nt(dz1c[h], g1_all[h]) for h in H]
    dsv = [(mask[h] * dm1[h]).astype(BF) for h in H]
    for h in H:
        dg1b[h] = -tn(mask[h] * sc[h], dz1c[h])
    for h in H:
        k1v[h] = nn(xk[h], dw1[h]) + db1[h]
    dr_row = [jnp.sum(coef * (sc[h] * dm1[h] + p[h] * dm2[h]), axis=0, keepdims=True) for h in H]
    dxq = [do[h] + nt(dz1c[h], w1_start[h]) + nn(dsv[h], xk[h]) for h in H]
    dxk = [tn(dsv[h], xq[h]) - nt((rcol[h] * (1.0 / CS)) * g1_all[h].astype(F32), dw1[h]) for h in H]
    dw1_out = [tn(xq[h], dz1c[h]) for h in H]
    d2 = [dw2[h] for h in H]
    e2 = [db2[h] for h in H]
    for i in reversed(range(STEPS)):
        rows = slice(CS * i, CS * (i + 1))
        k1 = [k1v[h, rows, :] for h in H]
        if i < STEPS - 2:
            k1 = [k1[h] + nn(kkt[h, rows, :][:, CS * (i + 2) :], dz1buf[h, CS * (i + 2) :, :]) for h in H]
        if i < STEPS - 1:
            k1 = [k1[h] + nn(kkt[h, rows, :][:, CS * (i + 1) : CS * (i + 2)], dz1buf[h, CS * (i + 1) : CS * (i + 2), :]) for h in H]
        dg1 = [dg1b[h, rows, :] - ecol[h, rows, :][:, :1] * k1[h] for h in H]
        da = [(dg1[h] * d1v[h, rows, :]).astype(BF) for h in H]
        d2b = [d2[h].astype(BF) for h in H]
        w2i = [w2s_ref[i, h] for h in H]
        g2 = [g2v[h, rows, :] for h in H]
        k2 = [nt(x2buf[h, rows, :], d2b[h]) + e2[h] for h in H]
        dg2 = [dg2b[h, rows, :] - ecol[h, rows, :] * k2[h] + nt(da[h], w2i[h]) for h in H]
        l2 = [dx2b[h, rows, :] - nn(ecol[h, rows, :] * g2[h], d2b[h]) for h in H]
        dz2 = []
        for h in H:
            g = small_ref[heads + h : heads + h + 1]
            a = g * g
            s, m2, mau, mauu, my = (q[rows] for q in st[h][:5])
            ma = st[h][5]
            u, y = uv[h][rows], yv[h][rows]
            dv = dg2[h]
            dva = dv * a
            n1, n2, n3, n4, n5 = mean(dv), mean(dv * u), mean(dv * g2[h]), mean(dva * u), mean(dva)
            dy = s * (dv - n1 - u * n2)
            muu = s * (n4 - n1 * mau - n2 * (mauu + 2.0 * m2))
            mu = s * (n5 - n1 * (ma + m2) - n2 * (mau + my))
            dz2.append(s * (dy * a - (s * m2) * dv - (s * n2) * y - mu - u * (muu + n3)))
            dyv[h, rows, :] = dy
            k2v[h, rows, :] = k2[h]
        dx2 = [l2[h] + nn(dz2[h], w2i[h]) for h in H]
        dz1 = [dx2[h] * d1v[h, rows, :] + dg1[h] * ad2[h, rows, :] for h in H]
        for h in H:
            dz1buf[h, rows, :] = dz1[h].astype(BF)
            d2[h] = d2[h] + tn(
                jnp.concatenate([g2[h], dz2[h]], axis=0), jnp.concatenate([da[h], x2buf[h, rows, :]], axis=0)
            )
            e2[h] = e2[h] + jnp.sum(dz2[h], axis=0, keepdims=True)
    dz1 = [dz1buf[h] for h in H]
    k1 = [k1v[h] + nn(kkt[h], dz1[h]) for h in H]
    dkk = [(-nt(dz1[h], g1_all[h]) * (before * (rrow[h] * (1.0 / CS)))).astype(BF) for h in H]
    dyg = [dyv[h] * gains[h] for h in H]
    dk = [dxk[h] + nt(dz1[h], w1_start[h]) + dyg[h] for h in H]
    dk = [dk[h] + nn(dkk[h], xk[h]) + tn(dkk[h], xk[h]) for h in H]
    de_col = [
        jnp.sum(g1_all[h].astype(F32) * k1[h], axis=1, keepdims=True)
        + jnp.sum(g2v[h] * k2v[h], axis=1, keepdims=True)
        for h in H
    ]
    for h in H:
        dg_ref[h] += jnp.sum(dyv[h] * (uv[h] * gains[h] * 2.0 + shifts[h] - xv[h] + xk[h]), axis=0, keepdims=True)
        dh_ref[h] += jnp.sum(dyg[h], axis=0, keepdims=True)
        off = HD + HD * h
        dpack_ref[:, off : off + HD] = dxq[h].astype(BF)
        off += HD * heads
        dpack_ref[:, off : off + HD] = dk[h].astype(BF)
        off += HD * heads
        dpack_ref[:, off : off + HD] = (-dyg[h]).astype(BF)
    for h in H:
        dw1[h] = dw1[h] + dw1_out[h] + tn(xk[h], dz1[h])
        db1[h] = db1[h] + db1_out[h] + jnp.sum(dz1[h].astype(F32), axis=0, keepdims=True)
        dw2[h] = d2[h] + dw2_out[h]
        db2[h] = e2[h] + db2_out[h]
    sub = lax.broadcasted_iota(jnp.int32, (CH, CH), 0)
    lane = lax.broadcasted_iota(jnp.int32, (CH, CH), 1)
    stack = jnp.zeros((CH, CH), F32)
    cols = jnp.zeros((CH, CH), F32)
    for h in H:
        stack = stack + jnp.where(sub == h, dr_row[h], 0.0)
        slope = rcol[h] * (1.0 - HD * rcol[h])
        cols = cols + jnp.where(lane == h, slope, 0.0)
    turned = stack.T
    for h in H:
        turned = turned - jnp.where(lane == h, de_col[h] * (1.0 / CS), 0.0)
    dpack_ref[:, :HD] = (turned * cols)[:, :HD].astype(dpack_ref.dtype)

    @pl.when(pl.program_id(0) == pl.num_programs(0) - 1)
    def _():
        mine = heads * HD
        block_ref[...] = jnp.zeros_like(block_ref)
        for h in H:
            block_ref[:, HD * h : HD * (h + 1)] = dw1[h].T
            block_ref[:, mine + HD * h : mine + HD * (h + 1)] = dw2[h].T
        bias = jnp.concatenate([db1[h] for h in H] + [jnp.zeros((8 - heads, INNER), F32)], axis=0)
        block_ref[:, 2 * mine : 2 * mine + heads] = bias.T[:, :heads]
        lines = [db2[h] for h in H] + [dg_ref[h] for h in H] + [dh_ref[h] for h in H]
        lines += [post_ref[i : i + 1, HD * h : HD * (h + 1)] for i in range(2) for h in H]
        few, step = HD // shares, INNER // shares
        small = jnp.concatenate(lines + [jnp.zeros((16 - 5 * heads, HD), F32)], axis=0).T
        for d in range(shares):
            block_ref[step * d : step * d + few, 2 * mine + heads : 2 * mine + 6 * heads] = small[
                few * d : few * (d + 1), : 5 * heads
            ]


def backward_call(place, pack, do, saved, small, post, dp):
    z1, a, z1b, c, z2b, w1s, w2s = saved
    heads = small.shape[0] // 5
    rows = pack.shape[0]
    chunks = rows // CH
    last = chunks - 1
    per_block = chunks // 4

    def spot(c, place):
        return (((last - c) // per_block) ^ place[0]) * per_block + (last - c) % per_block

    def whole(*shape):
        return pl.BlockSpec(shape, lambda c, place: (0,) * len(shape))

    def moved(n):
        return pl.BlockSpec((CH, n), lambda c, place: (spot(c, place), 0))

    def kept(n):
        return pl.BlockSpec((CH, n), lambda c, place: (last - c, 0))

    by_head = pl.BlockSpec((heads, CH, HD), lambda c, place: (0, last - c, 0))
    sds = jax.ShapeDtypeStruct
    return pl.pallas_call(
        functools.partial(backward_kernel, heads, dp),
        grid_spec=pltpu.PrefetchScalarGridSpec(
            num_scalar_prefetch=1,
            grid=(chunks,),
            in_specs=[
                moved(PACK),
                moved(heads * HD),
                kept(heads * INNER),
                kept(heads * INNER),
                kept(heads * INNER),
                by_head,
                by_head,
                pl.BlockSpec((1, heads, HD, INNER), lambda c, place: (last - c, 0, 0, 0)),
                pl.BlockSpec((STEPS, heads, HD, INNER), lambda c, place: (last - c, 0, 0, 0)),
                whole(*small.shape),
                whole(*post.shape),
            ],
            out_specs=[moved(PACK), whole(INNER, PACK)],
            scratch_shapes=[
                pltpu.VMEM((heads, HD, INNER), F32),
                pltpu.VMEM((heads, 1, INNER), F32),
                pltpu.VMEM((heads, HD, INNER), F32),
                pltpu.VMEM((heads, 1, HD), F32),
                pltpu.VMEM((heads, 1, HD), F32),
                pltpu.VMEM((heads, 1, HD), F32),
                pltpu.VMEM((heads, CH, INNER), F32),
                pltpu.VMEM((heads, CH, HD), F32),
                pltpu.VMEM((heads, CH, INNER), F32),
                pltpu.VMEM((heads, CH, INNER), F32),
                pltpu.VMEM((heads, CH, INNER), F32),
                pltpu.VMEM((heads, CH, HD), F32),
                pltpu.VMEM((heads, CH, CH), BF),
                pltpu.VMEM((heads, CH, INNER), BF),
                pltpu.VMEM((heads, CH, INNER), F32),
                pltpu.VMEM((heads, CH, HD), F32),
                pltpu.VMEM((heads, CH, HD), F32),
                pltpu.VMEM((heads, CH, HD), F32),
                pltpu.VMEM((heads, CH, INNER), BF),
            ],
        ),
        out_shape=[
            sds((rows, PACK), BF),
            sds((INNER, PACK), F32),
        ],
        compiler_params=pltpu.CompilerParams(vmem_limit_bytes=56 * 2**20),
        cost_estimate=pl.CostEstimate(flops=70 * 10**9, bytes_accessed=25 * 10**6, transcendentals=0),
    )(place, pack, do, z1, a, z1b, c, z2b, w1s, w2s, small, post)


D = 768
DP = ("line", "near")


def swap(x, bit):
    size = lax.axis_size("tensor")
    return lax.ppermute(x, "tensor", [(i, i ^ bit) for i in range(size)])


def widen(x):
    far = swap(x, 2)
    return jnp.concatenate([x, swap(x, 1), far, swap(far, 1)], axis=0)


def narrow_start(total):
    quarter = total.shape[0] // 4
    near, pair, far, cross = [total[quarter * i : quarter * (i + 1)] for i in range(4)]
    far = (far + swap(cross.astype(BF), 1).astype(F32)).astype(BF)
    return near + swap(pair.astype(BF), 1).astype(F32), far


def narrow(total, beside=None):
    near, far = narrow_start(total)
    moved = swap(far, 2)
    if beside is None:
        return near + moved.astype(F32)
    moved, beside = lax.optimization_barrier((moved, beside))
    return near + moved.astype(F32), beside


def sum_group(x):
    return x + swap(x, 1) + swap(x, 2) + swap(x, 3)


def dot(a, b):
    return lax.dot_general(a, b, (((1,), (0,)), ((), ())), preferred_element_type=F32)


def dot_t(a, b):
    return lax.dot_general(a, b, (((1,), (1,)), ((), ())), preferred_element_type=F32)


def t_dot(a, b):
    return lax.dot_general(a, b, (((0,), (0,)), ((), ())), preferred_element_type=F32)


def rms(x, gain):
    scale = lax.rsqrt(jnp.mean(x * x, axis=1, keepdims=True) + EPS)
    return (x * scale * gain).astype(BF), scale


def rms_back(x, scale, gain, grad):
    q = grad * gain
    back = scale * q - x * (scale * scale * scale) * jnp.mean(q * x, axis=1, keepdims=True)
    return back, jnp.sum(grad * (x * scale), axis=0)


def gather(x):
    return lax.all_gather(x, DP, axis=0, tiled=True)


def turned(x):
    return x.astype(F32).T.astype(BF)


def pack_kernel(
    q_ref, k_ref, v_ref, og_ref, r_ref, out_ref, i1_ref, i2_ref, gate_ref, up_ref, down_ref,
    mix_ref, early_ref, late_ref, inner_ref,
):
    heads = r_ref.shape[0]
    mine = heads * HD
    ff = gate_ref.shape[2]
    rest = 3 * ff + 2 * mine
    for l in range(2):
        mix, at = (mix_ref, 0) if l == 0 else (early_ref, rest)
        mix[:, at : at + HD] = jnp.zeros((mix.shape[0], HD), BF)
        mix[:, at : at + heads] = turned(r_ref[:, l])
        for i, ref in enumerate((q_ref, k_ref, v_ref)):
            mix[:, at + HD + mine * i : at + HD + mine * (i + 1)] = ref[l]
        group = early_ref if l == 0 else late_ref
        group[:, :ff] = gate_ref[l]
        group[:, ff : 2 * ff] = up_ref[l]
        group[:, 2 * ff : 3 * ff] = down_ref[l]
        group[:, 3 * ff : 3 * ff + mine] = og_ref[l]
        group[:, 3 * ff + mine : rest] = turned(out_ref[l])
        base = 2 * mine * l
        for h in range(heads):
            inner_ref[:, base + HD * h : base + HD * (h + 1)] = i1_ref[l, h]
            inner_ref[:, base + mine + HD * h : base + mine + HD * (h + 1)] = i2_ref[l, h]


def feed_grad_kernel(two_ref, branch_ref, gate_ref, up_ref, hid_ref, out_ref):
    ff = gate_ref.shape[1]
    two = two_ref[...]
    out_ref[:, :ff] = tn(two, gate_ref[...]).astype(BF)
    out_ref[:, ff : 2 * ff] = tn(two, up_ref[...]).astype(BF)
    out_ref[:, 2 * ff :] = tn(branch_ref[...], hid_ref[...]).astype(BF)


def mixer_grad_kernel(wide_ref, other_ref, pre_ref, ho_ref, held_ref, out_ref):
    mine = pre_ref.shape[1]
    out_ref[:, :mine] = tn(wide_ref[...], pre_ref[...]).astype(BF)
    out_ref[:, mine:] = tn(other_ref[...], ho_ref[...]).astype(BF)


def feed_grads(two, branch, gate, up, hid, extra):
    rows, width = two.shape
    step = 256
    left = pl.BlockSpec((rows, step), lambda i: (0, i))
    cols = 3 * gate.shape[1]

    def whole(x):
        return pl.BlockSpec(x.shape, lambda i: (0, 0))

    return pl.pallas_call(
        feed_grad_kernel,
        grid=(width // step,),
        in_specs=[left, left, whole(gate), whole(up), whole(hid)],
        out_specs=pl.BlockSpec((step, cols), lambda i: (i, 0)),
        out_shape=jax.ShapeDtypeStruct((width, cols + extra), BF),
        compiler_params=pltpu.CompilerParams(vmem_limit_bytes=32 * 2**20),
        cost_estimate=pl.CostEstimate(flops=2 * rows * width * cols, bytes_accessed=10 * 10**6, transcendentals=0),
    )(two, branch, gate, up, hid)


def mixer_grads(wide, other, pre, ho, held):
    rows, width = wide.shape
    step = 256
    left = pl.BlockSpec((rows, step), lambda i: (0, i))
    cols = 2 * pre.shape[1]
    at = held.shape[1] // cols - 1

    def whole(x):
        return pl.BlockSpec(x.shape, lambda i: (0, 0))

    return pl.pallas_call(
        mixer_grad_kernel,
        grid=(width // step,),
        in_specs=[left, left, whole(pre), whole(ho), pl.BlockSpec(memory_space=pl.ANY)],
        out_specs=pl.BlockSpec((step, cols), lambda i: (i, at)),
        out_shape=jax.ShapeDtypeStruct(held.shape, BF),
        input_output_aliases={4: 0},
        compiler_params=pltpu.CompilerParams(vmem_limit_bytes=32 * 2**20),
        cost_estimate=pl.CostEstimate(flops=2 * rows * width * cols, bytes_accessed=4 * 10**6, transcendentals=0),
    )(wide, other, pre, ho, held)


def gather_small(x):
    size = lax.axis_size("line")
    other = lax.ppermute(x, "near", [(0, 1), (1, 0)])
    first = lax.axis_index("near") == 0
    pair = jnp.concatenate([jnp.where(first, x, other), jnp.where(first, other, x)], axis=0)
    if size > 4:
        return lax.all_gather(pair, "line", axis=0, tiled=True)
    parts = [pair] + [lax.ppermute(pair, "line", [(i, (i - k) % size) for i in range(size)]) for k in range(1, size)]
    start = lax.rem(size - lax.axis_index("line"), size) * pair.shape[0]
    return lax.dynamic_slice_in_dim(jnp.concatenate(parts + parts[:-1], axis=0), start, size * pair.shape[0], axis=0)


def scatter(x):
    return lax.psum_scatter(x, DP, scatter_dimension=0, tiled=True).astype(F32)


def exchange_sum(x):
    moved = lax.all_to_all(x, DP, split_axis=0, concat_axis=0, tiled=True)
    return jnp.sum(moved.astype(F32), axis=0)


def per_device(
    hidden_in, cotangent, w_query, w_key, w_value, w_outgate, w_rate, w_output, init_first, init_first_bias,
    init_second, init_second_bias, inner_gain, inner_shift, post_gain, post_shift, mixer_gain, mlp_gain,
    w_gate, w_up, w_down,
):
    layers, part, mine = w_query.shape
    heads = w_rate.shape[2]
    ff = w_gate.shape[2]
    inner_part = init_first.shape[3]
    small_part = inner_gain.shape[2]
    gain_part = mixer_gain.shape[1]
    dp = lax.axis_size("line") * lax.axis_size("near")
    tp = lax.axis_size("tensor")
    rows = hidden_in.shape[0]
    place = lax.axis_index("tensor").astype(jnp.int32).reshape(1)
    lead = HD - heads

    gains_here = jnp.concatenate([mixer_gain, mlp_gain], axis=0)
    found = [gains_here] + [swap(gains_here, bit) for bit in (1, 2, 3)]
    for bit in (1, 2):
        flip = (lax.axis_index("tensor") & bit) > 0
        found = [jnp.where(flip, found[i ^ bit], found[i]) for i in range(4)]
    gains_group = jnp.concatenate(found, axis=1)
    span = 2 * mine + 6 * heads
    sds = jax.ShapeDtypeStruct
    rest_cols = 3 * ff + 2 * mine
    mix_here, early, late, inner_here = pl.pallas_call(
        pack_kernel,
        out_shape=[
            sds((part, PACK), BF),
            sds((part, rest_cols + PACK), BF),
            sds((part, rest_cols), BF),
            sds((inner_part, 2 * mine * layers), BF),
        ],
    )(
        w_query, w_key, w_value, w_outgate, w_rate.transpose(2, 0, 1), w_output, init_first.transpose(0, 1, 3, 2),
        init_second, w_gate, w_up, w_down.transpose(0, 2, 1),
    )
    smalls = jnp.concatenate([init_second_bias, inner_gain, inner_shift, post_gain, post_shift], axis=1)
    smalls = jnp.pad(smalls.reshape(layers * 5 * heads, small_part), ((0, 0), (0, inner_part - small_part)))
    biases = init_first_bias.reshape(layers * heads, inner_part)
    thin = jnp.concatenate([biases, smalls], axis=0).T
    raw_near, raw_far = swap(hidden_in, 1), swap(hidden_in, 2)
    thin, raw_near, raw_far = lax.optimization_barrier((thin, raw_near, raw_far))
    inner_all = gather_small(jnp.concatenate([inner_here, thin, gains_group.reshape(inner_part, -1)], axis=1))
    mix_here, early, inner_all = lax.optimization_barrier((mix_here, early, inner_all))
    mix_w = [gather(mix_here)]
    first_group, last_group = gather(early), gather(late)
    mix_w.append(first_group[:, rest_cols:])
    rest_w = [first_group[:, :rest_cols], last_group]
    states = 2 * mine * layers
    inner_in = []
    for l in range(layers):
        at = states + heads * layers + 5 * heads * l
        bias_at = states + heads * l
        inner_in.append(
            jnp.concatenate(
                [inner_all[:, 2 * mine * l : 2 * mine * (l + 1)], inner_all[:, bias_at : bias_at + heads],
                 inner_all[:, at : at + 5 * heads]],
                axis=1,
            )
        )
    gains = inner_all[:, layers * span :].reshape(dp, 2 * layers, tp * gain_part)
    gains = gains.transpose(1, 0, 2).reshape(2 * layers, D).astype(F32)
    edges = [0, ff, 2 * ff, 3 * ff, 3 * ff + mine, 3 * ff + 2 * mine]

    def piece(l, i):
        return rest_w[l][:, edges[i] : edges[i + 1]]

    residual = hidden_in.astype(F32)
    raw_wide = jnp.concatenate([hidden_in, raw_near, raw_far, swap(raw_far, 1)], axis=0)
    top_near, top_far = swap(cotangent, 1), swap(cotangent, 2)
    kept = []
    for l in range(layers):
        gain_one, gain_two = gains[l], gains[layers + l]
        res_one = residual
        if l == 0:
            wide_res = raw_wide.astype(F32)
            wide, wide_scale = rms(wide_res, gain_one)
            wide_unit = wide_res * wide_scale
            scale_one = lax.rsqrt(jnp.mean(residual * residual, axis=1, keepdims=True) + EPS)
        else:
            normed, scale_one = rms(residual, gain_one)
            wide = widen(normed)
        pack = dot(wide, mix_w[l]).astype(BF)
        outs = forward_call(place, pack, inner_in[l], heads, dp)
        inner_out, saved, small = outs[0], outs[1:-1], outs[-1]
        if l == 0:
            inner_out, top_near, top_far = lax.optimization_barrier((inner_out, top_near, top_far))
        pg = small[3 * heads : 4 * heads].reshape(-1)
        ps = small[4 * heads : 5 * heads].reshape(-1)
        gate_pre = dot(wide, piece(l, 3))
        sums = jnp.stack([jnp.sum(inner_out, axis=1), jnp.sum(inner_out * inner_out, axis=1)])
        sums = order_sum(sums)
        mean_all = sums[0] / D
        inv = lax.rsqrt(sums[1] / D - mean_all * mean_all + EPS)[:, None]
        unit = (inner_out - mean_all[:, None]) * inv
        post = unit * pg + ps
        heads_out = (jax.nn.gelu(gate_pre, approximate=True) * post).astype(BF)
        residual = residual + narrow(dot_t(heads_out, piece(l, 4)))
        res_two = residual
        normed, scale_two = rms(residual, gain_two)
        wide_two = widen(normed)
        gate = dot(wide_two, piece(l, 0))
        up = dot(wide_two, piece(l, 1))
        hidden = (jax.nn.silu(gate) * up).astype(BF)
        near, far = narrow_start(dot_t(hidden, piece(l, 2)))
        if l < layers - 1:
            residual = residual + near + swap(far, 2).astype(F32)
        kept.append(
            (res_one, scale_one, wide, pack, saved, gate_pre, unit, inv, heads_out, res_two, scale_two, wide_two,
             gate, up, hidden, small, pg, ps)
        )
    grad = cotangent.astype(F32)
    mix_grads, rest_grads = [None] * layers, [None] * layers
    gain_grads = [None] * (2 * layers)
    for l in reversed(range(layers)):
        gain_one, gain_two = gains[l], gains[layers + l]
        (res_one, scale_one, wide, pack, saved, gate_pre, unit, inv, heads_out, res_two, scale_two, wide_two,
         gate, up, hidden, small, pg, ps) = kept[l]
        if l == layers - 1:
            branch = jnp.concatenate([cotangent, top_near, top_far, swap(top_far, 1)], axis=0)
        else:
            branch = widen(grad.astype(BF))
        d_hidden = dot(branch, piece(l, 2))
        q = jax.nn.sigmoid(gate)
        swish = gate * q
        d_gate = (d_hidden * up * (q + swish * (1.0 - q))).astype(BF)
        d_up = (d_hidden * swish).astype(BF)
        held = feed_grads(wide_two, branch, d_gate, d_up, hidden, 2 * mine)
        d_norm, held = narrow(dot_t(d_gate, piece(l, 0)) + dot_t(d_up, piece(l, 1)), held)
        back, gain_grads[layers + l] = rms_back(res_two, scale_two, gain_two, d_norm)
        grad = grad + back
        branch_two = widen(grad.astype(BF))
        d_heads = dot(branch_two, piece(l, 4))
        post = unit * pg + ps
        ge, slope = gelu_two(gate_pre)
        d_pre = (d_heads * post * slope).astype(BF)
        d_post = d_heads * ge
        d_pg = jnp.sum(d_post * unit, axis=0)
        d_ps = jnp.sum(d_post, axis=0)
        p = d_post * pg
        sums = order_sum(jnp.stack([jnp.sum(p, axis=1), jnp.sum(p * unit, axis=1)])) / D
        rest_sum = mixer_grads(wide, branch_two, d_pre, heads_out, held)
        d_inner = inv * (p - sums[0][:, None] - unit * sums[1][:, None])
        rest_sum, d_inner = lax.optimization_barrier((rest_sum, d_inner))
        rest_grads[l] = scatter(rest_sum)
        if l == layers - 1:
            near, far, d_inner = lax.optimization_barrier((near, far, d_inner))
            moved = swap(far, 2)
        d_pack, block = backward_call(place, pack, d_inner, saved, small, jnp.stack([d_pg, d_ps]), dp)
        if l == layers - 1:
            d_pack, moved = lax.optimization_barrier((d_pack, moved))
            residual = residual + near + moved.astype(F32)
        mats = t_dot(wide, d_pack)
        if l == 0:
            d_wide = dot_t(d_pack, mix_w[l]) + dot_t(d_pre, piece(l, 3))
            gain_grads[l] = jnp.sum(d_wide * wide_unit, axis=0)
            mats = mats + jnp.pad(jnp.stack(gain_grads).T, ((0, 0), (heads, PACK - heads - 2 * layers)))
        mixed = jnp.concatenate([mats.reshape(dp, part, PACK), block.reshape(dp, inner_part, PACK)], axis=1).astype(BF)
        if l == 0:
            mixed, d_pack = lax.optimization_barrier((mixed, d_pack))
            d_norm = narrow(d_wide)
        else:
            d_norm, mixed = narrow(dot_t(d_pack, mix_w[l]) + dot_t(d_pre, piece(l, 3)), mixed)
        mix_grads[l] = exchange_sum(mixed)
        back, gain = rms_back(res_one, scale_one, gain_one, d_norm)
        if l > 0:
            gain_grads[l] = gain
        grad = grad + back
        if l > 0:
            grad, rest_grads[l], residual = lax.optimization_barrier((grad, rest_grads[l], residual))
    grad_in = grad
    block_out = residual.astype(BF)

    both = jnp.stack(mix_grads)
    mats, block = both[:, :part], both[:, part:]
    rest = jnp.stack(rest_grads)
    d_gains = sum_group(mix_grads[0][:part, heads : heads + 2 * layers].T)
    d_gains = lax.dynamic_slice_in_dim(d_gains, lax.axis_index("tensor") * gain_part, gain_part, axis=1)
    small = block[:, :small_part, 2 * mine + heads : span].transpose(0, 2, 1).reshape(layers, 5, heads, small_part)

    def matrix(i):
        return mats[:, :, HD + mine * i : HD + mine * (i + 1)]

    def tail_piece(i):
        return rest[:, :, edges[i] : edges[i + 1]]

    def state_part(i):
        return block[:, :, mine * i : mine * (i + 1)].reshape(layers, inner_part, heads, HD)

    return (
        block_out,
        grad_in,
        matrix(0),
        matrix(1),
        matrix(2),
        tail_piece(3),
        mats[:, :, :heads],
        tail_piece(4).transpose(0, 2, 1),
        state_part(0).transpose(0, 2, 3, 1),
        block[:, :, 2 * mine : 2 * mine + heads].transpose(0, 2, 1),
        state_part(1).transpose(0, 2, 1, 3),
        small[:, 0],
        small[:, 1],
        small[:, 2],
        small[:, 3],
        small[:, 4],
        d_gains[:layers],
        d_gains[layers:],
        tail_piece(0),
        tail_piece(1),
        tail_piece(2).transpose(0, 2, 1),
    )


def order_sum(sums):
    def turn(x, bit):
        parts = jnp.split(x, 4, axis=1)
        return jnp.concatenate([parts[i ^ bit] for i in range(4)], axis=1)

    sums = sums + turn(swap(sums, 1), 1)
    return sums + turn(swap(sums, 2), 2)


def solution(mesh):
    shape = (mesh.shape["dp"] // 2, 2, mesh.shape["tensor"])
    mesh = jax.sharding.Mesh(mesh.devices.reshape(shape), ("line", "near", "tensor"))
    placed = (
        P(("line", "near", "tensor"), None),
        P(("line", "near", "tensor"), None),
        P(None, DP, "tensor"),
        P(None, DP, "tensor"),
        P(None, DP, "tensor"),
        P(None, DP, "tensor"),
        P(None, DP, "tensor"),
        P(None, "tensor", DP),
        P(None, "tensor", None, DP),
        P(None, "tensor", DP),
        P(None, "tensor", DP, None),
        P(None, "tensor", DP),
        P(None, "tensor", DP),
        P(None, "tensor", DP),
        P(None, "tensor", DP),
        P(None, "tensor", DP),
        P(None, ("line", "near", "tensor")),
        P(None, ("line", "near", "tensor")),
        P(None, DP, "tensor"),
        P(None, DP, "tensor"),
        P(None, "tensor", DP),
    )
    return jax.shard_map(
        per_device,
        mesh=mesh,
        in_specs=placed,
        out_specs=(
            P(("line", "near", "tensor"), None),
            P(("line", "near", "tensor"), None),
            P(None, DP, "tensor"),
            P(None, DP, "tensor"),
            P(None, DP, "tensor"),
            P(None, DP, "tensor"),
            P(None, DP, "tensor"),
            P(None, "tensor", DP),
            P(None, "tensor", None, DP),
            P(None, "tensor", DP),
            P(None, "tensor", DP, None),
            P(None, "tensor", DP),
            P(None, "tensor", DP),
            P(None, "tensor", DP),
            P(None, "tensor", DP),
            P(None, "tensor", DP),
            P(None, ("line", "near", "tensor")),
            P(None, ("line", "near", "tensor")),
            P(None, DP, "tensor"),
            P(None, DP, "tensor"),
            P(None, "tensor", DP),
        ),
        check_vma=False,
    )
```

```python
import functools

import jax
import jax.numpy as jnp
from jax import lax
from jax.experimental import pallas as pl
from jax.sharding import PartitionSpec as P
from jax.experimental.pallas import tpu as pltpu

F32 = jnp.float32
BF = jnp.bfloat16
HD = 64
INNER = 256
CS = 16
CH = 128
STEPS = CH // CS
UNIT = 128
PACK = 640
EPS = 1e-6
K0 = 0.7978845608028654
K1 = 0.7978845608028654 * 0.044715


def mm(a, b, ca, cb):
    return lax.dot_general(
        a.astype(BF), b.astype(BF), (((ca,), (cb,)), ((), ())), preferred_element_type=F32
    )


def nn(a, b):
    return mm(a, b, 1, 0)


def nt(a, b):
    return mm(a, b, 1, 1)


def tn(a, b):
    return mm(a, b, 0, 0)


def gelu_two(z):
    zz = z * z
    t = jnp.tanh(z * (K0 + K1 * zz))
    half = 0.5 + 0.5 * t
    return z * half, half + 0.5 * z * (1.0 - t * t) * (K0 + 3.0 * K1 * zz)


def gelu_three(z):
    zz = z * z
    t = jnp.tanh(z * (K0 + K1 * zz))
    half = 0.5 + 0.5 * t
    rest = 1.0 - t * t
    p = K0 + 3.0 * K1 * zz
    return z * half, half + 0.5 * z * rest * p, rest * (p + 3.0 * K1 * zz - z * t * p * p)


def mean(x):
    return jnp.sum(x, axis=1, keepdims=True) * (1.0 / HD)


def masks():
    row = lax.broadcasted_iota(jnp.int32, (CH, CH), 0)
    col = lax.broadcasted_iota(jnp.int32, (CH, CH), 1)
    row_block, col_block = row >> 4, col >> 4
    inside = (row_block == col_block) & (col <= row)
    earlier = col_block < row_block
    own = 1.0 / ((row & (CS - 1)) + 1).astype(F32)
    coef = jnp.where(earlier, 1.0 / CS, jnp.where(inside, own, 0.0))
    return coef, jnp.where(earlier, 1.0, 0.0)


def split_pack(pack, heads):
    wide = pack.astype(F32)
    first = wide[:, :CH]
    turned = first.T
    rates_row = [jax.nn.sigmoid(turned[h : h + 1]) * (1.0 / HD) for h in range(heads)]
    rates_col = [jax.nn.sigmoid(first[:, h : h + 1]) * (1.0 / HD) for h in range(heads)]
    off = HD
    xq = [wide[:, off + HD * h : off + HD * (h + 1)] for h in range(heads)]
    off += HD * heads
    xk = [wide[:, off + HD * h : off + HD * (h + 1)] for h in range(heads)]
    off += HD * heads
    xv = [wide[:, off + HD * h : off + HD * (h + 1)] for h in range(heads)]
    return xq, xk, xv, rates_row, rates_col


def forward_kernel(
    heads, dp, place_ref, pack_ref, in_ref,
    o_ref, z1_ref, a_ref, z1b_ref, c_ref, z2b_ref, w1s_ref, w2s_ref, small_ref,
    w1, b1, w2, b2, pre, kke, cc, ecol, g1buf, g2buf, x2buf,
):
    H = range(heads)

    @pl.when(pl.program_id(0) == 0)
    def _():
        mine = heads * HD
        params = in_ref[...].astype(F32)
        first, second, rest = params[:, :mine].T, params[:, mine : 2 * mine].T, params[:, 2 * mine :]
        biases = rest.T
        few, step = HD // dp, INNER // dp
        small = jnp.concatenate([rest[step * d : step * d + few] for d in range(dp)], axis=0).T
        small_ref[...] = small[heads:]
        for h in H:
            w1[h] = first[HD * h : HD * (h + 1)]
            w2_own = second[HD * h : HD * (h + 1)]
            w2[h] = w2_own - jnp.mean(w2_own, axis=0, keepdims=True)
            b1[h] = biases[h : h + 1]
            b2_own = small[heads + h : heads + h + 1]
            b2[h] = b2_own - mean(b2_own)
        g1buf[...] = jnp.zeros_like(g1buf)

    coef, before = masks()
    xq, xk, xv, rrow, rcol = split_pack(pack_ref[...], heads)
    b2_start = [b2[h] for h in H]
    mcc = []
    for h in H:
        pre[h] = nn(xk[h], w1[h]) + b1[h]
        kke[h] = ((nt(xk[h], xk[h]) + 1.0) * (before * (rrow[h] * (1.0 / CS)))).astype(BF)
        g, sh = small_ref[heads + h : heads + h + 1], small_ref[2 * heads + h : 2 * heads + h + 1]
        cval = (sh - xv[h] + xk[h]) * g
        cc[h] = cval
        mcc.append(mean(cval))
        ecol[h] = jnp.broadcast_to(rcol[h] * (1.0 / CS), (CH, HD))
        w1s_ref[0, h] = w1[h].astype(w1s_ref.dtype)
    w1_start = [w1[h].astype(BF) for h in H]
    w2_start = [w2[h].astype(BF) for h in H]
    b1_start = [b1[h] for h in H]

    def finish(k):
        part, upto = slice(UNIT * k, UNIT * (k + 1)), UNIT * (k + 1)
        mask = [coef[part, :upto] * rrow[h][:, :upto] for h in H]
        score = [nt(xq[h][part], xk[h][:upto]) + 1.0 for h in H]
        z1b = [nn(xq[h][part], w1_start[h]) + b1_start[h] - nn(score[h] * mask[h], g1buf[h, :upto, :]) for h in H]
        x2q = [jax.nn.gelu(z1b[h], approximate=True).astype(BF) for h in H]
        p = [nt(x2q[h], x2buf[h, :upto, :]) + 1.0 for h in H]
        z2b = [nt(x2q[h], w2_start[h]) + b2_start[h] - nn(p[h] * mask[h], g2buf[h, :upto, :]) for h in H]
        for h in H:
            z1b_ref[part, INNER * h : INNER * (h + 1)] = z1b[h].astype(BF)
            centred = z2b[h] - mean(z2b[h])
            z2b_ref[h, part, :] = centred.astype(BF)
            unit = centred * lax.rsqrt(mean(centred * centred) + EPS)
            o_ref[part, HD * h : HD * (h + 1)] = (
                xq[h][part] + unit * small_ref[heads + h : heads + h + 1] + small_ref[2 * heads + h : 2 * heads + h + 1]
            )

    ma = [mean(small_ref[heads + h : heads + h + 1] * small_ref[heads + h : heads + h + 1]) for h in H]
    w2v = [w2[h] for h in H]
    b2v = list(b2_start)
    for i in range(STEPS):
        rows = slice(CS * i, CS * (i + 1))
        z1 = [pre[h, rows, :] for h in H]
        if i >= 2:
            z1 = [z1[h] - nn(kke[h, rows, : CS * (i - 1)], g1buf[h, : CS * (i - 1), :]) for h in H]
        if i >= 1:
            z1 = [z1[h] - nn(kke[h, rows, :][:, CS * (i - 1) : CS * i], g1buf[h, CS * (i - 1) : CS * i, :]) for h in H]
        xd = [gelu_two(z1[h]) for h in H]
        x2b = [xd[h][0].astype(BF) for h in H]
        w2b = [w2v[h].astype(BF) for h in H]
        c = [nt(x2b[h], w2b[h]) + b2v[h] for h in H]
        g2 = []
        for h in H:
            g = small_ref[heads + h : heads + h + 1]
            a = g * g
            ca = c[h] * a
            cch = cc[h, rows, :]
            mc = mcc[h][rows]
            mu, q1, q2, q3, q4 = mean(c[h]), mean(c[h] * c[h]), mean(ca), mean(ca * c[h]), mean(c[h] * cch)
            s = lax.rsqrt(q1 - mu * mu + EPS)
            m1 = s * (q2 - mu * ma[h]) + mc
            m2 = s * (s * (q3 - mu * (2.0 * q2 - mu * ma[h])) + (q4 - mu * mc))
            c[h] = c[h] - mu
            g2.append(s * (c[h] * (s * (a - m2)) + cch - m1))
        av = [nn(g2[h], w2b[h]) for h in H]
        g1 = [av[h] * xd[h][1] for h in H]
        for h in H:
            g1buf[h, rows, :] = g1[h].astype(BF)
            g2buf[h, rows, :] = g2[h].astype(BF)
            x2buf[h, rows, :] = x2b[h]
            w2s_ref[i, h] = w2b[h].astype(w2s_ref.dtype)
            z1_ref[rows, INNER * h : INNER * (h + 1)] = z1[h].astype(BF)
            a_ref[rows, INNER * h : INNER * (h + 1)] = av[h].astype(BF)
            c_ref[h, rows, :] = c[h].astype(BF)
            eg2 = ecol[h, rows, :] * g2[h]
            w2v[h] = w2v[h] - tn(eg2, x2b[h])
            b2v[h] = b2v[h] - jnp.sum(eg2, axis=0, keepdims=True)
        if (i + 1) % (UNIT // CS) == 0:
            finish(i // (UNIT // CS))
    for h in H:
        g1 = g1buf[h]
        w1[h] = w1[h] - tn(ecol[h] * xk[h], g1)
        b1[h] = b1[h] - jnp.sum(ecol[h][:, :1] * g1.astype(F32), axis=0, keepdims=True)
        w2[h] = w2v[h]
        b2[h] = b2v[h]


def forward_call(place, pack, params, heads, dp):
    rows = pack.shape[0]
    chunks = rows // CH
    per_block = chunks // 4

    def spot(c, place):
        return ((c // per_block) ^ place[0]) * per_block + c % per_block

    def whole(*shape):
        return pl.BlockSpec(shape, lambda c, place: (0,) * len(shape))

    def moved(n):
        return pl.BlockSpec((CH, n), lambda c, place: (spot(c, place), 0))

    def kept(n):
        return pl.BlockSpec((CH, n), lambda c, place: (c, 0))

    by_head = pl.BlockSpec((heads, CH, HD), lambda c, place: (0, c, 0))
    sds = jax.ShapeDtypeStruct
    return pl.pallas_call(
        functools.partial(forward_kernel, heads, dp),
        grid_spec=pltpu.PrefetchScalarGridSpec(
            num_scalar_prefetch=1,
            grid=(chunks,),
            in_specs=[
                moved(PACK),
                whole(*params.shape),
            ],
            out_specs=[
                moved(heads * HD),
                kept(heads * INNER),
                kept(heads * INNER),
                kept(heads * INNER),
                by_head,
                by_head,
                pl.BlockSpec((1, heads, HD, INNER), lambda c, place: (c, 0, 0, 0)),
                pl.BlockSpec((STEPS, heads, HD, INNER), lambda c, place: (c, 0, 0, 0)),
                whole(5 * heads, HD),
            ],
            scratch_shapes=[
                pltpu.VMEM((heads, HD, INNER), F32),
                pltpu.VMEM((heads, 1, INNER), F32),
                pltpu.VMEM((heads, HD, INNER), F32),
                pltpu.VMEM((heads, 1, HD), F32),
                pltpu.VMEM((heads, CH, INNER), F32),
                pltpu.VMEM((heads, CH, CH), BF),
                pltpu.VMEM((heads, CH, HD), F32),
                pltpu.VMEM((heads, CH, HD), F32),
                pltpu.VMEM((heads, CH, INNER), BF),
                pltpu.VMEM((heads, CH, HD), BF),
                pltpu.VMEM((heads, CH, INNER), BF),
            ],
        ),
        out_shape=[
            sds((rows, heads * HD), F32),
            sds((rows, heads * INNER), BF),
            sds((rows, heads * INNER), BF),
            sds((rows, heads * INNER), BF),
            sds((heads, rows, HD), BF),
            sds((heads, rows, HD), BF),
            sds((chunks, heads, HD, INNER), BF),
            sds((chunks * STEPS, heads, HD, INNER), BF),
            sds((5 * heads, HD), F32),
        ],
        compiler_params=pltpu.CompilerParams(vmem_limit_bytes=56 * 2**20),
        cost_estimate=pl.CostEstimate(flops=65 * 10**9, bytes_accessed=25 * 10**6, transcendentals=0),
    )(place, pack, params)


def backward_kernel(
    heads, shares, place_ref, pack_ref, do_ref, z1_ref, a_ref, z1b_ref, c_ref, z2b_ref, w1s_ref, w2s_ref, small_ref, post_ref,
    dpack_ref, packed_ref, block_ref, dw1, db1, dw2, db2, dg_ref, dh_ref,
    dg1b, dg2b, dx2b, d1v, ad2, g2v, kkt, dz1buf, k1v, k2v, dyv, ecol, x2buf,
):
    H = range(heads)

    @pl.when(pl.program_id(0) == 0)
    def _():
        dw1[...] = jnp.zeros_like(dw1)
        db1[...] = jnp.zeros_like(db1)
        dw2[...] = jnp.zeros_like(dw2)
        db2[...] = jnp.zeros_like(db2)
        dg_ref[...] = jnp.zeros_like(dg_ref)
        dh_ref[...] = jnp.zeros_like(dh_ref)
        dz1buf[...] = jnp.zeros_like(dz1buf)

    coef, before = masks()
    xq, xk, xv, rrow, rcol = split_pack(pack_ref[...], heads)
    wides = [slice(INNER * h, INNER * (h + 1)) for h in H]
    gains = [small_ref[heads + h : heads + h + 1] for h in H]
    shifts = [small_ref[2 * heads + h : 2 * heads + h + 1] for h in H]
    w1_start = [w1s_ref[0, h] for h in H]
    w2_start = [w2s_ref[0, h] for h in H]
    mask = [coef * rrow[h] for h in H]
    do = [do_ref[:, HD * h : HD * (h + 1)].astype(F32) for h in H]
    dz2b = []
    for h in H:
        z2b = z2b_ref[h].astype(F32)
        sb = lax.rsqrt(mean(z2b * z2b) + EPS)
        ub = z2b * sb
        dog = do[h] * gains[h]
        dg_ref[h] += jnp.sum(do[h] * ub, axis=0, keepdims=True)
        dh_ref[h] += jnp.sum(do[h], axis=0, keepdims=True)
        dz2b.append(sb * (dog - mean(dog) - ub * mean(dog * ub)))
    uv, yv, st, g2_all = [], [], [], []
    for h in H:
        a = gains[h] * gains[h]
        c = c_ref[h].astype(F32)
        cch = (shifts[h] - xv[h] + xk[h]) * gains[h]
        ca = c * a
        q1, q2, q3, q4 = mean(c * c), mean(ca), mean(ca * c), mean(c * cch)
        s = lax.rsqrt(q1 + EPS)
        m1 = s * q2 + mean(cch)
        m2 = s * (s * q3 + q4)
        u = c * s
        y = u * a + cch
        g2 = s * (y - m1 - u * m2)
        uv.append(u)
        yv.append(y)
        st.append((s, m2, s * q2, s * s * q3, mean(y), mean(a)))
        g2v[h] = g2
        g2_all.append(g2.astype(BF))
        ecol[h] = jnp.broadcast_to(rcol[h] * (1.0 / CS), (CH, HD))
    x2_all, g1_all, x2q, d1b = [], [], [], []
    for h in H:
        x2, d1, slope2 = gelu_three(z1_ref[:, wides[h]].astype(F32))
        av = a_ref[:, wides[h]].astype(F32)
        d1v[h] = d1
        ad2[h] = av * slope2
        x2_all.append(x2.astype(BF))
        x2buf[h] = x2_all[h]
        g1_all.append((av * d1).astype(BF))
    for h in H:
        value, slope = gelu_two(z1b_ref[:, wides[h]].astype(F32))
        x2q.append(value.astype(BF))
        d1b.append(slope)
    before_t = before.T
    sc = [nt(xq[h], xk[h]) + 1.0 for h in H]
    for h in H:
        kkt[h] = ((nt(xk[h], xk[h]) + 1.0) * before_t).astype(BF)
    p = [nt(x2q[h], x2_all[h]) + 1.0 for h in H]
    dm2 = [-nt(dz2b[h], g2_all[h]) for h in H]
    dpv = [(mask[h] * dm2[h]).astype(BF) for h in H]
    dz1b = [(nn(dz2b[h], w2_start[h]) + nn(dpv[h], x2_all[h])) * d1b[h] for h in H]
    for h in H:
        dg2b[h] = -tn(mask[h] * p[h], dz2b[h])
    for h in H:
        dx2b[h] = tn(dpv[h], x2q[h])
    dw2_out = [tn(dz2b[h], x2q[h]) for h in H]
    db2_out = [jnp.sum(dz2b[h], axis=0, keepdims=True) for h in H]
    db1_out = [jnp.sum(dz1b[h], axis=0, keepdims=True) for h in H]
    dz1c = [dz1b[h].astype(BF) for h in H]
    dm1 = [-nt(dz1c[h], g1_all[h]) for h in H]
    dsv = [(mask[h] * dm1[h]).astype(BF) for h in H]
    for h in H:
        dg1b[h] = -tn(mask[h] * sc[h], dz1c[h])
    for h in H:
        k1v[h] = nn(xk[h], dw1[h]) + db1[h]
    dr_row = [jnp.sum(coef * (sc[h] * dm1[h] + p[h] * dm2[h]), axis=0, keepdims=True) for h in H]
    dxq = [do[h] + nt(dz1c[h], w1_start[h]) + nn(dsv[h], xk[h]) for h in H]
    dxk = [tn(dsv[h], xq[h]) - nt((rcol[h] * (1.0 / CS)) * g1_all[h].astype(F32), dw1[h]) for h in H]
    dw1_out = [tn(xq[h], dz1c[h]) for h in H]
    d2 = [dw2[h] for h in H]
    e2 = [db2[h] for h in H]
    for i in reversed(range(STEPS)):
        rows = slice(CS * i, CS * (i + 1))
        k1 = [k1v[h, rows, :] for h in H]
        if i < STEPS - 2:
            k1 = [k1[h] + nn(kkt[h, rows, :][:, CS * (i + 2) :], dz1buf[h, CS * (i + 2) :, :]) for h in H]
        if i < STEPS - 1:
            k1 = [k1[h] + nn(kkt[h, rows, :][:, CS * (i + 1) : CS * (i + 2)], dz1buf[h, CS * (i + 1) : CS * (i + 2), :]) for h in H]
        dg1 = [dg1b[h, rows, :] - ecol[h, rows, :][:, :1] * k1[h] for h in H]
        da = [(dg1[h] * d1v[h, rows, :]).astype(BF) for h in H]
        d2b = [d2[h].astype(BF) for h in H]
        w2i = [w2s_ref[i, h] for h in H]
        g2 = [g2v[h, rows, :] for h in H]
        k2 = [nt(x2buf[h, rows, :], d2b[h]) + e2[h] for h in H]
        dg2 = [dg2b[h, rows, :] - ecol[h, rows, :] * k2[h] + nt(da[h], w2i[h]) for h in H]
        l2 = [dx2b[h, rows, :] - nn(ecol[h, rows, :] * g2[h], d2b[h]) for h in H]
        dz2 = []
        for h in H:
            g = small_ref[heads + h : heads + h + 1]
            a = g * g
            s, m2, mau, mauu, my = (q[rows] for q in st[h][:5])
            ma = st[h][5]
            u, y = uv[h][rows], yv[h][rows]
            dv = dg2[h]
            dva = dv * a
            n1, n2, n3, n4, n5 = mean(dv), mean(dv * u), mean(dv * g2[h]), mean(dva * u), mean(dva)
            dy = s * (dv - n1 - u * n2)
            muu = s * (n4 - n1 * mau - n2 * (mauu + 2.0 * m2))
            mu = s * (n5 - n1 * (ma + m2) - n2 * (mau + my))
            dz2.append(s * (dy * a - (s * m2) * dv - (s * n2) * y - mu - u * (muu + n3)))
            dyv[h, rows, :] = dy
            k2v[h, rows, :] = k2[h]
        dx2 = [l2[h] + nn(dz2[h], w2i[h]) for h in H]
        dz1 = [dx2[h] * d1v[h, rows, :] + dg1[h] * ad2[h, rows, :] for h in H]
        for h in H:
            dz1buf[h, rows, :] = dz1[h].astype(BF)
            d2[h] = d2[h] + tn(
                jnp.concatenate([g2[h], dz2[h]], axis=0), jnp.concatenate([da[h], x2buf[h, rows, :]], axis=0)
            )
            e2[h] = e2[h] + jnp.sum(dz2[h], axis=0, keepdims=True)
    dz1 = [dz1buf[h] for h in H]
    k1 = [k1v[h] + nn(kkt[h], dz1[h]) for h in H]
    dkk = [(-nt(dz1[h], g1_all[h]) * (before * (rrow[h] * (1.0 / CS)))).astype(BF) for h in H]
    dyg = [dyv[h] * gains[h] for h in H]
    dk = [dxk[h] + nt(dz1[h], w1_start[h]) + dyg[h] for h in H]
    dk = [dk[h] + nn(dkk[h], xk[h]) + tn(dkk[h], xk[h]) for h in H]
    de_col = [
        jnp.sum(g1_all[h].astype(F32) * k1[h], axis=1, keepdims=True)
        + jnp.sum(g2v[h] * k2v[h], axis=1, keepdims=True)
        for h in H
    ]
    for h in H:
        dg_ref[h] += jnp.sum(dyv[h] * (uv[h] * gains[h] * 2.0 + shifts[h] - xv[h] + xk[h]), axis=0, keepdims=True)
        dh_ref[h] += jnp.sum(dyg[h], axis=0, keepdims=True)
        off = HD + HD * h
        dpack_ref[:, off : off + HD] = dxq[h].astype(BF)
        off += HD * heads
        dpack_ref[:, off : off + HD] = dk[h].astype(BF)
        off += HD * heads
        dpack_ref[:, off : off + HD] = (-dyg[h]).astype(BF)
    for h in H:
        dw1[h] = dw1[h] + dw1_out[h] + tn(xk[h], dz1[h])
        db1[h] = db1[h] + db1_out[h] + jnp.sum(dz1[h].astype(F32), axis=0, keepdims=True)
        dw2[h] = d2[h] + dw2_out[h]
        db2[h] = e2[h] + db2_out[h]
    sub = lax.broadcasted_iota(jnp.int32, (CH, CH), 0)
    lane = lax.broadcasted_iota(jnp.int32, (CH, CH), 1)
    stack = jnp.zeros((CH, CH), F32)
    cols = jnp.zeros((CH, CH), F32)
    for h in H:
        stack = stack + jnp.where(sub == h, dr_row[h], 0.0)
        slope = rcol[h] * (1.0 - HD * rcol[h])
        cols = cols + jnp.where(lane == h, slope, 0.0)
    turned = stack.T
    for h in H:
        turned = turned - jnp.where(lane == h, de_col[h] * (1.0 / CS), 0.0)
    dpack_ref[:, :HD] = (turned * cols)[:, :HD].astype(dpack_ref.dtype)

    @pl.when(pl.program_id(0) == pl.num_programs(0) - 1)
    def _():
        mine = heads * HD
        block_ref[...] = jnp.zeros_like(block_ref)
        for h in H:
            block_ref[:, HD * h : HD * (h + 1)] = dw1[h].T
            block_ref[:, mine + HD * h : mine + HD * (h + 1)] = dw2[h].T
        bias = jnp.concatenate([db1[h] for h in H] + [jnp.zeros((8 - heads, INNER), F32)], axis=0)
        block_ref[:, 2 * mine : 2 * mine + heads] = bias.T[:, :heads]
        lines = [db2[h] for h in H] + [dg_ref[h] for h in H] + [dh_ref[h] for h in H]
        lines += [post_ref[i : i + 1, HD * h : HD * (h + 1)] for i in range(2) for h in H]
        few, step = HD // shares, INNER // shares
        small = jnp.concatenate(lines + [jnp.zeros((16 - 5 * heads, HD), F32)], axis=0).T
        for d in range(shares):
            block_ref[step * d : step * d + few, 2 * mine + heads : 2 * mine + 6 * heads] = small[
                few * d : few * (d + 1), : 5 * heads
            ]
        packed_ref[...] = block_ref[...].astype(BF)


def backward_call(place, pack, do, saved, small, post, dp):
    z1, a, z1b, c, z2b, w1s, w2s = saved
    heads = small.shape[0] // 5
    rows = pack.shape[0]
    chunks = rows // CH
    last = chunks - 1
    per_block = chunks // 4

    def spot(c, place):
        return (((last - c) // per_block) ^ place[0]) * per_block + (last - c) % per_block

    def whole(*shape):
        return pl.BlockSpec(shape, lambda c, place: (0,) * len(shape))

    def moved(n):
        return pl.BlockSpec((CH, n), lambda c, place: (spot(c, place), 0))

    def kept(n):
        return pl.BlockSpec((CH, n), lambda c, place: (last - c, 0))

    by_head = pl.BlockSpec((heads, CH, HD), lambda c, place: (0, last - c, 0))
    sds = jax.ShapeDtypeStruct
    return pl.pallas_call(
        functools.partial(backward_kernel, heads, dp),
        grid_spec=pltpu.PrefetchScalarGridSpec(
            num_scalar_prefetch=1,
            grid=(chunks,),
            in_specs=[
                moved(PACK),
                moved(heads * HD),
                kept(heads * INNER),
                kept(heads * INNER),
                kept(heads * INNER),
                by_head,
                by_head,
                pl.BlockSpec((1, heads, HD, INNER), lambda c, place: (last - c, 0, 0, 0)),
                pl.BlockSpec((STEPS, heads, HD, INNER), lambda c, place: (last - c, 0, 0, 0)),
                whole(*small.shape),
                whole(*post.shape),
            ],
            out_specs=[moved(PACK), whole(INNER, PACK)],
            scratch_shapes=[
                pltpu.VMEM((INNER, PACK), F32),
                pltpu.VMEM((heads, HD, INNER), F32),
                pltpu.VMEM((heads, 1, INNER), F32),
                pltpu.VMEM((heads, HD, INNER), F32),
                pltpu.VMEM((heads, 1, HD), F32),
                pltpu.VMEM((heads, 1, HD), F32),
                pltpu.VMEM((heads, 1, HD), F32),
                pltpu.VMEM((heads, CH, INNER), F32),
                pltpu.VMEM((heads, CH, HD), F32),
                pltpu.VMEM((heads, CH, INNER), F32),
                pltpu.VMEM((heads, CH, INNER), F32),
                pltpu.VMEM((heads, CH, INNER), F32),
                pltpu.VMEM((heads, CH, HD), F32),
                pltpu.VMEM((heads, CH, CH), BF),
                pltpu.VMEM((heads, CH, INNER), BF),
                pltpu.VMEM((heads, CH, INNER), F32),
                pltpu.VMEM((heads, CH, HD), F32),
                pltpu.VMEM((heads, CH, HD), F32),
                pltpu.VMEM((heads, CH, HD), F32),
                pltpu.VMEM((heads, CH, INNER), BF),
            ],
        ),
        out_shape=[
            sds((rows, PACK), BF),
            sds((INNER, PACK), BF),
        ],
        compiler_params=pltpu.CompilerParams(vmem_limit_bytes=56 * 2**20),
        cost_estimate=pl.CostEstimate(flops=70 * 10**9, bytes_accessed=25 * 10**6, transcendentals=0),
    )(place, pack, do, z1, a, z1b, c, z2b, w1s, w2s, small, post)


D = 768
DP = ("line", "near")


def swap(x, bit):
    size = lax.axis_size("tensor")
    return lax.ppermute(x, "tensor", [(i, i ^ bit) for i in range(size)])


def widen(x):
    far = swap(x, 2)
    return jnp.concatenate([x, swap(x, 1), far, swap(far, 1)], axis=0)


def narrow_start(total):
    quarter = total.shape[0] // 4
    near, pair, far, cross = [total[quarter * i : quarter * (i + 1)] for i in range(4)]
    far = (far + swap(cross.astype(BF), 1).astype(F32)).astype(BF)
    return near + swap(pair.astype(BF), 1).astype(F32), far


def narrow(total, beside=None):
    near, far = narrow_start(total)
    moved = swap(far, 2)
    if beside is None:
        return near + moved.astype(F32)
    moved, beside = lax.optimization_barrier((moved, beside))
    return near + moved.astype(F32), beside


def sum_group(x):
    return x + swap(x, 1) + swap(x, 2) + swap(x, 3)


def dot(a, b):
    return lax.dot_general(a, b, (((1,), (0,)), ((), ())), preferred_element_type=F32)


def dot_t(a, b):
    return lax.dot_general(a, b, (((1,), (1,)), ((), ())), preferred_element_type=F32)


def t_dot(a, b):
    return lax.dot_general(a, b, (((0,), (0,)), ((), ())), preferred_element_type=F32)


def rms(x, gain):
    scale = lax.rsqrt(jnp.mean(x * x, axis=1, keepdims=True) + EPS)
    return (x * scale * gain).astype(BF), scale


def rms_back(x, scale, gain, grad):
    q = grad * gain
    back = scale * q - x * (scale * scale * scale) * jnp.mean(q * x, axis=1, keepdims=True)
    return back, jnp.sum(grad * (x * scale), axis=0)


def gather(x):
    return lax.all_gather(x, DP, axis=0, tiled=True)


def turned(x):
    return x.astype(F32).T.astype(BF)


def pack_kernel(
    q_ref, k_ref, v_ref, og_ref, r_ref, out_ref, i1_ref, i2_ref, gate_ref, up_ref, down_ref,
    mix_ref, early_ref, late_ref, inner_ref,
):
    heads = r_ref.shape[0]
    mine = heads * HD
    ff = gate_ref.shape[2]
    rest = 3 * ff + 2 * mine
    for l in range(2):
        mix, at = (mix_ref, 0) if l == 0 else (early_ref, rest)
        mix[:, at : at + HD] = jnp.zeros((mix.shape[0], HD), BF)
        mix[:, at : at + heads] = turned(r_ref[:, l])
        for i, ref in enumerate((q_ref, k_ref, v_ref)):
            mix[:, at + HD + mine * i : at + HD + mine * (i + 1)] = ref[l]
        group = early_ref if l == 0 else late_ref
        group[:, :ff] = gate_ref[l]
        group[:, ff : 2 * ff] = up_ref[l]
        group[:, 2 * ff : 3 * ff] = down_ref[l]
        group[:, 3 * ff : 3 * ff + mine] = og_ref[l]
        group[:, 3 * ff + mine : rest] = turned(out_ref[l])
        base = 2 * mine * l
        for h in range(heads):
            inner_ref[:, base + HD * h : base + HD * (h + 1)] = i1_ref[l, h]
            inner_ref[:, base + mine + HD * h : base + mine + HD * (h + 1)] = i2_ref[l, h]


def feed_grad_kernel(two_ref, branch_ref, gate_ref, up_ref, hid_ref, out_ref):
    ff = gate_ref.shape[1]
    two = two_ref[...]
    out_ref[:, :ff] = tn(two, gate_ref[...]).astype(BF)
    out_ref[:, ff : 2 * ff] = tn(two, up_ref[...]).astype(BF)
    out_ref[:, 2 * ff :] = tn(branch_ref[...], hid_ref[...]).astype(BF)


def mixer_grad_kernel(wide_ref, other_ref, pre_ref, ho_ref, held_ref, out_ref):
    mine = pre_ref.shape[1]
    out_ref[:, :mine] = tn(wide_ref[...], pre_ref[...]).astype(BF)
    out_ref[:, mine:] = tn(other_ref[...], ho_ref[...]).astype(BF)


def feed_grads(two, branch, gate, up, hid, extra):
    rows, width = two.shape
    step = 256
    left = pl.BlockSpec((rows, step), lambda i: (0, i))
    cols = 3 * gate.shape[1]

    def whole(x):
        return pl.BlockSpec(x.shape, lambda i: (0, 0))

    return pl.pallas_call(
        feed_grad_kernel,
        grid=(width // step,),
        in_specs=[left, left, whole(gate), whole(up), whole(hid)],
        out_specs=pl.BlockSpec((step, cols), lambda i: (i, 0)),
        out_shape=jax.ShapeDtypeStruct((width, cols + extra), BF),
        compiler_params=pltpu.CompilerParams(vmem_limit_bytes=32 * 2**20),
        cost_estimate=pl.CostEstimate(flops=2 * rows * width * cols, bytes_accessed=10 * 10**6, transcendentals=0),
    )(two, branch, gate, up, hid)


def mixer_grads(wide, other, pre, ho, held):
    rows, width = wide.shape
    step = 256
    left = pl.BlockSpec((rows, step), lambda i: (0, i))
    cols = 2 * pre.shape[1]
    at = held.shape[1] // cols - 1

    def whole(x):
        return pl.BlockSpec(x.shape, lambda i: (0, 0))

    return pl.pallas_call(
        mixer_grad_kernel,
        grid=(width // step,),
        in_specs=[left, left, whole(pre), whole(ho), pl.BlockSpec(memory_space=pl.ANY)],
        out_specs=pl.BlockSpec((step, cols), lambda i: (i, at)),
        out_shape=jax.ShapeDtypeStruct(held.shape, BF),
        input_output_aliases={4: 0},
        compiler_params=pltpu.CompilerParams(vmem_limit_bytes=32 * 2**20),
        cost_estimate=pl.CostEstimate(flops=2 * rows * width * cols, bytes_accessed=4 * 10**6, transcendentals=0),
    )(wide, other, pre, ho, held)


def gather_small(x):
    size = lax.axis_size("line")
    other = lax.ppermute(x, "near", [(0, 1), (1, 0)])
    first = lax.axis_index("near") == 0
    pair = jnp.concatenate([jnp.where(first, x, other), jnp.where(first, other, x)], axis=0)
    if size > 4:
        return lax.all_gather(pair, "line", axis=0, tiled=True)
    parts = [pair] + [lax.ppermute(pair, "line", [(i, (i - k) % size) for i in range(size)]) for k in range(1, size)]
    start = lax.rem(size - lax.axis_index("line"), size) * pair.shape[0]
    return lax.dynamic_slice_in_dim(jnp.concatenate(parts + parts[:-1], axis=0), start, size * pair.shape[0], axis=0)


def scatter(x):
    return lax.psum_scatter(x, DP, scatter_dimension=0, tiled=True).astype(F32)


def exchange_sum(x):
    moved = lax.all_to_all(x, DP, split_axis=0, concat_axis=0, tiled=True)
    return jnp.sum(moved.astype(F32), axis=0)


def per_device(
    hidden_in, cotangent, w_query, w_key, w_value, w_outgate, w_rate, w_output, init_first, init_first_bias,
    init_second, init_second_bias, inner_gain, inner_shift, post_gain, post_shift, mixer_gain, mlp_gain,
    w_gate, w_up, w_down,
):
    layers, part, mine = w_query.shape
    heads = w_rate.shape[2]
    ff = w_gate.shape[2]
    inner_part = init_first.shape[3]
    small_part = inner_gain.shape[2]
    gain_part = mixer_gain.shape[1]
    dp = lax.axis_size("line") * lax.axis_size("near")
    tp = lax.axis_size("tensor")
    rows = hidden_in.shape[0]
    place = lax.axis_index("tensor").astype(jnp.int32).reshape(1)
    lead = HD - heads

    gains_here = jnp.concatenate([mixer_gain, mlp_gain], axis=0)
    found = [gains_here] + [swap(gains_here, bit) for bit in (1, 2, 3)]
    for bit in (1, 2):
        flip = (lax.axis_index("tensor") & bit) > 0
        found = [jnp.where(flip, found[i ^ bit], found[i]) for i in range(4)]
    gains_group = jnp.concatenate(found, axis=1)
    span = 2 * mine + 6 * heads
    sds = jax.ShapeDtypeStruct
    rest_cols = 3 * ff + 2 * mine
    mix_here, early, late, inner_here = pl.pallas_call(
        pack_kernel,
        out_shape=[
            sds((part, PACK), BF),
            sds((part, rest_cols + PACK), BF),
            sds((part, rest_cols), BF),
            sds((inner_part, 2 * mine * layers), BF),
        ],
    )(
        w_query, w_key, w_value, w_outgate, w_rate.transpose(2, 0, 1), w_output, init_first.transpose(0, 1, 3, 2),
        init_second, w_gate, w_up, w_down.transpose(0, 2, 1),
    )
    smalls = jnp.concatenate([init_second_bias, inner_gain, inner_shift, post_gain, post_shift], axis=1)
    smalls = jnp.pad(smalls.reshape(layers * 5 * heads, small_part), ((0, 0), (0, inner_part - small_part)))
    biases = init_first_bias.reshape(layers * heads, inner_part)
    thin = jnp.concatenate([biases, smalls], axis=0).T
    raw_near, raw_far = swap(hidden_in, 1), swap(hidden_in, 2)
    thin, raw_near, raw_far = lax.optimization_barrier((thin, raw_near, raw_far))
    inner_all = gather_small(jnp.concatenate([inner_here, thin, gains_group.reshape(inner_part, -1)], axis=1))
    mix_here, early, inner_all = lax.optimization_barrier((mix_here, early, inner_all))
    mix_w = [gather(mix_here)]
    first_group, last_group = gather(early), gather(late)
    mix_w.append(first_group[:, rest_cols:])
    rest_w = [first_group[:, :rest_cols], last_group]
    states = 2 * mine * layers
    inner_in = []
    for l in range(layers):
        at = states + heads * layers + 5 * heads * l
        bias_at = states + heads * l
        inner_in.append(
            jnp.concatenate(
                [inner_all[:, 2 * mine * l : 2 * mine * (l + 1)], inner_all[:, bias_at : bias_at + heads],
                 inner_all[:, at : at + 5 * heads]],
                axis=1,
            )
        )
    gains = inner_all[:, layers * span :].reshape(dp, 2 * layers, tp * gain_part)
    gains = gains.transpose(1, 0, 2).reshape(2 * layers, D).astype(F32)
    edges = [0, ff, 2 * ff, 3 * ff, 3 * ff + mine, 3 * ff + 2 * mine]

    def piece(l, i):
        return rest_w[l][:, edges[i] : edges[i + 1]]

    residual = hidden_in.astype(F32)
    raw_wide = jnp.concatenate([hidden_in, raw_near, raw_far, swap(raw_far, 1)], axis=0)
    top_near, top_far = swap(cotangent, 1), swap(cotangent, 2)
    kept = []
    for l in range(layers):
        gain_one, gain_two = gains[l], gains[layers + l]
        res_one = residual
        if l == 0:
            wide_res = raw_wide.astype(F32)
            wide, wide_scale = rms(wide_res, gain_one)
            wide_unit = wide_res * wide_scale
            scale_one = lax.rsqrt(jnp.mean(residual * residual, axis=1, keepdims=True) + EPS)
        else:
            normed, scale_one = rms(residual, gain_one)
            wide = widen(normed)
        pack = dot(wide, mix_w[l]).astype(BF)
        outs = forward_call(place, pack, inner_in[l], heads, dp)
        inner_out, saved, small = outs[0], outs[1:-1], outs[-1]
        if l == 0:
            inner_out, top_near, top_far = lax.optimization_barrier((inner_out, top_near, top_far))
        pg = small[3 * heads : 4 * heads].reshape(-1)
        ps = small[4 * heads : 5 * heads].reshape(-1)
        gate_pre = dot(wide, piece(l, 3))
        sums = jnp.stack([jnp.sum(inner_out, axis=1), jnp.sum(inner_out * inner_out, axis=1)])
        sums = order_sum(sums, True)
        mean_all = sums[0] / D
        inv = lax.rsqrt(sums[1] / D - mean_all * mean_all + EPS)[:, None]
        unit = (inner_out - mean_all[:, None]) * inv
        post = unit * pg + ps
        heads_out = (jax.nn.gelu(gate_pre, approximate=True) * post).astype(BF)
        partial = dot_t(heads_out, piece(l, 4))
        if l + 1 < layers:
            branch, inner_in[l + 1] = narrow(partial, inner_in[l + 1])
        else:
            branch = narrow(partial)
        residual = residual + branch
        res_two = residual
        normed, scale_two = rms(residual, gain_two)
        wide_two = widen(normed)
        gate = dot(wide_two, piece(l, 0))
        up = dot(wide_two, piece(l, 1))
        hidden = (jax.nn.silu(gate) * up).astype(BF)
        near, far = narrow_start(dot_t(hidden, piece(l, 2)))
        if l < layers - 1:
            residual = residual + near + swap(far, 2).astype(F32)
        kept.append(
            (res_one, scale_one, wide, pack, saved, gate_pre, unit, inv, heads_out, res_two, scale_two, wide_two,
             gate, up, hidden, small, pg, ps)
        )
    grad = cotangent.astype(F32)
    mix_grads, rest_grads = [None] * layers, [None] * layers
    gain_grads = [None] * (2 * layers)
    for l in reversed(range(layers)):
        gain_one, gain_two = gains[l], gains[layers + l]
        (res_one, scale_one, wide, pack, saved, gate_pre, unit, inv, heads_out, res_two, scale_two, wide_two,
         gate, up, hidden, small, pg, ps) = kept[l]
        if l == layers - 1:
            branch = jnp.concatenate([cotangent, top_near, top_far, swap(top_far, 1)], axis=0)
        else:
            branch = widen(grad.astype(BF))
        d_hidden = dot(branch, piece(l, 2))
        q = jax.nn.sigmoid(gate)
        swish = gate * q
        d_gate = (d_hidden * up * (q + swish * (1.0 - q))).astype(BF)
        d_up = (d_hidden * swish).astype(BF)
        held = feed_grads(wide_two, branch, d_gate, d_up, hidden, 2 * mine)
        d_norm, held = narrow(dot_t(d_gate, piece(l, 0)) + dot_t(d_up, piece(l, 1)), held)
        back, gain_grads[layers + l] = rms_back(res_two, scale_two, gain_two, d_norm)
        grad = grad + back
        branch_two = widen(grad.astype(BF))
        d_heads = dot(branch_two, piece(l, 4))
        post = unit * pg + ps
        ge, slope = gelu_two(gate_pre)
        d_pre = (d_heads * post * slope).astype(BF)
        d_post = d_heads * ge
        d_pg = jnp.sum(d_post * unit, axis=0)
        d_ps = jnp.sum(d_post, axis=0)
        p = d_post * pg
        sums = order_sum(jnp.stack([jnp.sum(p, axis=1), jnp.sum(p * unit, axis=1)]), False) / D
        rest_sum = mixer_grads(wide, branch_two, d_pre, heads_out, held)
        d_inner = inv * (p - sums[0][:, None] - unit * sums[1][:, None])
        rest_sum, d_inner = lax.optimization_barrier((rest_sum, d_inner))
        rest_grads[l] = scatter(rest_sum)
        if l == layers - 1:
            near, far, d_inner = lax.optimization_barrier((near, far, d_inner))
            moved = swap(far, 2)
        d_pack, block = backward_call(place, pack, d_inner, saved, small, jnp.stack([d_pg, d_ps]), dp)
        if l == layers - 1:
            d_pack, moved = lax.optimization_barrier((d_pack, moved))
            residual = residual + near + moved.astype(F32)
        mats = t_dot(wide, d_pack)
        if l == 0:
            d_wide = dot_t(d_pack, mix_w[l]) + dot_t(d_pre, piece(l, 3))
            gain_grads[l] = jnp.sum(d_wide * wide_unit, axis=0)
            mats = mats + jnp.pad(jnp.stack(gain_grads).T, ((0, 0), (heads, PACK - heads - 2 * layers)))
        mixed = jnp.concatenate([mats.astype(BF).reshape(dp, part, PACK), block.reshape(dp, inner_part, PACK)], axis=1)
        if l == 0:
            mixed, d_pack = lax.optimization_barrier((mixed, d_pack))
            d_norm = narrow(d_wide)
        else:
            d_norm, mixed = narrow(dot_t(d_pack, mix_w[l]) + dot_t(d_pre, piece(l, 3)), mixed)
        mix_grads[l] = exchange_sum(mixed)
        back, gain = rms_back(res_one, scale_one, gain_one, d_norm)
        if l > 0:
            gain_grads[l] = gain
        grad = grad + back
        if l > 0:
            grad, rest_grads[l], residual = lax.optimization_barrier((grad, rest_grads[l], residual))
    grad_in = grad
    block_out = residual.astype(BF)

    both = jnp.stack(mix_grads)
    mats, block = both[:, :part], both[:, part:]
    rest = jnp.stack(rest_grads)
    d_gains = sum_group(mix_grads[0][:part, heads : heads + 2 * layers].T)
    d_gains = lax.dynamic_slice_in_dim(d_gains, lax.axis_index("tensor") * gain_part, gain_part, axis=1)
    small = block[:, :small_part, 2 * mine + heads : span].transpose(0, 2, 1).reshape(layers, 5, heads, small_part)

    def matrix(i):
        return mats[:, :, HD + mine * i : HD + mine * (i + 1)]

    def tail_piece(i):
        return rest[:, :, edges[i] : edges[i + 1]]

    def state_part(i):
        return block[:, :, mine * i : mine * (i + 1)].reshape(layers, inner_part, heads, HD)

    return (
        block_out,
        grad_in,
        matrix(0),
        matrix(1),
        matrix(2),
        tail_piece(3),
        mats[:, :, :heads],
        tail_piece(4).transpose(0, 2, 1),
        state_part(0).transpose(0, 2, 3, 1),
        block[:, :, 2 * mine : 2 * mine + heads].transpose(0, 2, 1),
        state_part(1).transpose(0, 2, 1, 3),
        small[:, 0],
        small[:, 1],
        small[:, 2],
        small[:, 3],
        small[:, 4],
        d_gains[:layers],
        d_gains[layers:],
        tail_piece(0),
        tail_piece(1),
        tail_piece(2).transpose(0, 2, 1),
    )


def order_sum(sums, at_once):
    def turn(x, bit):
        parts = jnp.split(x, 4, axis=1)
        return jnp.concatenate([parts[i ^ bit] for i in range(4)], axis=1)

    if at_once:
        return sums + turn(swap(sums, 1), 1) + turn(swap(sums, 2), 2) + turn(swap(sums, 3), 3)
    sums = sums + turn(swap(sums, 1), 1)
    return sums + turn(swap(sums, 2), 2)


def solution(mesh):
    shape = (mesh.shape["dp"] // 2, 2, mesh.shape["tensor"])
    mesh = jax.sharding.Mesh(mesh.devices.reshape(shape), ("line", "near", "tensor"))
    placed = (
        P(("line", "near", "tensor"), None),
        P(("line", "near", "tensor"), None),
        P(None, DP, "tensor"),
        P(None, DP, "tensor"),
        P(None, DP, "tensor"),
        P(None, DP, "tensor"),
        P(None, DP, "tensor"),
        P(None, "tensor", DP),
        P(None, "tensor", None, DP),
        P(None, "tensor", DP),
        P(None, "tensor", DP, None),
        P(None, "tensor", DP),
        P(None, "tensor", DP),
        P(None, "tensor", DP),
        P(None, "tensor", DP),
        P(None, "tensor", DP),
        P(None, ("line", "near", "tensor")),
        P(None, ("line", "near", "tensor")),
        P(None, DP, "tensor"),
        P(None, DP, "tensor"),
        P(None, "tensor", DP),
    )
    return jax.shard_map(
        per_device,
        mesh=mesh,
        in_specs=placed,
        out_specs=(
            P(("line", "near", "tensor"), None),
            P(("line", "near", "tensor"), None),
            P(None, DP, "tensor"),
            P(None, DP, "tensor"),
            P(None, DP, "tensor"),
            P(None, DP, "tensor"),
            P(None, DP, "tensor"),
            P(None, "tensor", DP),
            P(None, "tensor", None, DP),
            P(None, "tensor", DP),
            P(None, "tensor", DP, None),
            P(None, "tensor", DP),
            P(None, "tensor", DP),
            P(None, "tensor", DP),
            P(None, "tensor", DP),
            P(None, "tensor", DP),
            P(None, ("line", "near", "tensor")),
            P(None, ("line", "near", "tensor")),
            P(None, DP, "tensor"),
            P(None, DP, "tensor"),
            P(None, "tensor", DP),
        ),
        check_vma=False,
    )
```
